32 devices in a mesh: section: 2 (over core), dp: 16 (over z, y, x).
Axes of the slice: x: 2, y: 2, z: 4, core: 2. Of those that a mesh axis runs over, the one named last changes fastest.
Arguments:
- patches: bfloat16 [16384, 768], P('dp'), may hold values from -6 to 6
- cotangent: bfloat16 [16384, 768], P('dp'), may hold values from -6 to 6
- codes: int32 [16384], P('dp'), may hold values from 0 to 6287, as said below
- lengths: int32 [32, 4], P('dp'), may hold values from 1 to 256, 512 in all within a row
- codebook: bfloat16 [6288, 768], P('dp'), may hold values from -6 to 6
- qkv_weight: bfloat16 [2, 768, 2304], P('section'), may hold values from -0.21875 to 0.21875
- out_weight: bfloat16 [2, 768, 768], P('section'), may hold values from -0.875 to 0.875
- up_weight: bfloat16 [2, 768, 3072], P('section'), may hold values from -0.21875 to 0.21875
- down_weight: bfloat16 [2, 3072, 768], P('section'), may hold values from -0.109375 to 0.109375
- up_bias: bfloat16 [2, 3072], P('section'), may hold values from -2 to 2
- vectors: bfloat16 [2, 8, 768], P('section'), may hold values from -2 to 2
Outputs:
- block_outputs: bfloat16 [2, 16384, 768], P('section', 'dp')
- input_grads: float32 [2, 16384, 768], P('section', 'dp')
- qkv_grad: float32 [2, 768, 2304], P('section', 'dp')
- out_grad: float32 [2, 768, 768], P('section', 'dp')
- up_grad: float32 [2, 768, 3072], P('section', 'dp')
- down_grad: float32 [2, 3072, 768], P('section', 'dp')
- up_bias_grad: float32 [2, 3072], P('section', 'dp')
- vectors_grad: float32 [2, 8, 768], P('section', None, 'dp')
- histogram: int32 [6288], replicated
- code_stats: float32 [2], replicated
The draws below stay inside these ranges and needn't reach their ends.
Inputs may be any that keep to these rules, and one draw needn't show every extreme that they name: A code's row lives on the index code // 393 of dp. The 1024 codes of one index of dp hold at most 128 codes for any one holding index, and in every draw some holding index gets exactly 128 from every index. `lengths`: each row sums to 512; its largest entry is exactly 256.
All inputs are finite; a program needn't handle non-finite values.
Results may differ from the reference program's by a relative error of at most 0.008.
Values may be sent and summed in bfloat16 or wider, within the bound.
A program may use at most 384 MiB of HBM per device.

```python
import math
import jax
import jax.numpy as jnp
import numpy as np
from jax import lax

D = 768
HEADS = 12
FF = 3072
V_DEV = 393
MB_TOK = 512
IMGS = 4
MICRO = 2
TOK_DEV = 1024
TOKENS = 16384
VOCAB = 6288
CAP = 128
N_DP = 16


def draw_codes(key, part):
    key = jax.random.fold_in(key, 11)
    full_holder = jax.random.randint(jax.random.fold_in(key, 1), (), 0, N_DP)
    slot_total = N_DP * CAP

    def one_device(device_number):
        own_key = jax.random.fold_in(key, device_number + 100)
        order = jax.random.permutation(jax.random.fold_in(own_key, 1), slot_total).astype(jnp.int32)
        holder = jnp.arange(slot_total, dtype=jnp.int32) // CAP
        priority = jnp.where(holder == full_holder, order - slot_total, order)
        picked = jnp.argsort(priority, stable=True)[:TOK_DEV].astype(jnp.int32)
        picked = picked[jax.random.permutation(jax.random.fold_in(own_key, 2), TOK_DEV)]
        row_pick = jax.random.randint(jax.random.fold_in(own_key, 3), (TOK_DEV,), 0, V_DEV)
        return picked // CAP * V_DEV + row_pick
    return jax.vmap(one_device)(jnp.arange(N_DP, dtype=jnp.int32)).reshape(-1).astype(jnp.int32)


def draw_cotangent(key, part):
    key = jax.random.fold_in(key, 23)
    common_raw = jax.random.normal(jax.random.fold_in(key, 1), (N_DP, 1, D), jnp.float32)
    common_part = jnp.clip(0.6 * common_raw, -2.4, 2.4)
    own_part = jnp.clip(0.8 * jax.random.normal(jax.random.fold_in(key, 2), (N_DP, TOK_DEV, D), jnp.float32), -3.6, 3.6)
    return (common_part + own_part).reshape(TOKENS, D).astype(jnp.bfloat16)


def block_levels(stream_key, dims, split, least, high):
    def one(dim, blocks):
        heights = jax.random.uniform(jax.random.fold_in(jax.random.fold_in(stream_key, 6), dim), (blocks,), jnp.float32, least / len(split), high / len(split))
        return jnp.repeat(jnp.exp(heights), dims[dim] // blocks).reshape((-1,) + (1,) * (len(dims) - dim - 1))

    factor_of = one(*split[0])
    for cut in split[1:]:
        factor_of = factor_of * one(*cut)
    return factor_of


def split_up(amount, total, reach, slope):
    weights = [(1 << 20) // math.isqrt(grade ** slope) + 1 for grade in range(2, amount + 1)]
    rest, given = total - reach - (amount - 1), [1] * (amount - 1)
    while rest > 0:
        free = [i for i in range(amount - 1) if given[i] < reach]
        pool, budget = sum([weights[i] for i in free]), rest
        for i in free:
            addition = min(reach - given[i], max(1, budget * weights[i] // pool), rest)
            given[i] = given[i] + addition
            rest = rest - addition
    return np.array([reach] + given)


def ragged(rng, number_of, total, limit, slope):
    if number_of == 2:
        one = jax.random.randint(rng, (), max(1, total - limit), min(limit, total - 1) + 1)
        return jnp.stack([one, total - one])
    tallies = jnp.asarray(split_up(number_of, total, limit, slope), jnp.int32)
    pairs = (number_of - 1) // 2
    source_of, receiver = tallies[1:1 + 2 * pairs:2], tallies[2:2 + 2 * pairs:2]
    slack = jnp.minimum(source_of - 1, limit - receiver)
    moved = jax.random.randint(jax.random.fold_in(rng, 1), (pairs,), 0, 1 << 20) % (slack + 1)
    tallies = tallies.at[1:1 + 2 * pairs:2].set(source_of - moved).at[2:2 + 2 * pairs:2].set(receiver + moved)
    return tallies[jax.random.permutation(jax.random.fold_in(rng, 2), number_of)]


def gaussian(key, extent, spread, limit, split=(), kind=jnp.bfloat16):
    drawn = spread * jax.random.normal(key, extent, jnp.float32)
    if split:
        drawn = drawn * block_levels(key, extent, split, -0.22, 0.18)
    return jnp.clip(drawn, -limit, limit).astype(kind)


def setup_inputs(seed: int = 0) -> dict:
    splits = jax.random.split(jax.random.key(seed), 12)
    patches = gaussian(splits[0], (TOKENS, D), 1.0, 6.0, ((0, 16),))
    cotangent = draw_cotangent(jax.random.fold_in(splits[11], 71), 0)
    codes = draw_codes(jax.random.fold_in(splits[11], 71), 0)
    lengths = jax.vmap(lambda own: ragged(own, IMGS, MB_TOK, MB_TOK // 2, 2))(jax.random.split(splits[3], (N_DP * MICRO))).reshape((N_DP * MICRO, IMGS)).astype(jnp.int32)
    codebook = gaussian(splits[4], (VOCAB, D), 1.0, 6.0, ((0, 16),))
    qkv_weight = gaussian(splits[5], (2, D, 3 * D), D ** -0.5, 0.21875, ((0, 2),))
    out_weight = gaussian(splits[6], (2, D, D), (D // 16) ** -0.5, 0.875, ((0, 2),))
    up_weight = gaussian(splits[7], (2, D, FF), D ** -0.5, 0.21875, ((0, 2),))
    down_weight = gaussian(splits[8], (2, FF, D), FF ** -0.5, 0.109375, ((0, 2),))
    up_bias = gaussian(splits[9], (2, FF), 0.3, 2.0, ((0, 2),))
    vectors = gaussian(splits[10], (2, 8, D), 0.3, 2.0, ((0, 2),))
    return {"patches": patches, "cotangent": cotangent, "codes": codes, "lengths": lengths, "codebook": codebook, "qkv_weight": qkv_weight, "out_weight": out_weight, "up_weight": up_weight, "down_weight": down_weight, "up_bias": up_bias, "vectors": vectors}


@jax.custom_vjp
def low(v):
    return lax.optimization_barrier(v.astype(jnp.bfloat16)).astype(jnp.float32)

@jax.custom_vjp
def low_back(v):
    return v

def low_keep(v):
    return (low(v), None)

def low_pass(kept, grad):
    return (grad,)

def back_keep(v):
    return (v, None)

def back_low(kept, grad):
    return (low(grad),)
low.defvjp(low_keep, low_pass)
low_back.defvjp(back_keep, back_low)

def product(first_term, second_term):
    return jnp.dot(first_term, second_term, precision=lax.Precision.HIGHEST, preferred_element_type=jnp.float32)

def layer_norm(input_rows, gain_row, bias_row):
    row_mean = lax.optimization_barrier(jnp.mean(input_rows, axis=-1, keepdims=True))
    centered = input_rows - row_mean
    variance = lax.optimization_barrier(jnp.mean(centered * centered, axis=-1, keepdims=True))
    return centered * lax.rsqrt(variance + 1e-06) * gain_row + bias_row

def segment_mask(length_row, row_count):
    image_ends = jnp.cumsum(length_row)
    positions = jnp.arange(row_count, dtype=jnp.int32)
    image_label = lax.optimization_barrier(jnp.sum((positions[:, None] >= image_ends[None, :-1]).astype(jnp.int32), axis=1))
    return image_label[:, None] == image_label[None, :]

def block(parameters, input_rows, allowed):
    qkv_matrix, out_matrix, up_matrix, down_matrix, up_shift, vector_rows = parameters
    row_count, model_width = input_rows.shape
    head_size = model_width // HEADS
    score_scale = head_size ** (-0.5)
    normed = low(layer_norm(input_rows, 1.0 + vector_rows[0], vector_rows[1]))
    projected = product(normed, qkv_matrix)
    query_rows = low(low_back(projected[:, :model_width] + vector_rows[2])).reshape(row_count, HEADS, head_size)
    key_rows = low(low_back(projected[:, model_width:2 * model_width])).reshape(row_count, HEADS, head_size)
    value_rows = low(low_back(projected[:, 2 * model_width:] + vector_rows[3])).reshape(row_count, HEADS, head_size)
    scores = low_back(jnp.einsum('qhd,khd->hqk', query_rows, key_rows, precision=lax.Precision.HIGHEST) * score_scale)
    scores = jnp.where(allowed[None], scores, -1e+30)
    row_max = lax.optimization_barrier(jnp.max(scores, axis=-1, keepdims=True))
    exponent = jnp.exp(scores - row_max)
    probabilities = low(exponent / lax.optimization_barrier(jnp.sum(exponent, axis=-1, keepdims=True)))
    mixed_heads = jnp.einsum('hqk,khd->qhd', probabilities, value_rows, precision=lax.Precision.HIGHEST)
    mixed_heads = low(low_back(mixed_heads.reshape(row_count, model_width)))
    hidden = input_rows + low_back(product(mixed_heads, out_matrix) + vector_rows[4])
    normed_two = low(layer_norm(hidden, 1.0 + vector_rows[5], vector_rows[6]))
    pre_act = low_back(product(normed_two, up_matrix) + up_shift)
    activated = low(jax.nn.gelu(pre_act))
    return hidden + low_back(product(activated, down_matrix) + vector_rows[7])

def add_pair(first_term, second_term):
    return first_term + second_term

def reference(patches, cotangent, codes, lengths, codebook, qkv_weight, out_weight, up_weight, down_weight, up_bias, vectors):
    block_count = N_DP * MICRO
    weight_list = (qkv_weight, out_weight, up_weight, down_weight, up_bias, vectors)
    encoder_params = tuple((weight_array[0].astype(jnp.float32) for weight_array in weight_list))
    decoder_params = tuple((weight_array[1].astype(jnp.float32) for weight_array in weight_list))

    def one_block(grad_state, block_items):
        patch_rows, cot_rows, code_rows, length_row = block_items
        allowed = segment_mask(length_row, MB_TOK)
        chosen = jnp.take(codebook, code_rows, axis=0).astype(jnp.float32)

        def decode(parameters, input_rows):
            return block(parameters, low_back(input_rows), allowed)

        def encode(parameters, input_rows):
            return block(parameters, input_rows, allowed)
        decoded, decode_back = jax.vjp(decode, decoder_params, chosen)
        decoder_grads, code_grad = decode_back(cot_rows.astype(jnp.float32))
        encoded, encode_back = jax.vjp(encode, encoder_params, patch_rows.astype(jnp.float32))
        encoder_grads, patch_grad = encode_back(code_grad + 0.5 * (encoded - chosen))
        grad_state = (jax.tree.map(add_pair, grad_state[0], encoder_grads), jax.tree.map(add_pair, grad_state[1], decoder_grads))
        return (grad_state, (encoded.astype(jnp.bfloat16), decoded.astype(jnp.bfloat16), patch_grad, code_grad))
    zero_grads = tuple((jnp.zeros_like(weight_array) for weight_array in encoder_params))
    block_items = (patches.reshape(block_count, MB_TOK, D), cotangent.reshape(block_count, MB_TOK, D), codes.reshape(block_count, MB_TOK), lengths)
    grad_state, per_block = lax.scan(one_block, (zero_grads, zero_grads), block_items)
    encoded, decoded, patch_grad, code_grad = per_block
    block_outputs = jnp.stack([encoded.reshape(TOKENS, D), decoded.reshape(TOKENS, D)])
    input_grads = jnp.stack([patch_grad.reshape(TOKENS, D), code_grad.reshape(TOKENS, D)])
    weight_grads = tuple((jnp.stack([first_grad, second_grad]) for first_grad, second_grad in zip(grad_state[0], grad_state[1])))
    histogram = jnp.zeros((VOCAB,), jnp.int32).at[codes].add(1)
    code_share = histogram.astype(jnp.float32) / TOKENS
    is_used = histogram > 0
    usage_share = jnp.mean(is_used.astype(jnp.float32))
    entropy = -jnp.sum(jnp.where(is_used, code_share * jnp.log(jnp.where(is_used, code_share, 1.0)), 0.0))
    code_stats = jnp.stack([usage_share, jnp.exp(entropy) / VOCAB])
    return (block_outputs, input_grads, weight_grads[0], weight_grads[1], weight_grads[2], weight_grads[3], weight_grads[4], weight_grads[5], histogram, code_stats)
```

```python
import functools
import math

import jax
import jax.numpy as jnp
from jax import lax
from jax.experimental import pallas as pl
from jax.experimental.pallas import tpu as pltpu
from jax.sharding import PartitionSpec as P

HEADS = 12
LANES = 128
TILE = 256
MESH = pl.DeviceIdType.MESH
MASKED = -1e30
GELU_SCALE = math.sqrt(2.0 / math.pi)
GELU_CUBIC = 0.044715


def times_transposed(first_term, second_term):
    return lax.dot_general(
        first_term, second_term, (((1,), (1,)), ((), ())), preferred_element_type=jnp.float32
    )


def transposed_times(first_term, second_term):
    return lax.dot_general(
        first_term, second_term, (((0,), (0,)), ((), ())), preferred_element_type=jnp.float32
    )


def times(first_term, second_term):
    return jnp.dot(first_term, second_term, preferred_element_type=jnp.float32)


def in_vmem():
    return pl.BlockSpec(memory_space=pltpu.VMEM)


def in_smem():
    return pl.BlockSpec(memory_space=pltpu.SMEM)


def in_place():
    return pl.BlockSpec(memory_space=pl.ANY)


def normalized(rows):
    row_mean = jnp.mean(rows, axis=-1, keepdims=True)
    centered = rows - row_mean
    variance = jnp.mean(centered * centered, axis=-1, keepdims=True)
    scale = lax.rsqrt(variance + 1e-06)
    return centered * scale, scale


def norm_backward(grad, hat, scale, gain_row):
    grad_hat = grad * gain_row
    first = jnp.mean(grad_hat, axis=-1, keepdims=True)
    second = jnp.mean(grad_hat * hat, axis=-1, keepdims=True)
    return scale * (grad_hat - first - hat * second)


def column_sum(rows):
    return jnp.sum(rows.astype(jnp.float32), axis=0, keepdims=True)


def fill_marks(lengths_ref, head_size, query_marks, key_marks):
    heads, rows, _ = query_marks.shape
    images = lengths_ref.shape[1]
    for head in range(heads):
        lane = lax.broadcasted_iota(jnp.int32, (1, LANES), 1) - (1 - head) * head_size
        inside = jnp.logical_and(lane >= 0, lane < images)
        for start in range(0, rows, LANES):
            positions = lax.broadcasted_iota(jnp.int32, (LANES, 1), 0) + start
            end, label = 0, jnp.zeros_like(positions)
            for image in range(images - 1):
                end = end + lengths_ref[lax.axis_index("section"), image]
                label = label + (positions >= end).astype(jnp.int32)
            same = label == lane
            other = jnp.logical_and(inside, jnp.logical_not(same))
            same = jnp.logical_and(inside, same)
            part = pl.ds(start, LANES)
            query_marks[head, part, :] = jnp.where(other, MASKED, 0.0).astype(jnp.bfloat16)
            key_marks[head, part, :] = jnp.where(same, 1.0, 0.0).astype(jnp.bfloat16)


def head_lanes(head, head_size, factor):
    lane = lax.broadcasted_iota(jnp.int32, (1, LANES), 1)
    inside = jnp.logical_and(lane >= head * head_size, lane < (head + 1) * head_size)
    return jnp.where(inside, factor, 0.0).astype(jnp.bfloat16)


def lane_block(index):
    return pl.ds(pl.multiple_of(index * LANES, LANES), LANES)


class Weights:
    def __init__(self, own_flag, own, other, held, sems):
        self.own_flag, self.own, self.other, self.held, self.sems = own_flag, own, other, held, sems

    def place(self, index):
        return self.held[index], self.sems.at[index]

    def start(self, index):
        @pl.when(self.own_flag == 1)
        def _():
            pltpu.make_async_copy(self.own[index], *self.place(index)).start()

        @pl.when(self.own_flag != 1)
        def _():
            pltpu.make_async_copy(self.other[index], *self.place(index)).start()

    def wait(self, index):
        pltpu.make_async_copy(self.own[index], *self.place(index)).wait()
        return self.place(index)[0]


def table_of(vectors, up_bias):
    width = vectors.shape[1]
    rows = jnp.concatenate([vectors, up_bias.reshape(-1, width)], axis=0).astype(jnp.float32)
    return jnp.pad(rows, ((0, -rows.shape[0] % 8), (0, 0)))


def up_bias_tile(table, first_row, j, width):
    per_row = width // TILE
    column = pl.multiple_of(j % per_row * TILE, TILE)
    return table[pl.ds(first_row + j // per_row, 1), pl.ds(column, TILE)]


VECTORS = 8
GROUP = 1 << 14
UNROLL = 4
SAVED = ("out", "hidden", "normed", "qkv", "mixed", "second", "slope", "act", "shown")


def saved_shapes(row_count, width, hidden_units):
    bfloat16, float32 = jnp.bfloat16, jnp.float32
    return [
        ((row_count, width), float32),
        ((row_count, width), float32),
        ((row_count, width), bfloat16),
        ((row_count, 3 * width), bfloat16),
        ((row_count, width), bfloat16),
        ((row_count, width), bfloat16),
        ((row_count, hidden_units), bfloat16),
        ((row_count, hidden_units), bfloat16),
        ((row_count, width), bfloat16),
    ]


def forward_steps(table, lengths_ref, rows_ref, stat_ref, buffers, work, weight, save, during):
    _, hidden_ref, normed_ref, qkv_ref, mixed_ref, second_ref = buffers[:6]
    query_marks, key_marks, max_columns, sum_columns = work
    rows, width = rows_ref.shape
    head_size = width // HEADS
    per_block = LANES // head_size
    half = rows // 2
    per_part = width // TILE

    fill_marks(lengths_ref, head_size, query_marks, key_marks)
    for start in range(0, rows, LANES):
        part = pl.ds(start, LANES)
        hat, _ = normalized(rows_ref[part, :].astype(jnp.float32))
        normed_ref[part, :] = (hat * (1.0 + table[0:1, :]) + table[1:2, :]).astype(jnp.bfloat16)
    save("normed")
    during("normed", 0)

    qkv_held = weight(0)
    for j in range(3 * per_part):
        columns = pl.ds(j * TILE, TILE)
        projected = times(normed_ref[...], qkv_held[:, columns])
        if j // per_part != 1:
            row = 2 + j // (2 * per_part)
            projected = projected + table[row : row + 1, pl.ds(j % per_part * TILE, TILE)]
        qkv_ref[:, columns] = projected.astype(jnp.bfloat16)

    save("qkv")
    during("qkv", 0)
    max_columns[...] = jnp.zeros_like(max_columns)
    sum_columns[...] = jnp.ones_like(sum_columns)

    @pl.loop(0, width // LANES)
    def _(i):
        keys = qkv_ref[:, lane_block(width // LANES + i)]
        values = qkv_ref[:, lane_block(2 * width // LANES + i)]
        lane = lax.broadcasted_iota(jnp.int32, (1, LANES), 1)
        keys_of = [keys * head_lanes(h, head_size, 1.0) + key_marks[h] for h in range(per_block)]
        values_of = [
            values * head_lanes(h, head_size, 1.0) + head_lanes(1 - h, head_size, 1.0) for h in range(per_block)
        ]
        units = [(start, h) for start in range(0, rows, half) for h in range(per_block)]

        def scores_of(unit):
            start, h = unit
            part = pl.ds(start, half)
            query = qkv_ref[part, lane_block(i)] * head_lanes(h, head_size, head_size**-0.5) + query_marks[h, part, :]
            return times_transposed(query, keys_of[h])

        ahead = scores_of(units[0])
        mixed = None
        for number, (start, h) in enumerate(units):
            part = pl.ds(start, half)
            scores = ahead
            if number + 1 < len(units):
                ahead = scores_of(units[number + 1])
            row_max = jnp.max(scores, axis=-1, keepdims=True)
            exponent = jnp.exp(scores - row_max).astype(jnp.bfloat16)
            sums = times(exponent, values_of[h])
            inside = jnp.logical_and(lane >= h * head_size, lane < (h + 1) * head_size)
            row_total = jnp.where(inside, pltpu.roll(sums, head_size, 1), sums)
            term = sums / row_total
            mixed = term if h == 0 else jnp.where(inside, term, mixed)
            here = lane == per_block * i + h
            max_columns[part, :] = jnp.where(here, row_max, max_columns[part, :])
            sum_columns[part, :] = jnp.where(here, row_total, sum_columns[part, :])
            if h == per_block - 1:
                mixed_ref[part, lane_block(i)] = mixed.astype(jnp.bfloat16)
        during("heads", i)

    save("mixed")
    stats = max_columns[...] + jnp.log(sum_columns[...])
    stat_ref[...] = jnp.transpose(stats)[: stat_ref.shape[0], :]

    out_held = weight(1)
    for start in range(0, width, TILE):
        columns = pl.ds(start, TILE)
        hidden_ref[:, columns] = (
            rows_ref[:, columns].astype(jnp.float32)
            + times(mixed_ref[...], out_held[:, columns])
            + table[4:5, columns]
        )
    save("hidden")
    for start in range(0, rows, LANES):
        part = pl.ds(start, LANES)
        hat, _ = normalized(hidden_ref[part, :])
        second_ref[part, :] = (hat * (1.0 + table[5:6, :]) + table[6:7, :]).astype(jnp.bfloat16)
    save("second")
    during("second", 0)


def up_product(table, second_ref, up_held, slope_ref, act_ref):
    tiles, width = up_held.shape[1] // TILE, second_ref.shape[1]

    @pl.loop(0, tiles // UNROLL)
    def _(group):
        def columns_of(j):
            return pl.ds(pl.multiple_of((group * UNROLL + j) * TILE, TILE), TILE)

        def pre_of(j):
            return times(second_ref[...], up_held[:, columns_of(j)])

        ahead = pre_of(0)
        for j in range(UNROLL):
            pre = ahead + up_bias_tile(table, VECTORS, group * UNROLL + j, width)
            if j + 1 < UNROLL:
                ahead = pre_of(j + 1)
            square = pre * pre
            bent = jnp.tanh(pre * (GELU_SCALE + (GELU_SCALE * GELU_CUBIC) * square))
            share = 0.5 + 0.5 * bent
            act_ref[:, columns_of(j)] = (pre * share).astype(jnp.bfloat16)
            steep = (0.5 - 0.5 * (bent * bent)) * (GELU_SCALE + (3.0 * GELU_SCALE * GELU_CUBIC) * square)
            slope_ref[:, columns_of(j)] = (share + pre * steep).astype(jnp.bfloat16)


def last_product(table, hidden_ref, act_ref, down_held, out_ref, shown_ref):
    for start in range(0, hidden_ref.shape[1], TILE):
        columns = pl.ds(start, TILE)
        result = hidden_ref[:, columns] + times(act_ref[...], down_held[:, columns]) + table[7:8, columns]
        if out_ref is not None:
            out_ref[:, columns] = result
        if shown_ref is not None:
            shown_ref[:, columns] = result.astype(jnp.bfloat16)


def forward_kernel(block, lengths_ref, rows_ref, tables_ref, *refs):
    own, other, made, (stat_ref,), held, buffers, work, (weight_sems, save_sems) = split_refs(
        refs, (4, 4, 9, 1, 4, 9, 4, 2)
    )
    weights = Weights((lax.axis_index("section") == block).astype(jnp.int32), own, other, held, weight_sems)
    for index in range(4):
        weights.start(index)
    saves = {
        name: pltpu.make_async_copy(source, target, save_sems.at[index])
        for index, (name, source, target) in enumerate(zip(SAVED, buffers, made))
    }
    table = tables_ref.at[block]
    forward_steps(
        table, lengths_ref, rows_ref, stat_ref, buffers, work, weights.wait,
        lambda name: saves[name].start(), lambda place, i: None,
    )
    up_product(table, buffers[5], weights.wait(2), buffers[6], buffers[7])
    last_product(table, buffers[1], buffers[7], weights.wait(3), buffers[0], buffers[8])
    for name in ("slope", "act", "out", "shown"):
        saves[name].start()
    for save in saves.values():
        save.wait()


def forward_work(row_count):
    return [
        pltpu.VMEM((2, row_count, LANES), jnp.bfloat16),
        pltpu.VMEM((2, row_count, LANES), jnp.bfloat16),
        pltpu.VMEM((row_count, LANES), jnp.float32),
        pltpu.VMEM((row_count, LANES), jnp.float32),
    ]


def forward_scratch(own, kept, row_count):
    return (
        [pltpu.VMEM(w.shape, w.dtype) for w in own]
        + [pltpu.VMEM(s, t) for s, t in kept]
        + forward_work(row_count)
        + [pltpu.SemaphoreType.DMA((4,)), pltpu.SemaphoreType.DMA((9,))]
    )


def forward_swap_kernel(lengths_ref, rows_ref, tables_ref, *refs):
    (
        own, other, (own_down,), made, (stat_ref, other_down), held, buffers, work,
        (own_held, other_held, weight_sems, save_sems, down_sems),
    ) = split_refs(refs, (3, 3, 1, 7, 2, 3, 8, 4, 5))
    section = lax.axis_index("section")
    barrier = pltpu.get_barrier_semaphore()
    pl.semaphore_signal(barrier, inc=1, device_id={"section": 1 - section}, device_id_type=MESH)
    weights = Weights((section == 1).astype(jnp.int32), own, other, held, weight_sems)
    for index in range(3):
        weights.start(index)
    down = pltpu.make_async_copy(own_down, own_held, down_sems.at[0])
    down.start()
    pl.semaphore_wait(barrier, 1)
    down.wait()
    swap = pltpu.make_async_remote_copy(
        src_ref=own_held, dst_ref=other_held, send_sem=down_sems.at[1], recv_sem=down_sems.at[2],
        device_id={"section": 1 - section}, device_id_type=MESH,
    )
    swap.start()
    saves = {
        name: pltpu.make_async_copy(source, target, save_sems.at[index])
        for index, (name, source, target) in enumerate(zip(SAVED[1:8], buffers[1:], made))
    }
    forward_steps(
        tables_ref.at[1], lengths_ref, rows_ref, stat_ref, buffers, work, weights.wait,
        lambda name: saves[name].start(), lambda place, i: None,
    )
    swap.wait()
    keep = pltpu.make_async_copy(other_held, other_down, down_sems.at[0])
    keep.start()
    up_product(tables_ref.at[1], buffers[5], weights.wait(2), buffers[6], buffers[7])
    saves["slope"].start()
    saves["act"].start()
    for save in saves.values():
        save.wait()
    keep.wait()


def forward_swap(lengths, rows, tables, own, other):
    row_count, width = rows.shape
    kept = saved_shapes(row_count, width, own[2].shape[1])[:8]
    shapes = kept[1:] + [((16, row_count), jnp.float32), (own[3].shape, own[3].dtype)]
    results = pl.pallas_call(
        forward_swap_kernel,
        out_shape=tuple(jax.ShapeDtypeStruct(s, t) for s, t in shapes),
        in_specs=[in_smem()] + [in_vmem()] * 2 + [in_place()] * 7,
        out_specs=[in_place()] * 7 + [in_vmem(), in_place()],
        scratch_shapes=[pltpu.VMEM(w.shape, w.dtype) for w in own[:3]]
        + [pltpu.VMEM(s, t) for s, t in kept]
        + forward_work(row_count)
        + [
            pltpu.VMEM(own[3].shape, own[3].dtype),
            pltpu.VMEM(own[3].shape, own[3].dtype),
            pltpu.SemaphoreType.DMA((4,)),
            pltpu.SemaphoreType.DMA((9,)),
            pltpu.SemaphoreType.DMA((3,)),
        ],
        compiler_params=pltpu.CompilerParams(
            collective_id=2, has_side_effects=True, vmem_limit_bytes=56 * 1024 * 1024
        ),
        name="forward_swap",
    )(lengths, rows, tables, *own[:3], *other, own[3])
    return results[:8], results[8]


def block_forward(block, lengths, rows, tables, own, other):
    row_count, width = rows.shape
    kept = saved_shapes(row_count, width, own[2].shape[1])
    stat_shape = (16, row_count)
    return pl.pallas_call(
        functools.partial(forward_kernel, block),
        out_shape=tuple(jax.ShapeDtypeStruct(s, t) for s, t in kept)
        + (jax.ShapeDtypeStruct(stat_shape, jnp.float32),),
        in_specs=[in_smem()] + [in_vmem()] * 2 + [in_place()] * 8,
        out_specs=[in_place()] * 9 + [in_vmem()],
        scratch_shapes=forward_scratch(own, kept, row_count),
        compiler_params=pltpu.CompilerParams(vmem_limit_bytes=56 * 1024 * 1024),
        cost_estimate=pl.CostEstimate(
            flops=2 * row_count * (12 * width * width + 2 * row_count * width),
            bytes_accessed=40 * 1024 * 1024,
            transcendentals=row_count * row_count * HEADS,
        ),
        name="block_forward",
    )(lengths, rows, tables, *own, *other)


def split_refs(refs, counts):
    groups, start = [], 0
    for count in counts:
        groups.append(refs[start : start + count])
        start = start + count
    return groups


def opening_kernel(real_shard, lengths_ref, code_tile_ref, vectors_ref, up_bias_ref, patches_ref, book_ref, *refs):
    (
        own, other, (tables_ref, all_codes_ref, chosen_ref), made, (stat_ref,), held, buffers, work,
        (weight_sems, save_sems),
        (rows_ref, book, total, half_out, half_in, table_in, code_slots, table_out, codes_ref),
        (load_sems, weight_send, weight_got, zero_send, zero_got, middle_send, middle_got, last_send, last_got,
         code_send, code_got, side_send, side_got, keep_sems),
    ) = split_refs(refs, (3, 3, 3, 7, 1, 3, 8, 4, 2, 9, 14))
    section, place = lax.axis_index("section"), lax.axis_index("dp")
    depth = book.shape[2]
    shard_rows, half_width = book.shape[3:]
    rows = rows_ref.shape[0]
    my_x, my_y, my_z = place % 2, place // 2 % 2, place // 4
    my_middle = my_y * (1 - section) + my_x * section
    my_last = my_x * (1 - section) + my_y * section
    middle_device = place + (1 - 2 * my_middle) * (2 - section)
    last_device = place + (1 - 2 * my_last) * (1 + section)

    barrier = pltpu.get_barrier_semaphore()
    pl.semaphore_signal(barrier, inc=1, device_id={"section": 1 - section}, device_id_type=MESH)
    for device in (middle_device, last_device):
        pl.semaphore_signal(barrier, inc=1, device_id={"dp": device}, device_id_type=MESH)
    for hop in range(1, depth):
        device = (my_z + hop) % depth * 4 + my_y * 2 + my_x
        pl.semaphore_signal(barrier, inc=1, device_id={"dp": device}, device_id_type=MESH)

    own_book = book.at[my_middle, my_last, my_z]
    load_book = pltpu.make_async_copy(
        book_ref.at[:, pl.ds(pl.multiple_of(section * half_width, LANES), half_width)], own_book, load_sems.at[0]
    )
    load_book.start()
    load_rows = pltpu.make_async_copy(
        patches_ref.at[pl.ds(pl.multiple_of(section * rows, rows), rows)], rows_ref, load_sems.at[1]
    )
    load_rows.start()
    own_codes = code_slots.at[my_z, my_middle, my_last]
    own_codes[...] = code_tile_ref[...]
    width = vectors_ref.shape[2]
    table_out[...] = jnp.zeros_like(table_out)
    table_out[:VECTORS, :] = vectors_ref[0].astype(jnp.float32)
    for j in range(up_bias_ref.shape[1] // width):
        table_out[VECTORS + j : VECTORS + j + 1, :] = up_bias_ref[:, j * width : (j + 1) * width].astype(jnp.float32)
    tables_ref[section] = table_out[...]
    codes = code_tile_ref[...]

    def shards_below(size):
        found = jnp.zeros_like(codes)
        for limit in range(size * real_shard, 4 * depth * real_shard, size * real_shard):
            found = found + (codes >= limit).astype(jnp.int32)
        return found

    holder, holder_z, holder_pair = shards_below(1), shards_below(4), shards_below(2)
    holder_y, holder_x = holder_pair - 2 * holder_z, holder - 2 * holder_pair
    holder_middle = holder_y * (1 - section) + holder_x * section
    holder_last = holder_x * (1 - section) + holder_y * section
    spot = (2 * holder_middle + holder_last) * GROUP + holder_z * shard_rows + codes - holder * real_shard
    turned = jnp.transpose(spot.astype(jnp.float32))
    for j in range(code_tile_ref.shape[0]):
        codes_ref[j * LANES : (j + 1) * LANES, :] = turned[:, j : j + 1].astype(jnp.int32)
    total[...] = jnp.zeros_like(total)

    def remote(source, land, send, got, **device):
        return pltpu.make_async_remote_copy(
            src_ref=source, dst_ref=land, send_sem=send, recv_sem=got, device_id=device, device_id_type=MESH
        )

    near = [sorted(range(depth), key=lambda z, here=here: (abs(z - here), z)) for here in range(depth)]

    def source_z(rank):
        found = my_z
        for here in range(depth):
            for other_rank in range(1, depth):
                here_now = jnp.logical_and(my_z == here, rank == other_rank)
                found = jnp.where(here_now, near[here][other_rank], found)
        return found

    def zero(source, target):
        part = book.at[my_middle, my_last, source]
        device = target * 4 + my_y * 2 + my_x
        return remote(part, part, zero_send.at[source, target], zero_got.at[source], dp=device)

    def zero_next(source):
        following = jnp.where(source < my_z, my_z + 1, my_z - 1)
        there = jnp.logical_and(following >= 0, following < depth)
        return jnp.clip(following, 0, depth - 1), there

    def zero_own(act):
        for step in (-1, 1):
            target = my_z + step
            there = jnp.logical_and(target >= 0, target < depth)

            @pl.when(there)
            def _():
                act(zero(my_z, jnp.clip(target, 0, depth - 1)))

    def middle(rank):
        source = source_z(rank)
        part = book.at[my_middle, my_last, source]
        return remote(part, part, middle_send.at[source], middle_got.at[source], dp=middle_device)

    def last(side, rank):
        source = source_z(rank)
        which = my_middle if side == 0 else 1 - my_middle
        part = book.at[which, my_last, source]
        return remote(part, part, last_send.at[side, source], last_got.at[side, source], dp=last_device)

    def codes_zero(hop):
        target = (my_z + hop) % depth * 4 + my_y * 2 + my_x
        return remote(own_codes, own_codes, code_send.at[hop - 1], code_got.at[hop - 1], dp=target)

    def codes_middle():
        part = code_slots.at[:, my_middle, my_last]
        return remote(part, part, code_send.at[depth], code_got.at[depth], dp=middle_device)

    def codes_last():
        part = code_slots.at[:, :, my_last]
        return remote(part, part, code_send.at[depth + 1], code_got.at[depth + 1], dp=last_device)

    def own_matrix(index):
        return pltpu.make_async_copy(own[index], held[index].at[section], weight_sems.at[index])

    def weight_across(index):
        part = held[index].at[section]
        return remote(part, part, weight_send.at[index], weight_got.at[index], section=1 - section)

    def keep(index):
        return pltpu.make_async_copy(held[index].at[1 - section], other[index], keep_sems.at[index])

    def send_matrix(index):
        own_matrix(index).wait()
        weight_across(index).start()

    table_across = remote(table_out, table_in, side_send.at[0], side_got.at[0], section=1 - section)
    half_across = remote(half_out, half_in, side_send.at[1], side_got.at[1], section=1 - section)

    def pick(which_middle, which_last):
        group = 2 * which_middle + which_last

        @pl.loop(0, total.shape[0] // rows)
        def _(block):
            part = pl.ds(pl.multiple_of(block * rows, rows), rows)
            inside = codes_ref[part, :] - group * GROUP
            lanes = lax.broadcasted_iota(jnp.int32, (1, depth * shard_rows), 1)
            hot = jnp.where(inside == lanes, 1.0, 0.0).astype(jnp.bfloat16)
            shards = book[which_middle, which_last].reshape(depth * shard_rows, half_width)
            total[part, :] = total[part, :] + times(hot, shards)

    for index in range(3):
        own_matrix(index).start()
    pl.semaphore_wait(barrier, 3 + depth - 1)
    table_across.start()
    load_book.wait()
    zero_own(lambda copy: copy.start())
    middle(0).start()
    last(0, 0).start()
    send_matrix(0)
    for hop in range(1, depth):
        codes_zero(hop).start()

    load_rows.wait()
    table_across.wait_recv()
    tables_ref[1 - section] = table_in[...]

    def weight(index):
        @pl.when(section == 1)
        def _():
            weight_across(index).wait_recv()
            keep(index).start()

        return held[index].at[0]

    def keep_late(index):
        @pl.when(section == 0)
        def _():
            weight_across(index).wait_recv()
            keep(index).start()

    saves = {
        name: pltpu.make_async_copy(source, target, save_sems.at[index])
        for index, (name, source, target) in enumerate(zip(SAVED[1:8], buffers[1:], made))
    }

    def from_zero(rank):
        source = source_z(rank)
        following, there = zero_next(source)
        zero(source, following).wait_recv()

        @pl.when(there)
        def _():
            zero(source, following).start()

        middle(rank).start()
        last(0, rank).start()

    def from_middle(rank):
        middle(rank).wait_recv()
        last(1, rank).start()

    def from_last(side):
        for rank in range(depth):
            last(side, rank).wait_recv()
        pick(my_middle if side == 0 else 1 - my_middle, 1 - my_last)

    def during(where, i):
        if where == "normed":
            from_zero(1)
            send_matrix(1)
            send_matrix(2)
        elif where == "qkv":
            from_middle(0)
            from_zero(2)
        elif where == "heads":

            @pl.when(i == 0)
            def _():
                from_middle(1)

            @pl.when(i == 1)
            def _():
                from_zero(3)

            @pl.when(i == 2)
            def _():
                from_middle(2)

            @pl.when(i == 3)
            def _():
                from_middle(3)

            @pl.when(i == 4)
            def _():
                pick(my_middle, my_last)

        elif where == "second":
            for hop in range(1, depth):
                codes_zero(hop).wait_recv()
            codes_middle().start()
            pick(1 - my_middle, my_last)

    forward_steps(
        tables_ref.at[0], lengths_ref, rows_ref, stat_ref, buffers, work, weight,
        lambda name: saves[name].start(), during,
    )
    table = tables_ref.at[0]
    keep_late(0)
    up_product(table, buffers[5], weight(2), buffers[6], buffers[7])
    saves["slope"].start()
    saves["act"].start()
    from_last(0)
    codes_middle().wait_recv()
    codes_last().start()
    keep_late(1)
    keep_late(2)
    from_last(1)
    own_rows = pl.ds(pl.multiple_of(section * rows, rows), rows)
    other_rows = pl.ds(pl.multiple_of((1 - section) * rows, rows), rows)
    half_out[...] = total[other_rows, :].astype(half_out.dtype)
    half_across.start()
    chosen_ref[:, pl.ds(pl.multiple_of(section * half_width, LANES), half_width)] = total[own_rows, :].astype(
        chosen_ref.dtype
    )
    half_across.wait_recv()
    chosen_ref[:, pl.ds(pl.multiple_of((1 - section) * half_width, LANES), half_width)] = half_in[...]
    codes_last().wait_recv()
    all_codes_ref[...] = code_slots[...]
    for index in range(3):
        weight_across(index).wait_send()
        keep(index).wait()
    table_across.wait_send()
    half_across.wait_send()
    zero_own(lambda copy: copy.wait_send())
    for hop in range(1, depth):
        source = source_z(hop)
        following, there = zero_next(source)

        @pl.when(there)
        def _():
            zero(source, following).wait_send()

        codes_zero(hop).wait_send()
    for hop in range(depth):
        middle(hop).wait_send()
        for side in range(2):
            last(side, hop).wait_send()
    codes_middle().wait_send()
    codes_last().wait_send()
    for save in saves.values():
        save.wait()


def opening(lengths, codes, vectors, up_bias, patches, codebook, own, devices, row_count):
    tokens, width = patches.shape
    half_width = width // 2
    depth, shard_rows = devices // 4, codebook.shape[0]
    padded = jnp.pad(codebook, ((0, -shard_rows % 16), (0, 0)))
    table_shape = (16, width)
    code_tile = codes.reshape(-1, LANES)
    kept = saved_shapes(row_count, width, own[2].shape[1])[:8]
    bfloat16, float32 = jnp.bfloat16, jnp.float32
    shapes = (
        [(w.shape, w.dtype) for w in own[:3]]
        + [
            ((2, *table_shape), float32),
            ((depth, 2, 2, *code_tile.shape), codes.dtype),
            ((row_count, width), bfloat16),
        ]
        + kept[1:]
        + [((16, row_count), float32)]
    )
    dma = pltpu.SemaphoreType.DMA
    results = pl.pallas_call(
        functools.partial(opening_kernel, shard_rows),
        out_shape=tuple(jax.ShapeDtypeStruct(s, t) for s, t in shapes),
        in_specs=[in_smem()] + [in_vmem()] * 3 + [in_place()] * 5,
        out_specs=[in_place()] * 3 + [in_vmem()] * 3 + [in_place()] * 7 + [in_vmem()],
        scratch_shapes=[pltpu.VMEM((2, *w.shape), w.dtype) for w in own[:3]] + forward_scratch((), kept, row_count)
        + [
            pltpu.VMEM((row_count, width), bfloat16),
            pltpu.VMEM((2, 2, depth, padded.shape[0], half_width), bfloat16),
            pltpu.VMEM((tokens, half_width), float32),
            pltpu.VMEM((row_count, half_width), bfloat16),
            pltpu.VMEM((row_count, half_width), bfloat16),
            pltpu.VMEM(table_shape, float32),
            pltpu.VMEM((depth, 2, 2, *code_tile.shape), codes.dtype),
            pltpu.VMEM(table_shape, float32),
            pltpu.VMEM((tokens, 1), jnp.int32),
            dma((2,)),
            dma((4,)),
            dma((4,)),
            dma((depth, depth)),
            dma((depth,)),
            dma((depth,)),
            dma((depth,)),
            dma((2, depth)),
            dma((2, depth)),
            dma((depth + 2,)),
            dma((depth + 2,)),
            dma((2,)),
            dma((2,)),
            dma((4,)),
        ],
        compiler_params=pltpu.CompilerParams(
            collective_id=1, has_side_effects=True, vmem_limit_bytes=60 * 1024 * 1024
        ),
        name="opening",
    )(lengths, code_tile, vectors, up_bias, patches, padded, *own[:3])
    return results[:3], results[3], results[4].reshape(devices, -1, LANES), results[5], results[6:]


def plain_opening(lengths, codes, table, patches, codebook, own, swapped, ordered, row_count):
    section = lax.axis_index("section")
    other = tuple(swapped(weight) for weight in own)
    tables = jnp.stack(ordered(table, swapped(table)))
    all_codes = lax.all_gather(codes, "dp", axis=0, tiled=True)
    half_width = patches.shape[1] // 2
    half_book = lax.dynamic_slice_in_dim(codebook, section * half_width, half_width, 1)
    half_book = lax.all_gather(half_book, "dp", axis=0, tiled=True)
    half_rows = jnp.take(half_book, codes, axis=0)

    def micro_rows(array, index):
        return lax.dynamic_slice_in_dim(array, index * row_count, row_count, 0)

    half_own = micro_rows(half_rows, section)
    half_other = swapped(micro_rows(half_rows, 1 - section))
    chosen = jnp.concatenate(ordered(half_own, half_other), axis=1)
    encoded = block_forward(0, lengths, micro_rows(patches, section), tables, own, other)
    return other, tables, all_codes, chosen, encoded


def backward_steps(from_code, lengths_ref, table, buffers, sums_ref, weight, arrived, save, during):
    (
        rows_ref, hidden_ref, qkv_ref, mixed_ref, slope_ref, stat_ref, branch_ref, attn_ref, projected_ref,
        grad_ref, second_ref, moved_ref, query_marks, key_marks,
    ) = buffers
    rows, width = rows_ref.shape
    hidden_units = slope_ref.shape[1]
    head_size = width // HEADS
    per_block = LANES // head_size
    half = rows // 2
    per_row = width // TILE
    sums_ref[...] = jnp.zeros_like(sums_ref)

    fill_marks(lengths_ref, head_size, query_marks, key_marks)
    arrived(("grads",))
    total = jnp.zeros((1, width), jnp.float32)
    for start in range(0, rows, LANES):
        part = pl.ds(start, LANES)
        grad = moved_ref[part, :].astype(jnp.float32)
        if from_code:
            grad = grad_ref[part, :] + 0.5 * (second_ref[part, :] - grad)
        grad_ref[part, :] = grad
        branch = grad.astype(jnp.bfloat16)
        branch_ref[part, :] = branch
        total = total + column_sum(branch)
    sums_ref[7:8, :] = total
    save("branch")
    during("branch")

    down_held = weight(3)
    arrived(("slope", "hidden"))

    def through_gelu(first, count):
        at_once = 3 if count % 3 == 0 else 1

        @pl.loop(0, count // at_once)
        def _(group):
            def tile_of(j):
                return first + group * at_once + j

            def block_of(j):
                return pl.ds(pl.multiple_of(tile_of(j) * TILE, TILE), TILE)

            def act_of(j):
                return times_transposed(branch_ref[...], down_held[block_of(j), :])

            ahead = act_of(0)
            for j in range(at_once):
                grad_act, block = ahead, block_of(j)
                if j + 1 < at_once:
                    ahead = act_of(j + 1)
                grad_pre = (grad_act * slope_ref[:, block].astype(jnp.float32)).astype(jnp.bfloat16)
                slope_ref[:, block] = grad_pre
                column = pl.multiple_of(tile_of(j) % per_row * TILE, TILE)
                sums_ref[pl.ds(VECTORS + tile_of(j) // per_row, 1), pl.ds(column, TILE)] = column_sum(grad_pre)

    tiles = hidden_units // TILE
    through_gelu(0, tiles // 4)
    during("gelu")
    through_gelu(tiles // 4, tiles - tiles // 4)
    save("pre")
    during("pre")
    up_held = weight(2)
    for start in range(0, width, TILE):
        block = pl.ds(start, TILE)
        second_ref[:, block] = times_transposed(slope_ref[...], up_held[block, :])
    during("second")

    gain_total, shift_total, attn_total = (jnp.zeros((1, width), jnp.float32) for _ in range(3))
    for start in range(0, rows, LANES):
        part = pl.ds(start, LANES)
        hat, scale = normalized(hidden_ref[part, :])
        grad = second_ref[part, :]
        gain_total = gain_total + column_sum(grad * hat)
        shift_total = shift_total + column_sum(grad)
        grad_hidden = grad_ref[part, :] + norm_backward(grad, hat, scale, 1.0 + table[5:6, :])
        grad_ref[part, :] = grad_hidden
        attn = grad_hidden.astype(jnp.bfloat16)
        attn_ref[part, :] = attn
        attn_total = attn_total + column_sum(attn)
    sums_ref[5:6, :] = gain_total
    sums_ref[6:7, :] = shift_total
    sums_ref[4:5, :] = attn_total
    save("attn")

    out_held = weight(1)
    for start in range(0, width, TILE):
        block = pl.ds(start, TILE)
        moved_ref[:, block] = times_transposed(attn_ref[...], out_held[block, :]).astype(jnp.bfloat16)
    during("attn")
    arrived(("mixed", "qkv", "stat"))

    def through_heads(first, count):
        @pl.loop(first, first + count)
        def _(i):
            query = qkv_ref[:, lane_block(i)]
            grad_mixed = moved_ref[:, lane_block(i)]
            products = jnp.transpose(
                grad_mixed.astype(jnp.float32) * mixed_ref[:, lane_block(i)].astype(jnp.float32)
            )
            mine = [head_lanes(h, head_size, 1.0) for h in range(per_block)]
            scaled = [head_lanes(h, head_size, head_size**-0.5) for h in range(per_block)]
            query_of = [query * scaled[h] for h in range(per_block)]
            marked_of = [query_of[h] + query_marks[h] for h in range(per_block)]
            grad_of = [grad_mixed * mine[h] for h in range(per_block)]
            row_dot = [
                jnp.sum(products[h * head_size : (h + 1) * head_size, :], axis=0, keepdims=True)
                for h in range(per_block)
            ]
            units = [(start, h) for start in range(0, rows, half) for h in range(per_block)]

            def products_of(unit):
                start, h = unit
                part = pl.ds(start, half)
                keys = qkv_ref[part, lane_block(width // LANES + i)]
                values = qkv_ref[part, lane_block(2 * width // LANES + i)]
                return (
                    times_transposed(keys * mine[h] + key_marks[h, part, :], marked_of[h]),
                    times_transposed(values, grad_of[h]),
                )

            ahead = products_of(units[0])
            grad_query = jnp.zeros((rows, LANES), jnp.float32)
            value_total = jnp.zeros((1, LANES), jnp.float32)
            for number, (start, h) in enumerate(units):
                part = pl.ds(start, half)
                scores, grad_probs = ahead
                if number + 1 < len(units):
                    ahead = products_of(units[number + 1])
                keys = qkv_ref[part, lane_block(width // LANES + i)]
                exact = jnp.exp(scores - stat_ref[pl.ds(per_block * i + h, 1), :])
                grad_scores = (exact * (grad_probs - row_dot[h])).astype(jnp.bfloat16)
                value_term = times(exact.astype(jnp.bfloat16), grad_of[h])
                key_term = times(grad_scores, query_of[h])
                grad_query = grad_query + transposed_times(grad_scores, keys * scaled[h])
                grad_value = value_term if h == 0 else grad_value + value_term
                grad_key = key_term if h == 0 else grad_key + key_term
                if h == per_block - 1:
                    grad_value = grad_value.astype(jnp.bfloat16)
                    projected_ref[part, lane_block(2 * width // LANES + i)] = grad_value
                    projected_ref[part, lane_block(width // LANES + i)] = grad_key.astype(jnp.bfloat16)
                    value_total = value_total + column_sum(grad_value)
            grad_query = grad_query.astype(jnp.bfloat16)
            projected_ref[:, lane_block(i)] = grad_query
            sums_ref[2:3, lane_block(i)] = column_sum(grad_query)
            sums_ref[3:4, lane_block(i)] = value_total

    groups = width // LANES
    for part in range(3):
        first, end = groups * part // 3, groups * (part + 1) // 3
        if end > first:
            through_heads(first, end - first)
        during(("heads", part))

    save("projected")
    qkv_held = weight(0)
    for start in range(0, width, TILE):
        grad_rows = None
        for j in range(3):
            term = times_transposed(
                projected_ref[:, j * width : (j + 1) * width], qkv_held[pl.ds(j * width + start, TILE), :]
            )
            grad_rows = term if grad_rows is None else grad_rows + term
        second_ref[:, pl.ds(start, TILE)] = grad_rows
    during("rows")

    arrived(("rows",))
    gain_total, shift_total = (jnp.zeros((1, width), jnp.float32) for _ in range(2))
    for start in range(0, rows, LANES):
        part = pl.ds(start, LANES)
        hat, scale = normalized(rows_ref[part, :].astype(jnp.float32))
        grad = second_ref[part, :]
        gain_total = gain_total + column_sum(grad * hat)
        shift_total = shift_total + column_sum(grad)
        grad_rows = grad_ref[part, :] + norm_backward(grad, hat, scale, 1.0 + table[0:1, :])
        grad_ref[part, :] = grad_rows if from_code else grad_rows.astype(jnp.bfloat16).astype(jnp.float32)
    sums_ref[0:1, :] = gain_total
    sums_ref[1:2, :] = shift_total
    save("grad")


class BackwardWeights(Weights):
    def place(self, index):
        return self.held[index - 1], self.sems.at[index - 1]

    def start(self, index):
        if index != 0:
            super().start(index)
            return
        width = self.own[0].shape[0]

        def begin(matrix):
            for j in range(3):
                block = pl.ds(j * width, width)
                pltpu.make_async_copy(
                    matrix[0].at[:, block], self.held[2].at[block, :], self.sems.at[3 + j]
                ).start()

        @pl.when(self.own_flag == 1)
        def _():
            begin(self.own)

        @pl.when(self.own_flag != 1)
        def _():
            begin(self.other)

    def wait(self, index):
        if index == 0:
            width = self.own[0].shape[0]
            for j in range(3):
                block = pl.ds(j * width, width)
                pltpu.make_async_copy(
                    self.own[0].at[:, block], self.held[2].at[block, :], self.sems.at[3 + j]
                ).wait()
            return self.held[2]
        return super().wait(index)


def backward_scratch(own, row_count):
    width, hidden_units = own[2].shape
    bfloat16, float32 = jnp.bfloat16, jnp.float32
    return [pltpu.VMEM(w.shape, w.dtype) for w in own[1:]] + [
        pltpu.VMEM((row_count, width), bfloat16),
        pltpu.VMEM((row_count, width), float32),
        pltpu.VMEM((row_count, 3 * width), bfloat16),
        pltpu.VMEM((row_count, width), bfloat16),
        pltpu.VMEM((row_count, hidden_units), bfloat16),
        pltpu.VMEM((16, row_count), float32),
        pltpu.VMEM((row_count, width), bfloat16),
        pltpu.VMEM((row_count, width), bfloat16),
        pltpu.VMEM((row_count, 3 * width), bfloat16),
        pltpu.VMEM((row_count, width), float32),
        pltpu.VMEM((row_count, width), float32),
        pltpu.VMEM((row_count, width), bfloat16),
        pltpu.VMEM((2, row_count, LANES), bfloat16),
        pltpu.VMEM((2, row_count, LANES), bfloat16),
        pltpu.SemaphoreType.DMA((6,)),
        pltpu.SemaphoreType.DMA((9,)),
    ]


def backward_loads(kept, grads_in, buffers, sems, whole_rows, whole_grad):
    rows_hbm, hidden_hbm, qkv_hbm, mixed_hbm, slope_hbm, stat_hbm = kept
    rows_ref, hidden_ref, qkv_ref, mixed_ref, slope_ref, stat_ref = buffers[:6]
    row_count = rows_ref.shape[0]
    mine = pl.ds(pl.multiple_of(lax.axis_index("section") * row_count, row_count), row_count)
    if whole_rows:
        rows_hbm = rows_hbm.at[mine, :]
    if len(grads_in) == 1 and not whole_grad:
        grad_pairs = [(grads_in[0], buffers[11])]
    elif whole_grad:
        grad_pairs = [(grads_in[0].at[mine, :], buffers[11])]
    else:
        grad_pairs = list(zip(grads_in, buffers[9:12]))
    pairs = {
        "slope": [(slope_hbm, slope_ref)], "hidden": [(hidden_hbm, hidden_ref)], "mixed": [(mixed_hbm, mixed_ref)],
        "qkv": [(qkv_hbm, qkv_ref)], "stat": [(stat_hbm, stat_ref)], "rows": [(rows_hbm, rows_ref)],
    }
    copies, index = {}, 0
    for name, entries in [("grads", grad_pairs), *pairs.items()]:
        copies[name] = []
        for source, target in entries:
            copies[name].append(pltpu.make_async_copy(source, target, sems.at[index]))
            index = index + 1
    return copies


def start_copies(copies):
    for copy in copies:
        copy.start()


def wait_copies(copies):
    for copy in copies:
        copy.wait()


def backward_kernel(block, lengths_ref, tables_ref, *refs):
    from_code = block == 0
    grads_in, kept, own, other, made, (sums_ref,), held, buffers, (weight_sems, load_sems, save_sems) = split_refs(
        refs, (3 if from_code else 1, 6, 4, 4, 5, 1, 3, 14, 3)
    )
    weights = BackwardWeights(
        (lax.axis_index("section") == block).astype(jnp.int32), own, other,
        held, weight_sems,
    )
    loads = backward_loads(kept, grads_in, buffers, load_sems, from_code, not from_code)
    saves = {
        name: pltpu.make_async_copy(source, target, save_sems.at[index])
        for index, (name, source, target) in enumerate(zip(
            ("grad", "branch", "pre", "attn", "projected"),
            (buffers[9], buffers[6], buffers[4], buffers[7], buffers[8]),
            made,
        ))
    }
    start_copies(loads["grads"])
    weights.start(3)
    start_copies(loads["slope"])
    weights.start(2)
    start_copies(loads["hidden"])
    weights.start(1)
    for name in ("mixed", "qkv", "stat", "rows"):
        start_copies(loads[name])

    def arrived(names):
        for name in names:
            wait_copies(loads[name])

    def during(where):
        if where == "pre":
            weights.start(0)

    backward_steps(
        from_code, lengths_ref, tables_ref.at[block], buffers, sums_ref, weights.wait, arrived,
        lambda name: saves[name].start(), during,
    )
    for save in saves.values():
        save.wait()


def block_backward(block, lengths, tables, grads_in, kept, own, other):
    row_count, width = kept[1].shape
    hidden_units = own[2].shape[1]
    bfloat16, float32 = jnp.bfloat16, jnp.float32
    made = [
        ((row_count, width), float32),
        ((row_count, width), bfloat16),
        ((row_count, hidden_units), bfloat16),
        ((row_count, width), bfloat16),
        ((row_count, 3 * width), bfloat16),
        (tables.shape[1:], float32),
    ]
    return pl.pallas_call(
        functools.partial(backward_kernel, block),
        out_shape=tuple(jax.ShapeDtypeStruct(s, t) for s, t in made),
        in_specs=[in_smem(), in_vmem()] + [in_place()] * (14 + len(grads_in)),
        out_specs=[in_place()] * 5 + [in_vmem()],
        scratch_shapes=backward_scratch(own, row_count) + [pltpu.SemaphoreType.DMA((5,))],
        compiler_params=pltpu.CompilerParams(vmem_limit_bytes=56 * 1024 * 1024),
        cost_estimate=pl.CostEstimate(
            flops=2 * row_count * (12 * width * width + 5 * row_count * width),
            bytes_accessed=40 * 1024 * 1024,
            transcendentals=row_count * row_count * HEADS,
        ),
        name="block_backward",
    )(lengths, tables, *grads_in, *kept, *own, *other)


SLOTS, HELD, RING, LAST_RING = 4, 6, 16, 12


def chunk_list(width, hidden_units):
    ups = hidden_units // width

    def of(block, operand, count):
        return [(block, operand, j) for j in range(count)]

    return (
        of(1, 3, ups) + of(1, 2, ups) + of(1, 1, 1) + of(1, 0, 3)
        + of(0, 3, ups) + of(0, 2, ups) + of(0, 1, 1) + of(0, 0, 3)
    )


def count_codes_in(codes_ref, code_count, counts_ref, stats_ref):
    high_count = counts_ref.shape[0]
    high_rows = -(-high_count // 16) * 16

    @pl.loop(0, codes_ref.shape[0], init_carry=jnp.zeros((high_rows, LANES), jnp.float32))
    def counts(block, total):
        codes = codes_ref[block]

        def hot(values, size):
            rows = lax.broadcasted_iota(jnp.int32, (size, 1), 0)
            pieces = [jnp.where(values[j : j + 1, :] == rows, 1.0, 0.0) for j in range(codes.shape[0])]
            return jnp.concatenate(pieces, axis=1).astype(jnp.bfloat16)

        return total + times_transposed(hot(codes >> 7, high_rows), hot(codes & (LANES - 1), LANES))

    counts = counts[:high_count, :]
    counts_ref[...] = counts.astype(jnp.int32)
    share = counts / float(codes_ref.shape[0] * codes_ref.shape[1] * LANES)
    used = counts > 0.0
    terms = jnp.where(used, share * jnp.log(jnp.where(used, share, 1.0)), 0.0)
    usage = jnp.sum(jnp.where(used, 1.0, 0.0), axis=(0, 1), keepdims=True) / code_count
    perplexity = jnp.exp(-jnp.sum(terms, axis=(0, 1), keepdims=True)) / code_count
    stats_ref[...] = jnp.concatenate([usage, perplexity], axis=1)


def closing_kernel(chunks, code_count, lengths_ref, tables_ref, codes_ref, *refs):
    (
        dec_grads_in, enc_grads_in, dec_kept, enc_kept, own, other, dec_left, enc_left,
        results, (vector_sums_ref, bias_sums_ref, counts_ref, stats_ref, shown_out, grads_out), held_weights, buffers,
        (weight_sems, load_sems, enc_weight_sems, enc_load_sems),
        (stage, zero, held, one, two, three, finals, fourth), (narrow, wide), (dec_grad_ref, dec_sums, enc_sums),
        (sums_send, sums_zero, sums_held, sums_first, sums_second, sums_third),
        (operand_sems, zero_send, zero_got, first_send, first_got, second_send, second_got, third_send, third_got,
         fourth_send, fourth_got, swap_sems, credit),
    ) = split_refs(refs, (1, 1, 6, 6, 4, 4, 3, 3, 4, 6, 3, 14, 4, 8, 2, 3, 6, 13))
    count = len(chunks)
    depth, share, width = stage.shape[1], stage.shape[4], stage.shape[5]
    half = width // 2
    rows = buffers[0].shape[0]
    ups = sum(1 for block, operand, _ in chunks if block == 0 and operand == 3)
    section, place = lax.axis_index("section"), lax.axis_index("dp")
    my_x, my_y, my_z = place % 2, place // 2 % 2, place // 4
    beside_x, beside_y = place + 1 - 2 * my_x, place + 2 - 4 * my_y
    first_device = beside_x * (1 - section) + beside_y * section
    second_device = beside_y * (1 - section) + beside_x * section
    own_half = pl.ds(pl.multiple_of(section * half, LANES), half)
    other_half = pl.ds(pl.multiple_of((1 - section) * half, LANES), half)

    barrier = pltpu.get_barrier_semaphore()
    pl.semaphore_signal(barrier, inc=1, device_id={"section": 1 - section}, device_id_type=MESH)
    for device in (beside_x, beside_y):
        pl.semaphore_signal(barrier, inc=1, device_id={"dp": device}, device_id_type=MESH)
    for hop in range(1, depth):
        device = (my_z + hop) % depth * 4 + my_y * 2 + my_x
        pl.semaphore_signal(barrier, inc=1, device_id={"dp": device}, device_id_type=MESH)

    operands = {
        0: (narrow.at[1], buffers[8]), 1: (buffers[3], buffers[7]), 2: (narrow.at[0], buffers[4]), 3: (wide, buffers[6]),
    }
    moves = {}
    for block, left in ((0, enc_left), (1, dec_left)):
        for operand, source in ((0, left[0]), (2, left[1]), (3, left[2])):
            moves[block, operand] = pltpu.make_async_copy(
                source, operands[operand][0], operand_sems.at[block, operand]
            )

    def matrices(block, sems):
        return BackwardWeights((section == block).astype(jnp.int32), own, other, held_weights, sems)

    dec_weights, enc_weights = matrices(1, weight_sems), matrices(0, enc_weight_sems)
    dec_loads = backward_loads(dec_kept, dec_grads_in, buffers, load_sems, False, True)
    enc_loads = backward_loads(enc_kept, enc_grads_in, buffers, enc_load_sems, True, False)
    start_copies(dec_loads["grads"])
    moves[1, 3].start()
    dec_weights.start(3)
    start_copies(dec_loads["slope"])
    dec_weights.start(2)
    moves[1, 2].start()
    start_copies(dec_loads["hidden"])
    dec_weights.start(1)
    for name in ("mixed", "qkv", "stat", "rows"):
        start_copies(dec_loads[name])
    moves[1, 0].start()
    pl.semaphore_wait(barrier, 3 + depth - 1)

    def remote(source, land, send, got, **device):
        return pltpu.make_async_remote_copy(
            src_ref=source, dst_ref=land, send_sem=send, recv_sem=got, device_id=device, device_id_type=MESH
        )

    def across(k):
        if k == count:
            return remote(sums_send, sums_zero, zero_send.at[k], zero_got.at[k], section=1 - section)
        return remote(
            stage.at[k % SLOTS, :, :, :, :, other_half], zero.at[k % SLOTS], zero_send.at[k], zero_got.at[k],
            section=1 - section,
        )

    def first(k):
        if k == count:
            return remote(sums_held, sums_first, first_send.at[k], first_got.at[k], dp=first_device)
        return remote(
            held.at[k % HELD, 1], one.at[k % RING], first_send.at[k], first_got.at[k], dp=first_device
        )

    def second(k):
        if k == count:
            return remote(sums_first, sums_second, second_send.at[k], second_got.at[k], dp=second_device)
        return remote(
            one.at[k % RING, 1], two.at[k % RING], second_send.at[k], second_got.at[k], dp=second_device
        )

    def third(k, hop):
        target = (my_z + hop) % depth
        device = target * 4 + my_y * 2 + my_x
        send, got = third_send.at[k, hop - 1], third_got.at[k, hop - 1]
        if k == count:
            return remote(sums_second, sums_third.at[hop - 1], send, got, dp=device)
        return remote(two.at[k % RING, target], three.at[k % LAST_RING, hop - 1], send, got, dp=device)

    def last(k):
        index = k % (count // 2)
        return remote(finals.at[index], fourth.at[index], fourth_send.at[k], fourth_got.at[k], section=1 - section)

    def send_across(k):
        if k >= SLOTS:
            pl.semaphore_wait(credit, 1)
        across(k).start()

    def give(k):
        if k == count:
            dec, enc = dec_sums[...], enc_sums[...]
            sums_held[...] = jnp.where(section == 0, enc, dec)
            sums_send[...] = jnp.where(section == 0, dec, enc)
            across(k).start()
            return
        block, operand, j = chunks[k]
        key = (block, operand)
        if operand == 3 and j != 0:
            send_across(k)
            return
        if j == 0 and key in moves and key != (0, 3):
            moves[key].wait()
        made = range(k, k + ups) if operand == 3 else range(k, k + 1)
        for each in made:
            if each >= SLOTS:
                across(each - SLOTS).wait_send()
        left, right = operands[operand]
        if operand == 3:

            @pl.loop(0, depth)
            def _(tile):
                columns = pl.ds(pl.multiple_of(tile * 4 * ups * share, LANES), 4 * ups * share)
                product = transposed_times(left[:, columns], right[...]).astype(stage.dtype)
                product = product.reshape(2, 2, ups, share, width)
                for j in range(ups):
                    stage[(k + j) % SLOTS, tile] = product[:, :, j]

        else:
            product = transposed_times(left[...], right[:, j * width : (j + 1) * width]).astype(stage.dtype)
            stage[k % SLOTS] = product.reshape(depth, 2, 2, share, width)
        send_across(k)
        last_of_key = operand == 3 or k + 1 == count or chunks[k + 1][:2] != key
        if last_of_key and block == 1 and operand in (0, 2):
            moves[0, operand].start()

    def begin(k):
        across(k).wait_recv()
        if k == count:
            sums_held[...] = sums_held[...] + sums_zero[...]
            first(k).start()
            return
        if k >= HELD:
            first(k - HELD).wait_send()
        slot = k % SLOTS
        for a in range(2):
            for b in range(2):
                chip_x = (my_x + (a * (1 - section) + b * section)) % 2
                chip_y = (my_y + (b * (1 - section) + a * section)) % 2
                held[k % HELD, a, b] = stage[slot, :, chip_y, chip_x, :, own_half] + zero[slot, :, chip_y, chip_x]
        first(k).start()
        if k + SLOTS < count:
            pl.semaphore_signal(credit, inc=1, device_id={"section": 1 - section}, device_id_type=MESH)

    def after_first(k):
        first(k).wait_recv()
        if k == count:
            first(k).wait_send()
            sums_first[...] = sums_first[...] + sums_held[...]
        else:
            slot = k % RING
            one[slot] = one[slot] + held[k % HELD, 0]
        second(k).start()

    def after_second(k):
        second(k).wait()
        if k == count:
            sums_second[...] = sums_second[...] + sums_first[...]
        else:
            slot = k % RING
            two[slot] = two[slot] + one[slot, 0]
        for hop in range(1, depth):
            third(k, hop).start()

    def after_third(k):
        if k == count:
            total = sums_second[...]
            for hop in range(1, depth):
                third(k, hop).wait()
                total = total + sums_third[hop - 1]
            vector_sums_ref[...] = total[:VECTORS, :]
            bias_sums_ref[...] = jnp.zeros_like(bias_sums_ref)
            for j in range(ups):
                bias_sums_ref[0:1, j * width : (j + 1) * width] = total[VECTORS + j : VECTORS + j + 1, :]
            return
        block = chunks[k][0]
        slot = k % RING
        total = two[slot, my_z].astype(jnp.float32)
        for hop in range(1, depth):
            third(k, hop).wait()
            total = total + three[k % LAST_RING, hop - 1].astype(jnp.float32)

        @pl.when(section == block)
        def _():
            put(k, total, own_half, section * half)

        @pl.when(section != block)
        def _():
            finals[k % (count // 2)] = total
            last(k).start()

    def put(k, total, lanes, offset):
        _, operand, j = chunks[k]
        if operand == 3:
            results[3][j * share : (j + 1) * share, lanes] = total
        else:
            start = pl.multiple_of(j * width + offset, LANES)
            results[operand][:, pl.ds(start, half)] = total

    def after_fourth(k):
        if k == count:
            return
        block = chunks[k][0]

        @pl.when(section == block)
        def _():
            last(k).wait_recv()
            put(k, fourth[k % (count // 2)], other_half, (1 - section) * half)

        @pl.when(section != block)
        def _():
            last(k).wait_send()

    phases = ((1, begin), (0, give), (3, after_first), (5, after_second), (7, after_third), (8, after_fourth))

    def step(number):
        for phase, action in phases:
            for k in range(count + 1):
                if min(k, count - 1) // 2 + phase == number:
                    action(k)

    mine = pl.ds(pl.multiple_of(section * rows, rows), rows)

    def deliver(block, source, target, sem, start):
        stay = pltpu.make_async_copy(source, target.at[mine, :], swap_sems.at[sem, 0])
        go = remote(source, target.at[mine, :], swap_sems.at[sem, 1], swap_sems.at[sem, 2], section=1 - section)

        @pl.when(section == block)
        def _():
            if start:
                stay.start()
            else:
                stay.wait()
                go.wait_recv()

        @pl.when(section != block)
        def _():
            if start:
                go.start()
            else:
                go.wait_send()

    branch_buffer, grad_buffer, second_buffer = buffers[6], buffers[9], buffers[10]
    shown_dec = (1, branch_buffer, shown_out, 0)
    grads_dec = (1, dec_grad_ref, grads_out, 1)
    shown_enc = (0, branch_buffer, shown_out, 2)
    grads_enc = (0, grad_buffer, grads_out, 3)

    def once(act):
        seen = set()

        def acted(name):
            if name not in seen:
                seen.add(name)
                act(name)

        return acted

    dec_arrive = once(lambda name: wait_copies(dec_loads[name]))
    enc_arrive = once(lambda name: wait_copies(enc_loads[name]))
    enc_matrix = once(lambda index: enc_weights.wait(index))

    def enc_weight(index):
        enc_matrix(index)
        return held_weights[2] if index == 0 else enc_weights.place(index)[0]

    def dec_arrived(names):
        for name in names:
            dec_arrive(name)

    def enc_arrived(names):
        for name in names:
            enc_arrive(name)
        if "grads" in names:
            enc_arrive("hidden")
            moves[0, 3].wait()
            last_product(tables_ref.at[0], buffers[1], wide, enc_weight(3), second_buffer, None)

    dec_steps = {"branch": 0, "gelu": 1, "pre": 2, "attn": 3, ("heads", 2): 4, "rows": 5}
    enc_steps = {"branch": 6, "gelu": 7, "pre": 8, ("heads", 0): 9, ("heads", 2): 10}

    def during_decoder(where):
        if where == "pre":
            last_product(tables_ref.at[1], buffers[1], wide, held_weights[2], None, branch_buffer)
            deliver(*shown_dec, True)
            dec_weights.start(0)
            moves[0, 3].start()
        if where in dec_steps:
            step(dec_steps[where])
        if where == "second":
            enc_weights.start(2)
        elif where == "attn":
            start_copies(enc_loads["slope"])
            start_copies(enc_loads["hidden"])
            enc_weights.start(1)
        elif where == ("heads", 2):
            for name in ("mixed", "qkv", "stat"):
                start_copies(enc_loads[name])
        elif where == "rows":
            enc_weights.start(3)

    def during_encoder(where):
        if where == "pre":
            branch_buffer[...] = second_buffer[...].astype(branch_buffer.dtype)
            deliver(*shown_enc, True)
            enc_weights.start(0)
        if where in enc_steps:
            step(enc_steps[where])

    def nothing(name):
        return None

    backward_steps(
        False, lengths_ref, tables_ref.at[1], buffers, dec_sums, dec_weights.wait, dec_arrived, nothing,
        during_decoder,
    )
    start_copies(enc_loads["grads"])
    start_copies(enc_loads["rows"])
    dec_grad_ref[...] = grad_buffer[...]
    deliver(*grads_dec, True)
    deliver(*shown_dec, False)
    backward_steps(
        True, lengths_ref, tables_ref.at[0], buffers, enc_sums, enc_weight, enc_arrived, nothing, during_encoder,
    )
    deliver(*grads_enc, True)
    for number in range(11, (count - 1) // 2 + 9):
        step(number)
        if number == 13:
            count_codes_in(codes_ref, code_count, counts_ref, stats_ref)
    for parts in (grads_dec, shown_enc, grads_enc):
        deliver(*parts, False)
    for k in range(count + 1):
        if k + SLOTS >= count:
            across(k).wait_send()
        if k != count and k + HELD >= count:
            first(k).wait_send()


def closing(lengths, tables, codes, code_count, cotangent, enc_grads_in, dec_kept, enc_kept, own, other, dec_left, enc_left, devices):
    row_count, width = dec_kept[0].shape
    hidden_units = own[2].shape[1]
    chunks = chunk_list(width, hidden_units)
    count, depth, share, half = len(chunks), devices // 4, width // devices, width // 2
    bfloat16, float32 = jnp.bfloat16, jnp.float32
    tokens = cotangent.shape[0]
    table = pltpu.VMEM(tables.shape[1:], float32)
    dma = pltpu.SemaphoreType.DMA
    shapes = [
        ((share, 3 * width), float32),
        ((share, width), float32),
        ((share, hidden_units), float32),
        ((hidden_units // devices, width), float32),
        ((VECTORS, width), float32),
        ((8, hidden_units), float32),
        ((-(-code_count // LANES), LANES), jnp.int32),
        ((1, 2), float32),
        ((tokens, width), bfloat16),
        ((tokens, width), float32),
    ]
    return pl.pallas_call(
        functools.partial(closing_kernel, chunks, code_count),
        out_shape=tuple(jax.ShapeDtypeStruct(s, t) for s, t in shapes),
        in_specs=[in_smem()] + [in_vmem()] * 2 + [in_place()] * 28,
        out_specs=[in_vmem()] * 8 + [in_place()] * 2,
        scratch_shapes=backward_scratch(own, row_count)
        + [
            dma((6,)),
            dma((9,)),
            pltpu.VMEM((SLOTS, depth, 2, 2, share, width), bfloat16),
            pltpu.VMEM((SLOTS, depth, 2, 2, share, half), bfloat16),
            pltpu.VMEM((HELD, 2, 2, depth, share, half), bfloat16),
            pltpu.VMEM((RING, 2, depth, share, half), bfloat16),
            pltpu.VMEM((RING, depth, share, half), bfloat16),
            pltpu.VMEM((LAST_RING, depth - 1, share, half), bfloat16),
            pltpu.VMEM((count // 2, share, half), float32),
            pltpu.VMEM((count // 2, share, half), float32),
            pltpu.VMEM((2, row_count, width), bfloat16),
            pltpu.VMEM((row_count, hidden_units), bfloat16),
            pltpu.VMEM((row_count, width), float32),
            table,
            table,
            table,
            table,
            table,
            table,
            table,
            pltpu.VMEM((depth - 1, *tables.shape[1:]), float32),
            dma((2, 4)),
        ]
        + [dma((count + 1,))] * 6
        + [dma((count + 1, depth - 1))] * 2
        + [dma((count,))] * 2
        + [dma((4, 3)), pltpu.SemaphoreType.REGULAR],
        compiler_params=pltpu.CompilerParams(
            collective_id=0, has_side_effects=True, vmem_limit_bytes=62 * 1024 * 1024
        ),
        name="closing",
    )(lengths, tables, codes, cotangent, *enc_grads_in, *dec_kept, *enc_kept, *own, *other, *dec_left, *enc_left)


def finish_kernel(vectors_ref, bias_ref, *refs):
    sources, targets, (bias_out, vectors_out), held, (in_sems, out_sems) = split_refs(refs, (6, 6, 2, 6, 2))
    loads = [pltpu.make_async_copy(s, h, in_sems.at[i]) for i, (s, h) in enumerate(zip(sources, held))]
    saves = [pltpu.make_async_copy(h, t, out_sems.at[i]) for i, (h, t) in enumerate(zip(held, targets))]
    start_copies(loads)
    place = lax.axis_index("dp")

    def from_place(ref, out):
        whole, part = ref.shape[1], out.shape[1]
        turned = pltpu.roll(ref[...], (whole - place * part) % whole, 1)
        out[...] = turned[: out.shape[0], :part]

    from_place(vectors_ref, vectors_out)
    from_place(bias_ref, bias_out)
    for load, save in zip(loads, saves):
        load.wait()
        save.start()
    wait_copies(saves)


def finish(results, vector_sums, bias_sums, devices):
    small = [
        jax.ShapeDtypeStruct((1, bias_sums.shape[1] // devices), jnp.float32),
        jax.ShapeDtypeStruct((VECTORS, vector_sums.shape[1] // devices), jnp.float32),
    ]
    return pl.pallas_call(
        finish_kernel,
        out_shape=tuple(jax.ShapeDtypeStruct(a.shape, a.dtype) for a in results) + tuple(small),
        in_specs=[in_vmem()] * 2 + [in_place()] * 6,
        out_specs=[in_place()] * 6 + [in_vmem()] * 2,
        scratch_shapes=[pltpu.VMEM(a.shape, a.dtype) for a in results]
        + [pltpu.SemaphoreType.DMA((6,)), pltpu.SemaphoreType.DMA((6,))],
        compiler_params=pltpu.CompilerParams(vmem_limit_bytes=60 * 1024 * 1024),
        name="finish",
    )(vector_sums, bias_sums, *results)


def count_codes(all_codes, code_count):
    high = -(-code_count // LANES)
    high_hot = (all_codes[:, None] // LANES == jnp.arange(high, dtype=jnp.int32)).astype(jnp.bfloat16)
    low_hot = (all_codes[:, None] % LANES == jnp.arange(LANES, dtype=jnp.int32)).astype(jnp.bfloat16)
    counts = transposed_times(high_hot, low_hot)
    return counts.reshape(-1)[:code_count].astype(jnp.int32)


def code_statistics(histogram, rows):
    code_share = histogram.astype(jnp.float32) / rows
    is_used = histogram > 0
    usage_share = jnp.mean(is_used.astype(jnp.float32))
    entropy = -jnp.sum(
        jnp.where(is_used, code_share * jnp.log(jnp.where(is_used, code_share, 1.0)), 0.0)
    )
    return jnp.stack([usage_share, jnp.exp(entropy) / histogram.shape[0]])


def plain_closing(
    is_first, lengths, tables, cotangent, enc_grads_in, dec_kept, enc_kept, own, other, encoded, decoded, shown,
    swapped, ordered, vector_count, width,
):
    code_grad, dec_branch, dec_pre, dec_attn, dec_projected, dec_sums = block_backward(
        1, lengths, tables, (cotangent,), dec_kept, own, other
    )
    grad, branch, pre, attn, projected, enc_sums = block_backward(
        0, lengths, tables, (code_grad, *enc_grads_in), enc_kept, own, other
    )
    encoder = ((encoded[1], encoded[3], encoded[4], encoded[6]), (projected, attn, pre, branch))
    decoder = ((decoded[1], decoded[3], decoded[4], decoded[6]), (dec_projected, dec_attn, dec_pre, dec_branch))
    results = []
    for index in range(4):
        enc = transposed_times(encoder[0][index], encoder[1][index])
        dec = transposed_times(decoder[0][index], decoder[1][index])
        results.append(jnp.where(is_first, enc, dec) + swapped(jnp.where(is_first, dec, enc)))
    own_sums, other_sums = ordered(enc_sums, dec_sums)
    sums = own_sums + swapped(other_sums)
    bias_rows = own[2].shape[1] // width
    results = results + [sums[vector_count : vector_count + bias_rows].reshape(-1), sums[:vector_count]]
    weight_grads = tuple(
        lax.psum_scatter(part, "dp", scatter_dimension=axis, tiled=True)
        for part, axis in zip(results, (0, 0, 0, 0, 0, 1))
    )

    def both_micro(enc_rows, dec_rows):
        own_rows, other_rows = ordered(enc_rows, dec_rows)
        return jnp.concatenate(ordered(own_rows, swapped(other_rows)), axis=0)

    return weight_grads, both_micro(*shown), both_micro(grad, code_grad)


def body(
    patches,
    cotangent,
    codes,
    lengths,
    codebook,
    qkv_weight,
    out_weight,
    up_weight,
    down_weight,
    up_bias,
    vectors,
):
    section_index = lax.axis_index("section")
    is_first = section_index == 0
    devices = lax.axis_size("dp")
    tok_rows, model_width = patches.shape
    row_count = tok_rows // lengths.shape[0]
    code_count = codebook.shape[0] * devices

    def swapped(array):
        return lax.ppermute(array, "section", [(0, 1), (1, 0)])

    def ordered(own, other):
        return jnp.where(is_first, own, other), jnp.where(is_first, other, own)

    own = (qkv_weight[0], out_weight[0], up_weight[0], down_weight[0])
    if devices == 16:
        other, tables, all_codes, chosen, encoded = opening(
            lengths, codes, vectors, up_bias, patches, codebook, own, devices, row_count
        )
        decoded, other_down = forward_swap(lengths, chosen, tables, own, other)
        other = (*other, other_down)
    else:
        other, tables, all_codes, chosen, encoded = plain_opening(
            lengths, codes, table_of(vectors[0], up_bias[0]), patches, codebook, own, swapped, ordered, row_count
        )
        decoded = block_forward(1, lengths, chosen, tables, own, other)
        shown = (encoded[8], decoded[8])
        enc_grads_in = (encoded[0], chosen)
        encoded, decoded = ((*made[1:8], made[9]) for made in (encoded, decoded))

    def saved(rows, made):
        hidden, _, projected, mixed, _, slope, _, stats = made
        return rows, hidden, projected, mixed, slope, stats

    if devices == 16:
        *weight_grads, vector_sums, bias_sums, counts, code_stats, outputs, input_grad = closing(
            lengths, tables, all_codes, code_count, cotangent, (chosen,), saved(chosen, decoded),
            saved(patches, encoded), own, other, (decoded[1], decoded[4], decoded[6]),
            (encoded[1], encoded[4], encoded[6]), devices,
        )
        histogram, code_stats = counts.reshape(-1)[:code_count], code_stats[0]
        *weight_grads, outputs, input_grad, bias_grad, vector_grad = finish(
            (*weight_grads, outputs, input_grad), vector_sums, bias_sums, devices
        )
        weight_grads = (*weight_grads, bias_grad[0], vector_grad)
    else:
        histogram = count_codes(all_codes, code_count)
        code_stats = code_statistics(histogram, tok_rows * devices)
        weight_grads, outputs, input_grad = plain_closing(
            is_first, lengths, tables, cotangent, enc_grads_in, saved(chosen, decoded), saved(patches, encoded), own,
            other, encoded, decoded, shown, swapped, ordered, vectors.shape[1], model_width,
        )
    return (outputs[None], input_grad[None], *(part[None] for part in weight_grads), histogram, code_stats)


def solution(mesh):
    placed = (
        P("dp", None),
        P("dp", None),
        P("dp"),
        P("dp", None),
        P("dp", None),
        P("section", None, None),
        P("section", None, None),
        P("section", None, None),
        P("section", None, None),
        P("section", None),
        P("section", None, None),
    )
    return jax.shard_map(
        body,
        mesh=mesh,
        in_specs=placed,
        out_specs=(
            P("section", "dp", None),
            P("section", "dp", None),
            P("section", "dp", None),
            P("section", "dp", None),
            P("section", "dp", None),
            P("section", "dp", None),
            P("section", "dp"),
            P("section", None, "dp"),
            P(),
            P(),
        ),
        check_vma=False,
    )
```

```python
import functools
import math

import jax
import jax.numpy as jnp
from jax import lax
from jax.experimental import pallas as pl
from jax.experimental.pallas import tpu as pltpu
from jax.sharding import PartitionSpec as P

HEADS = 12
LANES = 128
TILE = 256
MESH = pl.DeviceIdType.MESH
MASKED = -1e30
GELU_SCALE = math.sqrt(2.0 / math.pi)
GELU_CUBIC = 0.044715


def times_transposed(first_term, second_term):
    return lax.dot_general(
        first_term, second_term, (((1,), (1,)), ((), ())), preferred_element_type=jnp.float32
    )


def transposed_times(first_term, second_term):
    return lax.dot_general(
        first_term, second_term, (((0,), (0,)), ((), ())), preferred_element_type=jnp.float32
    )


def times(first_term, second_term):
    return jnp.dot(first_term, second_term, preferred_element_type=jnp.float32)


def in_vmem():
    return pl.BlockSpec(memory_space=pltpu.VMEM)


def in_smem():
    return pl.BlockSpec(memory_space=pltpu.SMEM)


def in_place():
    return pl.BlockSpec(memory_space=pl.ANY)


def normalized(rows):
    row_mean = jnp.mean(rows, axis=-1, keepdims=True)
    centered = rows - row_mean
    variance = jnp.mean(centered * centered, axis=-1, keepdims=True)
    scale = lax.rsqrt(variance + 1e-06)
    return centered * scale, scale


def norm_backward(grad, hat, scale, gain_row):
    grad_hat = grad * gain_row
    first = jnp.mean(grad_hat, axis=-1, keepdims=True)
    second = jnp.mean(grad_hat * hat, axis=-1, keepdims=True)
    return scale * (grad_hat - first - hat * second)


def column_sum(rows):
    return jnp.sum(rows.astype(jnp.float32), axis=0, keepdims=True)


def fill_marks(lengths_ref, head_size, query_marks, key_marks):
    heads, rows, _ = query_marks.shape
    images = lengths_ref.shape[1]
    for head in range(heads):
        lane = lax.broadcasted_iota(jnp.int32, (1, LANES), 1) - (1 - head) * head_size
        inside = jnp.logical_and(lane >= 0, lane < images)
        for start in range(0, rows, LANES):
            positions = lax.broadcasted_iota(jnp.int32, (LANES, 1), 0) + start
            end, label = 0, jnp.zeros_like(positions)
            for image in range(images - 1):
                end = end + lengths_ref[lax.axis_index("section"), image]
                label = label + (positions >= end).astype(jnp.int32)
            same = label == lane
            other = jnp.logical_and(inside, jnp.logical_not(same))
            same = jnp.logical_and(inside, same)
            part = pl.ds(start, LANES)
            query_marks[head, part, :] = jnp.where(other, MASKED, 0.0).astype(jnp.bfloat16)
            key_marks[head, part, :] = jnp.where(same, 1.0, 0.0).astype(jnp.bfloat16)


def head_lanes(head, head_size, factor):
    lane = lax.broadcasted_iota(jnp.int32, (1, LANES), 1)
    inside = jnp.logical_and(lane >= head * head_size, lane < (head + 1) * head_size)
    return jnp.where(inside, factor, 0.0).astype(jnp.bfloat16)


def lane_block(index):
    return pl.ds(pl.multiple_of(index * LANES, LANES), LANES)


class Weights:
    def __init__(self, own_flag, own, other, held, sems):
        self.own_flag, self.own, self.other, self.held, self.sems = own_flag, own, other, held, sems

    def place(self, index):
        return self.held[index], self.sems.at[index]

    def start(self, index):
        @pl.when(self.own_flag == 1)
        def _():
            pltpu.make_async_copy(self.own[index], *self.place(index)).start()

        @pl.when(self.own_flag != 1)
        def _():
            pltpu.make_async_copy(self.other[index], *self.place(index)).start()

    def wait(self, index):
        pltpu.make_async_copy(self.own[index], *self.place(index)).wait()
        return self.place(index)[0]


def table_of(vectors, up_bias):
    width = vectors.shape[1]
    rows = jnp.concatenate([vectors, up_bias.reshape(-1, width)], axis=0).astype(jnp.float32)
    return jnp.pad(rows, ((0, -rows.shape[0] % 8), (0, 0)))


def up_bias_tile(table, first_row, j, width):
    per_row = width // TILE
    column = pl.multiple_of(j % per_row * TILE, TILE)
    return table[pl.ds(first_row + j // per_row, 1), pl.ds(column, TILE)]


VECTORS = 8
GROUP = 1 << 14
UNROLL = 4
PIECES = 3
SAVED = ("out", "hidden", "normed", "qkv", "mixed", "second", "slope", "act", "shown")


def saved_shapes(row_count, width, hidden_units):
    bfloat16, float32 = jnp.bfloat16, jnp.float32
    return [
        ((row_count, width), float32),
        ((row_count, width), float32),
        ((row_count, width), bfloat16),
        ((row_count, 3 * width), bfloat16),
        ((row_count, width), bfloat16),
        ((row_count, width), bfloat16),
        ((row_count, hidden_units), bfloat16),
        ((row_count, hidden_units), bfloat16),
        ((row_count, width), bfloat16),
    ]


def turned_sources(buffers, work):
    out, hidden, _, qkv, mixed, _, *rest = buffers
    return (out, hidden, work[4], qkv, mixed, work[5], *rest)


def turned_shapes(kept):
    return [((shape[1], shape[0]), kind) if index in (2, 5) else (shape, kind) for index, (shape, kind) in enumerate(kept)]


def forward_steps(table, lengths_ref, rows_ref, stat_ref, buffers, work, weight, save, during):
    _, hidden_ref, normed_ref, qkv_ref, mixed_ref, second_ref = buffers[:6]
    query_marks, key_marks, max_columns, sum_columns, normed_turned, second_turned = work
    rows, width = rows_ref.shape
    head_size = width // HEADS
    per_block = LANES // head_size
    half = rows // 2
    per_part = width // TILE

    fill_marks(lengths_ref, head_size, query_marks, key_marks)
    for start in range(0, rows, LANES):
        part = pl.ds(start, LANES)
        hat, _ = normalized(rows_ref[part, :].astype(jnp.float32))
        normed_ref[part, :] = (hat * (1.0 + table[0:1, :]) + table[1:2, :]).astype(jnp.bfloat16)
    normed_turned[...] = jnp.transpose(normed_ref[...])
    save("normed")
    during("normed", 0)

    qkv_held = weight(0)
    for j in range(3 * per_part):
        columns = pl.ds(j * TILE, TILE)
        projected = times(normed_ref[...], qkv_held[:, columns])
        if j // per_part != 1:
            row = 2 + j // (2 * per_part)
            projected = projected + table[row : row + 1, pl.ds(j % per_part * TILE, TILE)]
        qkv_ref[:, columns] = projected.astype(jnp.bfloat16)

    save("qkv")
    during("qkv", 0)
    max_columns[...] = jnp.zeros_like(max_columns)
    sum_columns[...] = jnp.ones_like(sum_columns)

    @pl.loop(0, width // LANES)
    def _(i):
        keys = qkv_ref[:, lane_block(width // LANES + i)]
        values = qkv_ref[:, lane_block(2 * width // LANES + i)]
        lane = lax.broadcasted_iota(jnp.int32, (1, LANES), 1)
        keys_of = [keys * head_lanes(h, head_size, 1.0) + key_marks[h] for h in range(per_block)]
        values_of = [
            values * head_lanes(h, head_size, 1.0) + head_lanes(1 - h, head_size, 1.0) for h in range(per_block)
        ]
        units = [(start, h) for start in range(0, rows, half) for h in range(per_block)]

        def scores_of(unit):
            start, h = unit
            part = pl.ds(start, half)
            query = qkv_ref[part, lane_block(i)] * head_lanes(h, head_size, head_size**-0.5) + query_marks[h, part, :]
            return times_transposed(query, keys_of[h])

        ahead = scores_of(units[0])
        mixed = None
        for number, (start, h) in enumerate(units):
            part = pl.ds(start, half)
            scores = ahead
            if number + 1 < len(units):
                ahead = scores_of(units[number + 1])
            row_max = jnp.max(scores, axis=-1, keepdims=True)
            exponent = jnp.exp(scores - row_max).astype(jnp.bfloat16)
            sums = times(exponent, values_of[h])
            inside = jnp.logical_and(lane >= h * head_size, lane < (h + 1) * head_size)
            row_total = jnp.where(inside, pltpu.roll(sums, head_size, 1), sums)
            term = sums / row_total
            mixed = term if h == 0 else jnp.where(inside, term, mixed)
            here = lane == per_block * i + h
            max_columns[part, :] = jnp.where(here, row_max, max_columns[part, :])
            sum_columns[part, :] = jnp.where(here, row_total, sum_columns[part, :])
            if h == per_block - 1:
                mixed_ref[part, lane_block(i)] = mixed.astype(jnp.bfloat16)
        during("heads", i)

    save("mixed")
    stats = max_columns[...] + jnp.log(sum_columns[...])
    stat_ref[...] = jnp.transpose(stats)[: stat_ref.shape[0], :]

    out_held = weight(1)
    for start in range(0, width, TILE):
        columns = pl.ds(start, TILE)
        hidden_ref[:, columns] = (
            rows_ref[:, columns].astype(jnp.float32)
            + times(mixed_ref[...], out_held[:, columns])
            + table[4:5, columns]
        )
    save("hidden")
    for start in range(0, rows, LANES):
        part = pl.ds(start, LANES)
        hat, _ = normalized(hidden_ref[part, :])
        second_ref[part, :] = (hat * (1.0 + table[5:6, :]) + table[6:7, :]).astype(jnp.bfloat16)
    second_turned[...] = jnp.transpose(second_ref[...])
    save("second")
    during("second", 0)


def up_product(table, second_ref, up_held, slope_ref, act_ref):
    tiles, width = up_held.shape[1] // TILE, second_ref.shape[1]

    @pl.loop(0, tiles // UNROLL)
    def _(group):
        def columns_of(j):
            return pl.ds(pl.multiple_of((group * UNROLL + j) * TILE, TILE), TILE)

        def pre_of(j):
            return times(second_ref[...], up_held[:, columns_of(j)])

        ahead = pre_of(0)
        for j in range(UNROLL):
            pre = ahead + up_bias_tile(table, VECTORS, group * UNROLL + j, width)
            if j + 1 < UNROLL:
                ahead = pre_of(j + 1)
            square = pre * pre
            bent = jnp.tanh(pre * (GELU_SCALE + (GELU_SCALE * GELU_CUBIC) * square))
            share = 0.5 + 0.5 * bent
            act_ref[:, columns_of(j)] = (pre * share).astype(jnp.bfloat16)
            steep = (0.5 - 0.5 * (bent * bent)) * (GELU_SCALE + (3.0 * GELU_SCALE * GELU_CUBIC) * square)
            slope_ref[:, columns_of(j)] = (share + pre * steep).astype(jnp.bfloat16)


def last_product(table, hidden_ref, act_ref, down_held, out_ref, shown_ref):
    for start in range(0, hidden_ref.shape[1], TILE):
        columns = pl.ds(start, TILE)
        result = hidden_ref[:, columns] + times(act_ref[...], down_held[:, columns]) + table[7:8, columns]
        if out_ref is not None:
            out_ref[:, columns] = result
        if shown_ref is not None:
            shown_ref[:, columns] = result.astype(jnp.bfloat16)


def forward_kernel(block, lengths_ref, rows_ref, tables_ref, *refs):
    own, other, made, (stat_ref,), held, buffers, work, (weight_sems, save_sems) = split_refs(
        refs, (4, 4, 9, 1, 4, 9, 6, 2)
    )
    weights = Weights((lax.axis_index("section") == block).astype(jnp.int32), own, other, held, weight_sems)
    for index in range(4):
        weights.start(index)
    saves = {
        name: pltpu.make_async_copy(source, target, save_sems.at[index])
        for index, (name, source, target) in enumerate(zip(SAVED, turned_sources(buffers, work), made))
    }
    table = tables_ref.at[block]
    forward_steps(
        table, lengths_ref, rows_ref, stat_ref, buffers, work, weights.wait,
        lambda name: saves[name].start(), lambda place, i: None,
    )
    up_product(table, buffers[5], weights.wait(2), buffers[6], buffers[7])
    last_product(table, buffers[1], buffers[7], weights.wait(3), buffers[0], buffers[8])
    for name in ("slope", "act", "out", "shown"):
        saves[name].start()
    for save in saves.values():
        save.wait()


def forward_work(row_count, width):
    return [
        pltpu.VMEM((2, row_count, LANES), jnp.bfloat16),
        pltpu.VMEM((2, row_count, LANES), jnp.bfloat16),
        pltpu.VMEM((row_count, LANES), jnp.float32),
        pltpu.VMEM((row_count, LANES), jnp.float32),
        pltpu.VMEM((width, row_count), jnp.bfloat16),
        pltpu.VMEM((width, row_count), jnp.bfloat16),
    ]


def forward_scratch(own, kept, row_count):
    return (
        [pltpu.VMEM(w.shape, w.dtype) for w in own]
        + [pltpu.VMEM(s, t) for s, t in kept]
        + forward_work(row_count, kept[0][0][1])
        + [pltpu.SemaphoreType.DMA((4,)), pltpu.SemaphoreType.DMA((9,))]
    )


def forward_swap_kernel(lengths_ref, rows_ref, tables_ref, *refs):
    (
        own, other, (own_down,), made, (stat_ref, other_down), held, buffers, work,
        (own_held, other_held, weight_sems, save_sems, down_sems),
    ) = split_refs(refs, (3, 3, 1, 7, 2, 3, 8, 6, 5))
    section = lax.axis_index("section")
    barrier = pltpu.get_barrier_semaphore()
    pl.semaphore_signal(barrier, inc=1, device_id={"section": 1 - section}, device_id_type=MESH)
    weights = Weights((section == 1).astype(jnp.int32), own, other, held, weight_sems)
    for index in range(3):
        weights.start(index)
    size = own_down.shape[0] // PIECES
    parts = [pl.ds(piece * size, size) for piece in range(PIECES)]
    loads = [
        pltpu.make_async_copy(own_down.at[part], own_held.at[part], down_sems.at[0, piece])
        for piece, part in enumerate(parts)
    ]
    start_copies(loads)
    pl.semaphore_wait(barrier, 1)
    swaps = [
        pltpu.make_async_remote_copy(
            src_ref=own_held.at[part], dst_ref=other_held.at[part], send_sem=down_sems.at[1, piece],
            recv_sem=down_sems.at[2, piece], device_id={"section": 1 - section}, device_id_type=MESH,
        )
        for piece, part in enumerate(parts)
    ]
    for load, swap in zip(loads, swaps):
        load.wait()
        swap.start()
    saves = {
        name: pltpu.make_async_copy(source, target, save_sems.at[index])
        for index, (name, source, target) in enumerate(zip(SAVED[1:8], turned_sources(buffers, work)[1:], made))
    }
    forward_steps(
        tables_ref.at[1], lengths_ref, rows_ref, stat_ref, buffers, work, weights.wait,
        lambda name: saves[name].start(), lambda place, i: None,
    )
    wait_copies(swaps)
    keep = pltpu.make_async_copy(other_held, other_down, down_sems.at[0, 0])
    keep.start()
    up_product(tables_ref.at[1], buffers[5], weights.wait(2), buffers[6], buffers[7])
    saves["slope"].start()
    saves["act"].start()
    for save in saves.values():
        save.wait()
    keep.wait()


def forward_swap(lengths, rows, tables, own, other):
    row_count, width = rows.shape
    kept = saved_shapes(row_count, width, own[2].shape[1])[:8]
    shapes = turned_shapes(kept)[1:] + [((16, row_count), jnp.float32), (own[3].shape, own[3].dtype)]
    results = pl.pallas_call(
        forward_swap_kernel,
        out_shape=tuple(jax.ShapeDtypeStruct(s, t) for s, t in shapes),
        in_specs=[in_smem()] + [in_vmem()] * 2 + [in_place()] * 7,
        out_specs=[in_place()] * 7 + [in_vmem(), in_place()],
        scratch_shapes=[pltpu.VMEM(w.shape, w.dtype) for w in own[:3]]
        + [pltpu.VMEM(s, t) for s, t in kept]
        + forward_work(row_count, width)
        + [
            pltpu.VMEM(own[3].shape, own[3].dtype),
            pltpu.VMEM(own[3].shape, own[3].dtype),
            pltpu.SemaphoreType.DMA((4,)),
            pltpu.SemaphoreType.DMA((9,)),
            pltpu.SemaphoreType.DMA((3, PIECES)),
        ],
        compiler_params=pltpu.CompilerParams(
            collective_id=2, has_side_effects=True, vmem_limit_bytes=56 * 1024 * 1024
        ),
        name="forward_swap",
    )(lengths, rows, tables, *own[:3], *other, own[3])
    return results[:8], results[8]


def block_forward(block, lengths, rows, tables, own, other):
    row_count, width = rows.shape
    kept = saved_shapes(row_count, width, own[2].shape[1])
    stat_shape = (16, row_count)
    return pl.pallas_call(
        functools.partial(forward_kernel, block),
        out_shape=tuple(jax.ShapeDtypeStruct(s, t) for s, t in turned_shapes(kept))
        + (jax.ShapeDtypeStruct(stat_shape, jnp.float32),),
        in_specs=[in_smem()] + [in_vmem()] * 2 + [in_place()] * 8,
        out_specs=[in_place()] * 9 + [in_vmem()],
        scratch_shapes=forward_scratch(own, kept, row_count),
        compiler_params=pltpu.CompilerParams(vmem_limit_bytes=56 * 1024 * 1024),
        cost_estimate=pl.CostEstimate(
            flops=2 * row_count * (12 * width * width + 2 * row_count * width),
            bytes_accessed=40 * 1024 * 1024,
            transcendentals=row_count * row_count * HEADS,
        ),
        name="block_forward",
    )(lengths, rows, tables, *own, *other)


def split_refs(refs, counts):
    groups, start = [], 0
    for count in counts:
        groups.append(refs[start : start + count])
        start = start + count
    return groups


def opening_kernel(real_shard, lengths_ref, code_tile_ref, vectors_ref, up_bias_ref, patches_ref, book_ref, book_end_ref, *refs):
    (
        own, other, (tables_ref, all_codes_ref, chosen_ref), made, (stat_ref,), held, buffers, work,
        (weight_sems, save_sems),
        (rows_ref, book, total, half_out, half_in, table_in, code_slots, table_out, codes_ref),
        (load_sems, weight_send, weight_got, zero_send, zero_got, middle_send, middle_got, last_send, last_got,
         code_send, code_got, side_send, side_got, keep_sems),
    ) = split_refs(refs, (3, 3, 3, 7, 1, 3, 8, 6, 2, 9, 14))
    section, place = lax.axis_index("section"), lax.axis_index("dp")
    depth = book.shape[2]
    shard_rows, half_width = book.shape[3:]
    rows = rows_ref.shape[0]
    my_x, my_y, my_z = place % 2, place // 2 % 2, place // 4
    my_middle = my_y * (1 - section) + my_x * section
    my_last = my_x * (1 - section) + my_y * section
    middle_device = place + (1 - 2 * my_middle) * (2 - section)
    last_device = place + (1 - 2 * my_last) * (1 + section)

    barrier = pltpu.get_barrier_semaphore()
    pl.semaphore_signal(barrier, inc=1, device_id={"section": 1 - section}, device_id_type=MESH)
    for device in (middle_device, last_device):
        pl.semaphore_signal(barrier, inc=1, device_id={"dp": device}, device_id_type=MESH)
    for hop in range(1, depth):
        device = (my_z + hop) % depth * 4 + my_y * 2 + my_x
        pl.semaphore_signal(barrier, inc=1, device_id={"dp": device}, device_id_type=MESH)

    own_book = book.at[my_middle, my_last, my_z]
    columns = pl.ds(pl.multiple_of(section * half_width, LANES), half_width)
    whole = shard_rows - book_end_ref.shape[0]
    load_book = pltpu.make_async_copy(
        book_ref.at[pl.ds(0, whole), columns], own_book.at[pl.ds(0, whole)], load_sems.at[0]
    )
    load_end = pltpu.make_async_copy(
        book_end_ref.at[:, columns], own_book.at[pl.ds(whole, shard_rows - whole)], load_sems.at[2]
    )
    load_end.start()
    load_book.start()
    load_rows = pltpu.make_async_copy(
        patches_ref.at[pl.ds(pl.multiple_of(section * rows, rows), rows)], rows_ref, load_sems.at[1]
    )
    load_rows.start()
    own_codes = code_slots.at[my_z, my_middle, my_last]
    own_codes[...] = code_tile_ref[...]
    width = vectors_ref.shape[2]
    table_out[...] = jnp.zeros_like(table_out)
    table_out[:VECTORS, :] = vectors_ref[0].astype(jnp.float32)
    for j in range(up_bias_ref.shape[1] // width):
        table_out[VECTORS + j : VECTORS + j + 1, :] = up_bias_ref[:, j * width : (j + 1) * width].astype(jnp.float32)
    tables_ref[section] = table_out[...]
    codes = code_tile_ref[...]

    def shards_below(size):
        found = jnp.zeros_like(codes)
        for limit in range(size * real_shard, 4 * depth * real_shard, size * real_shard):
            found = found + (codes >= limit).astype(jnp.int32)
        return found

    holder, holder_z, holder_pair = shards_below(1), shards_below(4), shards_below(2)
    holder_y, holder_x = holder_pair - 2 * holder_z, holder - 2 * holder_pair
    holder_middle = holder_y * (1 - section) + holder_x * section
    holder_last = holder_x * (1 - section) + holder_y * section
    spot = (2 * holder_middle + holder_last) * GROUP + holder_z * shard_rows + codes - holder * real_shard
    turned = jnp.transpose(spot.astype(jnp.float32))
    for j in range(code_tile_ref.shape[0]):
        codes_ref[j * LANES : (j + 1) * LANES, :] = turned[:, j : j + 1].astype(jnp.int32)
    total[...] = jnp.zeros_like(total)

    def remote(source, land, send, got, **device):
        return pltpu.make_async_remote_copy(
            src_ref=source, dst_ref=land, send_sem=send, recv_sem=got, device_id=device, device_id_type=MESH
        )

    near = [sorted(range(depth), key=lambda z, here=here: (abs(z - here), z)) for here in range(depth)]

    def source_z(rank):
        found = my_z
        for here in range(depth):
            for other_rank in range(1, depth):
                here_now = jnp.logical_and(my_z == here, rank == other_rank)
                found = jnp.where(here_now, near[here][other_rank], found)
        return found

    def zero(source, target):
        part = book.at[my_middle, my_last, source]
        device = target * 4 + my_y * 2 + my_x
        return remote(part, part, zero_send.at[source, target], zero_got.at[source], dp=device)

    def zero_next(source):
        following = jnp.where(source < my_z, my_z + 1, my_z - 1)
        there = jnp.logical_and(following >= 0, following < depth)
        return jnp.clip(following, 0, depth - 1), there

    def zero_own(act):
        for step in (-1, 1):
            target = my_z + step
            there = jnp.logical_and(target >= 0, target < depth)

            @pl.when(there)
            def _():
                act(zero(my_z, jnp.clip(target, 0, depth - 1)))

    def middle(rank):
        source = source_z(rank)
        part = book.at[my_middle, my_last, source]
        return remote(part, part, middle_send.at[source], middle_got.at[source], dp=middle_device)

    def last(side, rank):
        source = source_z(rank)
        which = my_middle if side == 0 else 1 - my_middle
        part = book.at[which, my_last, source]
        return remote(part, part, last_send.at[side, source], last_got.at[side, source], dp=last_device)

    def codes_zero(hop):
        target = (my_z + hop) % depth * 4 + my_y * 2 + my_x
        return remote(own_codes, own_codes, code_send.at[hop - 1], code_got.at[hop - 1], dp=target)

    def codes_middle():
        part = code_slots.at[:, my_middle, my_last]
        return remote(part, part, code_send.at[depth], code_got.at[depth], dp=middle_device)

    def codes_last():
        part = code_slots.at[:, :, my_last]
        return remote(part, part, code_send.at[depth + 1], code_got.at[depth + 1], dp=last_device)

    def own_matrix(index):
        return pltpu.make_async_copy(own[index], held[index].at[section], weight_sems.at[index])

    def weight_across(index):
        copies, size = [], held[index].shape[1] // PIECES
        for piece in range(PIECES):
            part = held[index].at[section, pl.ds(piece * size, size)]
            send, got = weight_send.at[index, piece], weight_got.at[index, piece]
            copies.append(remote(part, part, send, got, section=1 - section))
        return copies

    def weight_arrived(index):
        for copy in weight_across(index):
            copy.wait_recv()

    def keep(index):
        return pltpu.make_async_copy(held[index].at[1 - section], other[index], keep_sems.at[index])

    def send_matrix(index):
        own_matrix(index).wait()
        start_copies(weight_across(index))

    table_across = remote(table_out, table_in, side_send.at[0], side_got.at[0], section=1 - section)
    half_across = remote(half_out, half_in, side_send.at[1], side_got.at[1], section=1 - section)

    def pick_rows(which_middle, which_last, block):
        group = 2 * which_middle + which_last
        part = pl.ds(pl.multiple_of(block * rows, rows), rows)
        inside = codes_ref[part, :] - group * GROUP
        lanes = lax.broadcasted_iota(jnp.int32, (1, depth * shard_rows), 1)
        hot = jnp.where(inside == lanes, 1.0, 0.0).astype(jnp.bfloat16)
        shards = book[which_middle, which_last].reshape(depth * shard_rows, half_width)
        total[part, :] = total[part, :] + times(hot, shards)

    def pick(which_middle, which_last):
        @pl.loop(0, total.shape[0] // rows)
        def _(block):
            pick_rows(which_middle, which_last, block)

    for index in range(3):
        own_matrix(index).start()
    pl.semaphore_wait(barrier, 3 + depth - 1)
    table_across.start()
    load_book.wait()
    load_end.wait()
    zero_own(lambda copy: copy.start())
    middle(0).start()
    last(0, 0).start()
    send_matrix(0)
    for hop in range(1, depth):
        codes_zero(hop).start()

    load_rows.wait()
    table_across.wait_recv()
    tables_ref[1 - section] = table_in[...]

    def weight(index):
        @pl.when(section == 1)
        def _():
            weight_arrived(index)
            keep(index).start()

        return held[index].at[0]

    def keep_late(index):
        @pl.when(section == 0)
        def _():
            weight_arrived(index)
            keep(index).start()

    saves = {
        name: pltpu.make_async_copy(source, target, save_sems.at[index])
        for index, (name, source, target) in enumerate(zip(SAVED[1:8], turned_sources(buffers, work)[1:], made))
    }

    def from_zero(rank):
        source = source_z(rank)
        following, there = zero_next(source)
        zero(source, following).wait_recv()

        @pl.when(there)
        def _():
            zero(source, following).start()

        middle(rank).start()
        last(0, rank).start()

    def from_middle(rank):
        middle(rank).wait_recv()
        last(1, rank).start()

    def arrived_last(side):
        for rank in range(depth):
            last(side, rank).wait_recv()

    def during(where, i):
        if where == "normed":
            from_zero(1)
            send_matrix(1)
            send_matrix(2)
        elif where == "qkv":
            from_middle(0)
            from_zero(2)
        elif where == "heads":

            @pl.when(i == 0)
            def _():
                from_middle(1)

            @pl.when(i == 1)
            def _():
                from_zero(3)

            @pl.when(i == 2)
            def _():
                from_middle(2)

            @pl.when(i == 3)
            def _():
                from_middle(3)

            @pl.when(i == 4)
            def _():
                pick(my_middle, my_last)

        elif where == "second":
            for hop in range(1, depth):
                codes_zero(hop).wait_recv()
            codes_middle().start()
            pick(1 - my_middle, my_last)

    forward_steps(
        tables_ref.at[0], lengths_ref, rows_ref, stat_ref, buffers, work, weight,
        lambda name: saves[name].start(), during,
    )
    table = tables_ref.at[0]
    keep_late(0)
    up_product(table, buffers[5], weight(2), buffers[6], buffers[7])
    saves["slope"].start()
    saves["act"].start()
    arrived_last(0)
    pick(my_middle, 1 - my_last)
    codes_middle().wait_recv()
    codes_last().start()
    keep_late(1)
    keep_late(2)
    arrived_last(1)
    own_rows = pl.ds(pl.multiple_of(section * rows, rows), rows)
    other_rows = pl.ds(pl.multiple_of((1 - section) * rows, rows), rows)
    pick_rows(1 - my_middle, 1 - my_last, 1 - section)
    half_out[...] = total[other_rows, :].astype(half_out.dtype)
    half_across.start()
    pick_rows(1 - my_middle, 1 - my_last, section)
    chosen_ref[:, pl.ds(pl.multiple_of(section * half_width, LANES), half_width)] = total[own_rows, :].astype(
        chosen_ref.dtype
    )
    half_across.wait_recv()
    chosen_ref[:, pl.ds(pl.multiple_of((1 - section) * half_width, LANES), half_width)] = half_in[...]
    codes_last().wait_recv()
    all_codes_ref[...] = code_slots[...]
    for index in range(3):
        for copy in weight_across(index):
            copy.wait_send()
        keep(index).wait()
    table_across.wait_send()
    half_across.wait_send()
    zero_own(lambda copy: copy.wait_send())
    for hop in range(1, depth):
        source = source_z(hop)
        following, there = zero_next(source)

        @pl.when(there)
        def _():
            zero(source, following).wait_send()

        codes_zero(hop).wait_send()
    for hop in range(depth):
        middle(hop).wait_send()
        for side in range(2):
            last(side, hop).wait_send()
    codes_middle().wait_send()
    codes_last().wait_send()
    for save in saves.values():
        save.wait()


def opening(lengths, codes, vectors, up_bias, patches, codebook, own, devices, row_count):
    tokens, width = patches.shape
    half_width = width // 2
    depth, shard_rows = devices // 4, codebook.shape[0]
    whole = (shard_rows - 1) // 16 * 16
    book_end = jnp.pad(codebook[whole:], ((0, -shard_rows % 16), (0, 0)))
    padded_rows = whole + book_end.shape[0]
    table_shape = (16, width)
    code_tile = codes.reshape(-1, LANES)
    kept = saved_shapes(row_count, width, own[2].shape[1])[:8]
    bfloat16, float32 = jnp.bfloat16, jnp.float32
    shapes = (
        [(w.shape, w.dtype) for w in own[:3]]
        + [
            ((2, *table_shape), float32),
            ((depth, 2, 2, *code_tile.shape), codes.dtype),
            ((row_count, width), bfloat16),
        ]
        + turned_shapes(kept)[1:]
        + [((16, row_count), float32)]
    )
    dma = pltpu.SemaphoreType.DMA
    results = pl.pallas_call(
        functools.partial(opening_kernel, shard_rows),
        out_shape=tuple(jax.ShapeDtypeStruct(s, t) for s, t in shapes),
        in_specs=[in_smem()] + [in_vmem()] * 3 + [in_place()] * 6,
        out_specs=[in_place()] * 3 + [in_vmem()] * 3 + [in_place()] * 7 + [in_vmem()],
        scratch_shapes=[pltpu.VMEM((2, *w.shape), w.dtype) for w in own[:3]] + forward_scratch((), kept, row_count)
        + [
            pltpu.VMEM((row_count, width), bfloat16),
            pltpu.VMEM((2, 2, depth, padded_rows, half_width), bfloat16),
            pltpu.VMEM((tokens, half_width), float32),
            pltpu.VMEM((row_count, half_width), bfloat16),
            pltpu.VMEM((row_count, half_width), bfloat16),
            pltpu.VMEM(table_shape, float32),
            pltpu.VMEM((depth, 2, 2, *code_tile.shape), codes.dtype),
            pltpu.VMEM(table_shape, float32),
            pltpu.VMEM((tokens, 1), jnp.int32),
            dma((3,)),
            dma((3, PIECES)),
            dma((3, PIECES)),
            dma((depth, depth)),
            dma((depth,)),
            dma((depth,)),
            dma((depth,)),
            dma((2, depth)),
            dma((2, depth)),
            dma((depth + 2,)),
            dma((depth + 2,)),
            dma((2,)),
            dma((2,)),
            dma((4,)),
        ],
        compiler_params=pltpu.CompilerParams(
            collective_id=1, has_side_effects=True, vmem_limit_bytes=60 * 1024 * 1024
        ),
        name="opening",
    )(lengths, code_tile, vectors, up_bias, patches, codebook, book_end, *own[:3])
    return results[:3], results[3], results[4].reshape(devices, -1, LANES), results[5], results[6:]


def plain_opening(lengths, codes, table, patches, codebook, own, swapped, ordered, row_count):
    section = lax.axis_index("section")
    other = tuple(swapped(weight) for weight in own)
    tables = jnp.stack(ordered(table, swapped(table)))
    all_codes = lax.all_gather(codes, "dp", axis=0, tiled=True)
    half_width = patches.shape[1] // 2
    half_book = lax.dynamic_slice_in_dim(codebook, section * half_width, half_width, 1)
    half_book = lax.all_gather(half_book, "dp", axis=0, tiled=True)
    half_rows = jnp.take(half_book, codes, axis=0)

    def micro_rows(array, index):
        return lax.dynamic_slice_in_dim(array, index * row_count, row_count, 0)

    half_own = micro_rows(half_rows, section)
    half_other = swapped(micro_rows(half_rows, 1 - section))
    chosen = jnp.concatenate(ordered(half_own, half_other), axis=1)
    encoded = block_forward(0, lengths, micro_rows(patches, section), tables, own, other)
    return other, tables, all_codes, chosen, encoded


def backward_steps(from_code, lengths_ref, table, buffers, sums_ref, weight, arrived, save, during):
    (
        rows_ref, hidden_ref, qkv_ref, mixed_ref, slope_ref, stat_ref, branch_ref, attn_ref, projected_ref,
        grad_ref, second_ref, moved_ref, query_marks, key_marks,
    ) = buffers
    rows, width = rows_ref.shape
    hidden_units = slope_ref.shape[1]
    head_size = width // HEADS
    per_block = LANES // head_size
    half = rows // 2
    per_row = width // TILE
    sums_ref[...] = jnp.zeros_like(sums_ref)

    fill_marks(lengths_ref, head_size, query_marks, key_marks)
    arrived(("grads",))
    total = jnp.zeros((1, width), jnp.float32)
    for start in range(0, rows, LANES):
        part = pl.ds(start, LANES)
        grad = moved_ref[part, :].astype(jnp.float32)
        if from_code:
            grad = grad_ref[part, :] + 0.5 * (second_ref[part, :] - grad)
        grad_ref[part, :] = grad
        branch = grad.astype(jnp.bfloat16)
        branch_ref[part, :] = branch
        total = total + column_sum(branch)
    sums_ref[7:8, :] = total
    save("branch")
    during("branch")

    down_held = weight(3)
    arrived(("slope", "hidden"))

    def through_gelu(first, count):
        at_once = 3 if count % 3 == 0 else 1

        @pl.loop(0, count // at_once)
        def _(group):
            def tile_of(j):
                return first + group * at_once + j

            def block_of(j):
                return pl.ds(pl.multiple_of(tile_of(j) * TILE, TILE), TILE)

            def act_of(j):
                return times_transposed(branch_ref[...], down_held[block_of(j), :])

            ahead = act_of(0)
            for j in range(at_once):
                grad_act, block = ahead, block_of(j)
                if j + 1 < at_once:
                    ahead = act_of(j + 1)
                grad_pre = (grad_act * slope_ref[:, block].astype(jnp.float32)).astype(jnp.bfloat16)
                slope_ref[:, block] = grad_pre
                column = pl.multiple_of(tile_of(j) % per_row * TILE, TILE)
                sums_ref[pl.ds(VECTORS + tile_of(j) // per_row, 1), pl.ds(column, TILE)] = column_sum(grad_pre)

    tiles = hidden_units // TILE
    through_gelu(0, tiles // 4)
    during("gelu")
    through_gelu(tiles // 4, tiles - tiles // 4)
    save("pre")
    during("pre")
    up_held = weight(2)
    for start in range(0, width, TILE):
        block = pl.ds(start, TILE)
        second_ref[:, block] = times_transposed(slope_ref[...], up_held[block, :])
    during("second")

    gain_total, shift_total, attn_total = (jnp.zeros((1, width), jnp.float32) for _ in range(3))
    for start in range(0, rows, LANES):
        part = pl.ds(start, LANES)
        hat, scale = normalized(hidden_ref[part, :])
        grad = second_ref[part, :]
        gain_total = gain_total + column_sum(grad * hat)
        shift_total = shift_total + column_sum(grad)
        grad_hidden = grad_ref[part, :] + norm_backward(grad, hat, scale, 1.0 + table[5:6, :])
        grad_ref[part, :] = grad_hidden
        attn = grad_hidden.astype(jnp.bfloat16)
        attn_ref[part, :] = attn
        attn_total = attn_total + column_sum(attn)
    sums_ref[5:6, :] = gain_total
    sums_ref[6:7, :] = shift_total
    sums_ref[4:5, :] = attn_total
    save("attn")

    out_held = weight(1)
    for start in range(0, width, TILE):
        block = pl.ds(start, TILE)
        moved_ref[:, block] = times_transposed(attn_ref[...], out_held[block, :]).astype(jnp.bfloat16)
    during("attn")
    arrived(("mixed", "qkv", "stat"))

    def through_heads(first, count):
        @pl.loop(first, first + count)
        def _(i):
            query = qkv_ref[:, lane_block(i)]
            grad_mixed = moved_ref[:, lane_block(i)]
            products = jnp.transpose(
                grad_mixed.astype(jnp.float32) * mixed_ref[:, lane_block(i)].astype(jnp.float32)
            )
            mine = [head_lanes(h, head_size, 1.0) for h in range(per_block)]
            scaled = [head_lanes(h, head_size, head_size**-0.5) for h in range(per_block)]
            query_of = [query * scaled[h] for h in range(per_block)]
            marked_of = [query_of[h] + query_marks[h] for h in range(per_block)]
            grad_of = [grad_mixed * mine[h] for h in range(per_block)]
            row_dot = [
                jnp.sum(products[h * head_size : (h + 1) * head_size, :], axis=0, keepdims=True)
                for h in range(per_block)
            ]
            units = [(start, h) for start in range(0, rows, half) for h in range(per_block)]

            def products_of(unit):
                start, h = unit
                part = pl.ds(start, half)
                keys = qkv_ref[part, lane_block(width // LANES + i)]
                values = qkv_ref[part, lane_block(2 * width // LANES + i)]
                return (
                    times_transposed(keys * mine[h] + key_marks[h, part, :], marked_of[h]),
                    times_transposed(values, grad_of[h]),
                )

            ahead = products_of(units[0])
            grad_query = jnp.zeros((rows, LANES), jnp.float32)
            value_total = jnp.zeros((1, LANES), jnp.float32)
            for number, (start, h) in enumerate(units):
                part = pl.ds(start, half)
                scores, grad_probs = ahead
                if number + 1 < len(units):
                    ahead = products_of(units[number + 1])
                keys = qkv_ref[part, lane_block(width // LANES + i)]
                exact = jnp.exp(scores - stat_ref[pl.ds(per_block * i + h, 1), :])
                grad_scores = (exact * (grad_probs - row_dot[h])).astype(jnp.bfloat16)
                value_term = times(exact.astype(jnp.bfloat16), grad_of[h])
                key_term = times(grad_scores, query_of[h])
                grad_query = grad_query + transposed_times(grad_scores, keys * scaled[h])
                grad_value = value_term if h == 0 else grad_value + value_term
                grad_key = key_term if h == 0 else grad_key + key_term
                if h == per_block - 1:
                    grad_value = grad_value.astype(jnp.bfloat16)
                    projected_ref[part, lane_block(2 * width // LANES + i)] = grad_value
                    projected_ref[part, lane_block(width // LANES + i)] = grad_key.astype(jnp.bfloat16)
                    value_total = value_total + column_sum(grad_value)
            grad_query = grad_query.astype(jnp.bfloat16)
            projected_ref[:, lane_block(i)] = grad_query
            sums_ref[2:3, lane_block(i)] = column_sum(grad_query)
            sums_ref[3:4, lane_block(i)] = value_total

    groups = width // LANES
    for part in range(3):
        first, end = groups * part // 3, groups * (part + 1) // 3
        if end > first:
            through_heads(first, end - first)
        during(("heads", part))

    save("projected")
    qkv_held = weight(0)
    for start in range(0, width, TILE):
        grad_rows = None
        for j in range(3):
            term = times_transposed(
                projected_ref[:, j * width : (j + 1) * width], qkv_held[pl.ds(j * width + start, TILE), :]
            )
            grad_rows = term if grad_rows is None else grad_rows + term
        second_ref[:, pl.ds(start, TILE)] = grad_rows
    during("rows")

    arrived(("rows",))
    gain_total, shift_total = (jnp.zeros((1, width), jnp.float32) for _ in range(2))
    for start in range(0, rows, LANES):
        part = pl.ds(start, LANES)
        hat, scale = normalized(rows_ref[part, :].astype(jnp.float32))
        grad = second_ref[part, :]
        gain_total = gain_total + column_sum(grad * hat)
        shift_total = shift_total + column_sum(grad)
        grad_rows = grad_ref[part, :] + norm_backward(grad, hat, scale, 1.0 + table[0:1, :])
        grad_ref[part, :] = grad_rows if from_code else grad_rows.astype(jnp.bfloat16).astype(jnp.float32)
    sums_ref[0:1, :] = gain_total
    sums_ref[1:2, :] = shift_total
    save("grad")


class BackwardWeights(Weights):
    def place(self, index):
        return self.held[index - 1], self.sems.at[index - 1]

    def start(self, index):
        if index != 0:
            super().start(index)
            return
        width = self.own[0].shape[0]

        def begin(matrix):
            for j in range(3):
                block = pl.ds(j * width, width)
                pltpu.make_async_copy(
                    matrix[0].at[:, block], self.held[2].at[block, :], self.sems.at[3 + j]
                ).start()

        @pl.when(self.own_flag == 1)
        def _():
            begin(self.own)

        @pl.when(self.own_flag != 1)
        def _():
            begin(self.other)

    def wait(self, index):
        if index == 0:
            width = self.own[0].shape[0]
            for j in range(3):
                block = pl.ds(j * width, width)
                pltpu.make_async_copy(
                    self.own[0].at[:, block], self.held[2].at[block, :], self.sems.at[3 + j]
                ).wait()
            return self.held[2]
        return super().wait(index)


def backward_scratch(own, row_count):
    width, hidden_units = own[2].shape
    bfloat16, float32 = jnp.bfloat16, jnp.float32
    return [pltpu.VMEM(w.shape, w.dtype) for w in own[1:]] + [
        pltpu.VMEM((row_count, width), bfloat16),
        pltpu.VMEM((row_count, width), float32),
        pltpu.VMEM((row_count, 3 * width), bfloat16),
        pltpu.VMEM((row_count, width), bfloat16),
        pltpu.VMEM((row_count, hidden_units), bfloat16),
        pltpu.VMEM((16, row_count), float32),
        pltpu.VMEM((row_count, width), bfloat16),
        pltpu.VMEM((row_count, width), bfloat16),
        pltpu.VMEM((row_count, 3 * width), bfloat16),
        pltpu.VMEM((row_count, width), float32),
        pltpu.VMEM((row_count, width), float32),
        pltpu.VMEM((row_count, width), bfloat16),
        pltpu.VMEM((2, row_count, LANES), bfloat16),
        pltpu.VMEM((2, row_count, LANES), bfloat16),
        pltpu.SemaphoreType.DMA((6,)),
        pltpu.SemaphoreType.DMA((9,)),
    ]


def backward_loads(kept, grads_in, buffers, sems, whole_rows, whole_grad):
    rows_hbm, hidden_hbm, qkv_hbm, mixed_hbm, slope_hbm, stat_hbm = kept
    rows_ref, hidden_ref, qkv_ref, mixed_ref, slope_ref, stat_ref = buffers[:6]
    row_count = rows_ref.shape[0]
    mine = pl.ds(pl.multiple_of(lax.axis_index("section") * row_count, row_count), row_count)
    if whole_rows:
        rows_hbm = rows_hbm.at[mine, :]
    if len(grads_in) == 1 and not whole_grad:
        grad_pairs = [(grads_in[0], buffers[11])]
    elif whole_grad:
        grad_pairs = [(grads_in[0].at[mine, :], buffers[11])]
    else:
        grad_pairs = list(zip(grads_in, buffers[9:12]))
    pairs = {
        "slope": [(slope_hbm, slope_ref)], "hidden": [(hidden_hbm, hidden_ref)], "mixed": [(mixed_hbm, mixed_ref)],
        "qkv": [(qkv_hbm, qkv_ref)], "stat": [(stat_hbm, stat_ref)], "rows": [(rows_hbm, rows_ref)],
    }
    copies, index = {}, 0
    for name, entries in [("grads", grad_pairs), *pairs.items()]:
        copies[name] = []
        for source, target in entries:
            copies[name].append(pltpu.make_async_copy(source, target, sems.at[index]))
            index = index + 1
    return copies


def start_copies(copies):
    for copy in copies:
        copy.start()


def wait_copies(copies):
    for copy in copies:
        copy.wait()


def backward_kernel(block, lengths_ref, tables_ref, *refs):
    from_code = block == 0
    grads_in, kept, own, other, made, (sums_ref,), held, buffers, (weight_sems, load_sems, save_sems) = split_refs(
        refs, (3 if from_code else 1, 6, 4, 4, 5, 1, 3, 14, 3)
    )
    weights = BackwardWeights(
        (lax.axis_index("section") == block).astype(jnp.int32), own, other,
        held, weight_sems,
    )
    loads = backward_loads(kept, grads_in, buffers, load_sems, from_code, not from_code)
    saves = {
        name: pltpu.make_async_copy(source, target, save_sems.at[index])
        for index, (name, source, target) in enumerate(zip(
            ("grad", "branch", "pre", "attn", "projected"),
            (buffers[9], buffers[6], buffers[4], buffers[7], buffers[8]),
            made,
        ))
    }
    start_copies(loads["grads"])
    weights.start(3)
    start_copies(loads["slope"])
    weights.start(2)
    start_copies(loads["hidden"])
    weights.start(1)
    for name in ("mixed", "qkv", "stat", "rows"):
        start_copies(loads[name])

    def arrived(names):
        for name in names:
            wait_copies(loads[name])

    def during(where):
        if where == "pre":
            weights.start(0)

    backward_steps(
        from_code, lengths_ref, tables_ref.at[block], buffers, sums_ref, weights.wait, arrived,
        lambda name: saves[name].start(), during,
    )
    for save in saves.values():
        save.wait()


def block_backward(block, lengths, tables, grads_in, kept, own, other):
    row_count, width = kept[1].shape
    hidden_units = own[2].shape[1]
    bfloat16, float32 = jnp.bfloat16, jnp.float32
    made = [
        ((row_count, width), float32),
        ((row_count, width), bfloat16),
        ((row_count, hidden_units), bfloat16),
        ((row_count, width), bfloat16),
        ((row_count, 3 * width), bfloat16),
        (tables.shape[1:], float32),
    ]
    return pl.pallas_call(
        functools.partial(backward_kernel, block),
        out_shape=tuple(jax.ShapeDtypeStruct(s, t) for s, t in made),
        in_specs=[in_smem(), in_vmem()] + [in_place()] * (14 + len(grads_in)),
        out_specs=[in_place()] * 5 + [in_vmem()],
        scratch_shapes=backward_scratch(own, row_count) + [pltpu.SemaphoreType.DMA((5,))],
        compiler_params=pltpu.CompilerParams(vmem_limit_bytes=56 * 1024 * 1024),
        cost_estimate=pl.CostEstimate(
            flops=2 * row_count * (12 * width * width + 5 * row_count * width),
            bytes_accessed=40 * 1024 * 1024,
            transcendentals=row_count * row_count * HEADS,
        ),
        name="block_backward",
    )(lengths, tables, *grads_in, *kept, *own, *other)


SLOTS, HELD, RING = 4, 6, 16


def chunk_list(width, hidden_units):
    ups = hidden_units // width

    def of(block, operand, count):
        return [(block, operand, j) for j in range(count)]

    return (
        of(1, 3, ups) + of(1, 2, ups) + of(1, 1, 1) + of(1, 0, 3)
        + of(0, 3, ups) + of(0, 2, ups) + of(0, 1, 1) + of(0, 0, 3)
    )


def count_codes_in(codes_ref, code_count, counts_ref, stats_ref):
    high_count = counts_ref.shape[0]
    high_rows = -(-high_count // 16) * 16

    @pl.loop(0, codes_ref.shape[0], init_carry=jnp.zeros((high_rows, LANES), jnp.float32))
    def counts(block, total):
        codes = codes_ref[block]

        def hot(values, size):
            rows = lax.broadcasted_iota(jnp.int32, (size, 1), 0)
            pieces = [jnp.where(values[j : j + 1, :] == rows, 1.0, 0.0) for j in range(codes.shape[0])]
            return jnp.concatenate(pieces, axis=1).astype(jnp.bfloat16)

        return total + times_transposed(hot(codes >> 7, high_rows), hot(codes & (LANES - 1), LANES))

    counts = counts[:high_count, :]
    counts_ref[...] = counts.astype(jnp.int32)
    share = counts / float(codes_ref.shape[0] * codes_ref.shape[1] * LANES)
    used = counts > 0.0
    terms = jnp.where(used, share * jnp.log(jnp.where(used, share, 1.0)), 0.0)
    usage = jnp.sum(jnp.where(used, 1.0, 0.0), axis=(0, 1), keepdims=True) / code_count
    perplexity = jnp.exp(-jnp.sum(terms, axis=(0, 1), keepdims=True)) / code_count
    stats_ref[...] = jnp.concatenate([usage, perplexity], axis=1)


def closing_kernel(chunks, code_count, lengths_ref, tables_ref, codes_ref, *refs):
    (
        dec_grads_in, enc_grads_in, dec_kept, enc_kept, own, other, dec_left, enc_left,
        results, (vector_sums_ref, bias_sums_ref, counts_ref, stats_ref, shown_out, grads_out), held_weights, buffers,
        (weight_sems, load_sems, enc_weight_sems, enc_load_sems),
        (stage, zero, held, one, two, three, finals, fourth), (narrow, wide), (dec_grad_ref, dec_sums, enc_sums),
        (sums_send, sums_zero, sums_held, sums_first, sums_second, sums_third),
        (operand_sems, zero_send, zero_got, first_send, first_got, second_send, second_got, third_send, third_got,
         fourth_send, fourth_got, swap_sems, credit),
    ) = split_refs(refs, (1, 1, 6, 6, 4, 4, 3, 3, 4, 6, 3, 14, 4, 8, 2, 3, 6, 13))
    count = len(chunks)
    depth, share, width = stage.shape[1], stage.shape[4], stage.shape[5]
    half = width // 2
    rows = buffers[0].shape[0]
    ups = sum(1 for block, operand, _ in chunks if block == 0 and operand == 3)
    section, place = lax.axis_index("section"), lax.axis_index("dp")
    my_x, my_y, my_z = place % 2, place // 2 % 2, place // 4
    beside_x, beside_y = place + 1 - 2 * my_x, place + 2 - 4 * my_y
    first_device = beside_x * (1 - section) + beside_y * section
    second_device = beside_y * (1 - section) + beside_x * section
    own_half = pl.ds(pl.multiple_of(section * half, LANES), half)
    other_half = pl.ds(pl.multiple_of((1 - section) * half, LANES), half)

    barrier = pltpu.get_barrier_semaphore()
    pl.semaphore_signal(barrier, inc=1, device_id={"section": 1 - section}, device_id_type=MESH)
    for device in (beside_x, beside_y):
        pl.semaphore_signal(barrier, inc=1, device_id={"dp": device}, device_id_type=MESH)
    for hop in range(1, depth):
        device = (my_z + hop) % depth * 4 + my_y * 2 + my_x
        pl.semaphore_signal(barrier, inc=1, device_id={"dp": device}, device_id_type=MESH)

    operands = {
        0: (narrow.at[1], buffers[8]), 1: (buffers[3], buffers[7]), 2: (narrow.at[0], buffers[4]), 3: (wide, buffers[6]),
    }
    moves = {}
    for block, left in ((0, enc_left), (1, dec_left)):
        for operand, source in ((0, left[0]), (2, left[1]), (3, left[2])):
            moves[block, operand] = pltpu.make_async_copy(
                source, operands[operand][0], operand_sems.at[block, operand]
            )

    def matrices(block, sems):
        return BackwardWeights((section == block).astype(jnp.int32), own, other, held_weights, sems)

    dec_weights, enc_weights = matrices(1, weight_sems), matrices(0, enc_weight_sems)
    dec_loads = backward_loads(dec_kept, dec_grads_in, buffers, load_sems, False, True)
    enc_loads = backward_loads(enc_kept, enc_grads_in, buffers, enc_load_sems, True, False)
    start_copies(dec_loads["grads"])
    moves[1, 3].start()
    dec_weights.start(3)
    start_copies(dec_loads["slope"])
    dec_weights.start(2)
    moves[1, 2].start()
    start_copies(dec_loads["hidden"])
    dec_weights.start(1)
    for name in ("mixed", "qkv", "stat", "rows"):
        start_copies(dec_loads[name])
    moves[1, 0].start()
    pl.semaphore_wait(barrier, 3 + depth - 1)

    def remote(source, land, send, got, **device):
        return pltpu.make_async_remote_copy(
            src_ref=source, dst_ref=land, send_sem=send, recv_sem=got, device_id=device, device_id_type=MESH
        )

    def across(k):
        if k == count:
            return remote(sums_send, sums_zero, zero_send.at[k], zero_got.at[k], section=1 - section)
        return remote(
            stage.at[k % SLOTS, :, :, :, :, other_half], zero.at[k % SLOTS], zero_send.at[k], zero_got.at[k],
            section=1 - section,
        )

    def first(k):
        if k == count:
            return remote(sums_held, sums_first, first_send.at[k], first_got.at[k], dp=first_device)
        return remote(
            held.at[k % HELD, 1], one.at[k % RING], first_send.at[k], first_got.at[k], dp=first_device
        )

    def second(k):
        if k == count:
            return remote(sums_first, sums_second, second_send.at[k], second_got.at[k], dp=second_device)
        return remote(
            one.at[k % RING, 1], two.at[k % RING], second_send.at[k], second_got.at[k], dp=second_device
        )

    def third(k, hop):
        target = (my_z + hop) % depth
        device = target * 4 + my_y * 2 + my_x
        send, got = third_send.at[k, hop - 1], third_got.at[k, hop - 1]
        if k == count:
            return remote(sums_second, sums_third.at[hop - 1], send, got, dp=device)
        return remote(two.at[k % RING, target], three.at[k % RING, hop - 1], send, got, dp=device)

    def last(k):
        index = k % (count // 2)
        return remote(finals.at[index], fourth.at[index], fourth_send.at[k], fourth_got.at[k], section=1 - section)

    def send_across(k):
        if k >= SLOTS:
            pl.semaphore_wait(credit, 1)
        across(k).start()

    def give(k):
        if k == count:
            dec, enc = dec_sums[...], enc_sums[...]
            sums_held[...] = jnp.where(section == 0, enc, dec)
            sums_send[...] = jnp.where(section == 0, dec, enc)
            across(k).start()
            return
        block, operand, j = chunks[k]
        key = (block, operand)
        if operand == 3 and j != 0:
            send_across(k)
            return
        if j == 0 and key in moves and key != (0, 3):
            moves[key].wait()
        made = range(k, k + ups) if operand == 3 else range(k, k + 1)
        for each in made:
            if each >= SLOTS:
                across(each - SLOTS).wait_send()
        left, right = operands[operand]
        if operand == 3:

            @pl.loop(0, depth)
            def _(tile):
                columns = pl.ds(pl.multiple_of(tile * 4 * ups * share, LANES), 4 * ups * share)
                product = transposed_times(left[:, columns], right[...]).astype(stage.dtype)
                product = product.reshape(2, 2, ups, share, width)
                for j in range(ups):
                    stage[(k + j) % SLOTS, tile] = product[:, :, j]

        else:
            columns = right[:, j * width : (j + 1) * width]
            product = transposed_times(left[...], columns) if operand == 1 else times(left[...], columns)
            product = product.astype(stage.dtype)
            stage[k % SLOTS] = product.reshape(depth, 2, 2, share, width)
        send_across(k)
        last_of_key = operand == 3 or k + 1 == count or chunks[k + 1][:2] != key
        if last_of_key and block == 1 and operand in (0, 2):
            moves[0, operand].start()

    def begin(k):
        across(k).wait_recv()
        if k == count:
            sums_held[...] = sums_held[...] + sums_zero[...]
            first(k).start()
            return
        if k >= HELD:
            first(k - HELD).wait_send()
        slot = k % SLOTS
        for a in range(2):
            for b in range(2):
                chip_x = (my_x + (a * (1 - section) + b * section)) % 2
                chip_y = (my_y + (b * (1 - section) + a * section)) % 2
                held[k % HELD, a, b] = stage[slot, :, chip_y, chip_x, :, own_half] + zero[slot, :, chip_y, chip_x]
        first(k).start()
        if k + SLOTS < count:
            pl.semaphore_signal(credit, inc=1, device_id={"section": 1 - section}, device_id_type=MESH)

    def after_first(k):
        first(k).wait_recv()
        if k == count:
            first(k).wait_send()
            sums_first[...] = sums_first[...] + sums_held[...]
        else:
            slot = k % RING
            one[slot] = one[slot] + held[k % HELD, 0]
        second(k).start()

    def after_second(k):
        second(k).wait()
        if k == count:
            sums_second[...] = sums_second[...] + sums_first[...]
        else:
            slot = k % RING
            two[slot] = two[slot] + one[slot, 0]
        for hop in range(1, depth):
            third(k, hop).start()

    def after_third(k):
        if k == count:
            total = sums_second[...]
            for hop in range(1, depth):
                third(k, hop).wait()
                total = total + sums_third[hop - 1]
            vector_sums_ref[...] = total[:VECTORS, :]
            bias_sums_ref[...] = jnp.zeros_like(bias_sums_ref)
            for j in range(ups):
                bias_sums_ref[0:1, j * width : (j + 1) * width] = total[VECTORS + j : VECTORS + j + 1, :]
            return
        block = chunks[k][0]
        slot = k % RING
        total = two[slot, my_z].astype(jnp.float32)
        for hop in range(1, depth):
            third(k, hop).wait()
            total = total + three[k % RING, hop - 1].astype(jnp.float32)

        @pl.when(section == block)
        def _():
            put(k, total, own_half, section * half)

        @pl.when(section != block)
        def _():
            finals[k % (count // 2)] = total
            last(k).start()

    def put(k, total, lanes, offset):
        _, operand, j = chunks[k]
        if operand == 3:
            results[3][j * share : (j + 1) * share, lanes] = total
        else:
            start = pl.multiple_of(j * width + offset, LANES)
            results[operand][:, pl.ds(start, half)] = total

    def after_fourth(k):
        if k == count:
            return
        block = chunks[k][0]

        @pl.when(section == block)
        def _():
            last(k).wait_recv()
            put(k, fourth[k % (count // 2)], other_half, (1 - section) * half)

        @pl.when(section != block)
        def _():
            last(k).wait_send()

    close = 11

    def times_of(k):
        start = min(k, count - 1) // 2
        second_time = max(start + 2, min(start + 3, close + 1))
        third_time = max(second_time + 1, min(start + 5, close))
        fourth_time = max(third_time + 1, min(start + 7, close + 1))
        return start, start + 1, second_time, third_time, fourth_time, fourth_time + 1

    phases = ((1, begin), (0, give), (2, after_first), (3, after_second), (4, after_third), (5, after_fourth))

    def step(number):
        for phase, action in phases:
            for k in range(count + 1):
                if times_of(k)[phase] == number:
                    action(k)

    mine = pl.ds(pl.multiple_of(section * rows, rows), rows)

    def deliver(block, source, target, sem, start):
        stay = pltpu.make_async_copy(source, target.at[mine, :], swap_sems.at[sem, 0])
        go = remote(source, target.at[mine, :], swap_sems.at[sem, 1], swap_sems.at[sem, 2], section=1 - section)

        @pl.when(section == block)
        def _():
            if start:
                stay.start()
            else:
                stay.wait()
                go.wait_recv()

        @pl.when(section != block)
        def _():
            if start:
                go.start()
            else:
                go.wait_send()

    branch_buffer, grad_buffer, second_buffer = buffers[6], buffers[9], buffers[10]
    shown_dec = (1, branch_buffer, shown_out, 0)
    grads_dec = (1, dec_grad_ref, grads_out, 1)
    shown_enc = (0, branch_buffer, shown_out, 2)
    grads_enc = (0, grad_buffer, grads_out, 3)

    def once(act):
        seen = set()

        def acted(name):
            if name not in seen:
                seen.add(name)
                act(name)

        return acted

    dec_arrive = once(lambda name: wait_copies(dec_loads[name]))
    enc_arrive = once(lambda name: wait_copies(enc_loads[name]))
    enc_matrix = once(lambda index: enc_weights.wait(index))

    def enc_weight(index):
        enc_matrix(index)
        return held_weights[2] if index == 0 else enc_weights.place(index)[0]

    def dec_arrived(names):
        for name in names:
            dec_arrive(name)

    def enc_arrived(names):
        for name in names:
            enc_arrive(name)
        if "grads" in names:
            enc_arrive("hidden")
            moves[0, 3].wait()
            last_product(tables_ref.at[0], buffers[1], wide, enc_weight(3), second_buffer, None)

    dec_steps = {"branch": 0, "gelu": 1, "pre": 2, "attn": 3, ("heads", 2): 4, "rows": 5}
    enc_steps = {"branch": 6, "gelu": 7, "pre": 8, ("heads", 0): 9, ("heads", 2): 10}

    def during_decoder(where):
        if where == "pre":
            last_product(tables_ref.at[1], buffers[1], wide, held_weights[2], None, branch_buffer)
            deliver(*shown_dec, True)
            dec_weights.start(0)
            moves[0, 3].start()
        if where in dec_steps:
            step(dec_steps[where])
        if where == "second":
            enc_weights.start(2)
        elif where == "attn":
            start_copies(enc_loads["slope"])
            start_copies(enc_loads["hidden"])
            enc_weights.start(1)
        elif where == ("heads", 2):
            for name in ("mixed", "qkv", "stat"):
                start_copies(enc_loads[name])
        elif where == "rows":
            enc_weights.start(3)

    def during_encoder(where):
        if where == "pre":
            branch_buffer[...] = second_buffer[...].astype(branch_buffer.dtype)
            deliver(*shown_enc, True)
            enc_weights.start(0)
        if where in enc_steps:
            step(enc_steps[where])

    def nothing(name):
        return None

    backward_steps(
        False, lengths_ref, tables_ref.at[1], buffers, dec_sums, dec_weights.wait, dec_arrived, nothing,
        during_decoder,
    )
    start_copies(enc_loads["grads"])
    start_copies(enc_loads["rows"])
    dec_grad_ref[...] = grad_buffer[...]
    deliver(*grads_dec, True)
    deliver(*shown_dec, False)
    backward_steps(
        True, lengths_ref, tables_ref.at[0], buffers, enc_sums, enc_weight, enc_arrived, nothing, during_encoder,
    )
    deliver(*grads_enc, True)
    for number in range(close, times_of(count)[5] + 1):
        step(number)
        if number == 13:
            count_codes_in(codes_ref, code_count, counts_ref, stats_ref)
    for parts in (grads_dec, shown_enc, grads_enc):
        deliver(*parts, False)
    for k in range(count + 1):
        if k + SLOTS >= count:
            across(k).wait_send()
        if k != count and k + HELD >= count:
            first(k).wait_send()


def closing(lengths, tables, codes, code_count, cotangent, enc_grads_in, dec_kept, enc_kept, own, other, dec_left, enc_left, devices):
    row_count, width = dec_kept[0].shape
    hidden_units = own[2].shape[1]
    chunks = chunk_list(width, hidden_units)
    count, depth, share, half = len(chunks), devices // 4, width // devices, width // 2
    bfloat16, float32 = jnp.bfloat16, jnp.float32
    tokens = cotangent.shape[0]
    table = pltpu.VMEM(tables.shape[1:], float32)
    dma = pltpu.SemaphoreType.DMA
    shapes = [
        ((share, 3 * width), float32),
        ((share, width), float32),
        ((share, hidden_units), float32),
        ((hidden_units // devices, width), float32),
        ((VECTORS, width), float32),
        ((8, hidden_units), float32),
        ((-(-code_count // LANES), LANES), jnp.int32),
        ((1, 2), float32),
        ((tokens, width), bfloat16),
        ((tokens, width), float32),
    ]
    return pl.pallas_call(
        functools.partial(closing_kernel, chunks, code_count),
        out_shape=tuple(jax.ShapeDtypeStruct(s, t) for s, t in shapes),
        in_specs=[in_smem()] + [in_vmem()] * 2 + [in_place()] * 28,
        out_specs=[in_vmem()] * 8 + [in_place()] * 2,
        scratch_shapes=backward_scratch(own, row_count)
        + [
            dma((6,)),
            dma((9,)),
            pltpu.VMEM((SLOTS, depth, 2, 2, share, width), bfloat16),
            pltpu.VMEM((SLOTS, depth, 2, 2, share, half), bfloat16),
            pltpu.VMEM((HELD, 2, 2, depth, share, half), bfloat16),
            pltpu.VMEM((RING, 2, depth, share, half), bfloat16),
            pltpu.VMEM((RING, depth, share, half), bfloat16),
            pltpu.VMEM((RING, depth - 1, share, half), bfloat16),
            pltpu.VMEM((count // 2, share, half), float32),
            pltpu.VMEM((count // 2, share, half), float32),
            pltpu.VMEM((2, width, row_count), bfloat16),
            pltpu.VMEM((row_count, hidden_units), bfloat16),
            pltpu.VMEM((row_count, width), float32),
            table,
            table,
            table,
            table,
            table,
            table,
            table,
            pltpu.VMEM((depth - 1, *tables.shape[1:]), float32),
            dma((2, 4)),
        ]
        + [dma((count + 1,))] * 6
        + [dma((count + 1, depth - 1))] * 2
        + [dma((count,))] * 2
        + [dma((4, 3)), pltpu.SemaphoreType.REGULAR],
        compiler_params=pltpu.CompilerParams(
            collective_id=0, has_side_effects=True, vmem_limit_bytes=62 * 1024 * 1024
        ),
        name="closing",
    )(lengths, tables, codes, cotangent, *enc_grads_in, *dec_kept, *enc_kept, *own, *other, *dec_left, *enc_left)


def finish_kernel(vectors_ref, bias_ref, *refs):
    sources, targets, (bias_out, vectors_out), held, (in_sems, out_sems) = split_refs(refs, (6, 6, 2, 6, 2))
    pieces = []
    for source, target, room in zip(sources, targets, held):
        rows = source.shape[0]
        step = rows // 4 if rows >= 512 else rows
        pieces = pieces + [
            tuple(ref.at[pl.ds(start, step)] for ref in (source, room, target)) for start in range(0, rows, step)
        ]
    loads = [pltpu.make_async_copy(s, h, in_sems.at[i]) for i, (s, h, _) in enumerate(pieces)]
    saves = [pltpu.make_async_copy(h, t, out_sems.at[i]) for i, (_, h, t) in enumerate(pieces)]
    start_copies(loads)
    place = lax.axis_index("dp")

    def from_place(ref, out):
        whole, part = ref.shape[1], out.shape[1]
        turned = pltpu.roll(ref[...], (whole - place * part) % whole, 1)
        out[...] = turned[: out.shape[0], :part]

    for load, save in zip(loads, saves):
        load.wait()
        save.start()
    from_place(vectors_ref, vectors_out)
    from_place(bias_ref, bias_out)
    wait_copies(saves)


def finish(results, vector_sums, bias_sums, devices):
    small = [
        jax.ShapeDtypeStruct((1, bias_sums.shape[1] // devices), jnp.float32),
        jax.ShapeDtypeStruct((VECTORS, vector_sums.shape[1] // devices), jnp.float32),
    ]
    return pl.pallas_call(
        finish_kernel,
        out_shape=tuple(jax.ShapeDtypeStruct(a.shape, a.dtype) for a in results) + tuple(small),
        in_specs=[in_vmem()] * 2 + [in_place()] * 6,
        out_specs=[in_place()] * 6 + [in_vmem()] * 2,
        scratch_shapes=[pltpu.VMEM(a.shape, a.dtype) for a in results]
        + [pltpu.SemaphoreType.DMA((12,)), pltpu.SemaphoreType.DMA((12,))],
        compiler_params=pltpu.CompilerParams(vmem_limit_bytes=60 * 1024 * 1024),
        name="finish",
    )(vector_sums, bias_sums, *results)


def count_codes(all_codes, code_count):
    high = -(-code_count // LANES)
    high_hot = (all_codes[:, None] // LANES == jnp.arange(high, dtype=jnp.int32)).astype(jnp.bfloat16)
    low_hot = (all_codes[:, None] % LANES == jnp.arange(LANES, dtype=jnp.int32)).astype(jnp.bfloat16)
    counts = transposed_times(high_hot, low_hot)
    return counts.reshape(-1)[:code_count].astype(jnp.int32)


def code_statistics(histogram, rows):
    code_share = histogram.astype(jnp.float32) / rows
    is_used = histogram > 0
    usage_share = jnp.mean(is_used.astype(jnp.float32))
    entropy = -jnp.sum(
        jnp.where(is_used, code_share * jnp.log(jnp.where(is_used, code_share, 1.0)), 0.0)
    )
    return jnp.stack([usage_share, jnp.exp(entropy) / histogram.shape[0]])


def plain_closing(
    is_first, lengths, tables, cotangent, enc_grads_in, dec_kept, enc_kept, own, other, encoded, decoded, shown,
    swapped, ordered, vector_count, width,
):
    code_grad, dec_branch, dec_pre, dec_attn, dec_projected, dec_sums = block_backward(
        1, lengths, tables, (cotangent,), dec_kept, own, other
    )
    grad, branch, pre, attn, projected, enc_sums = block_backward(
        0, lengths, tables, (code_grad, *enc_grads_in), enc_kept, own, other
    )
    encoder = ((encoded[1], encoded[3], encoded[4], encoded[6]), (projected, attn, pre, branch))
    decoder = ((decoded[1], decoded[3], decoded[4], decoded[6]), (dec_projected, dec_attn, dec_pre, dec_branch))
    results = []
    for index in range(4):
        product = times if index in (0, 2) else transposed_times
        enc = product(encoder[0][index], encoder[1][index])
        dec = product(decoder[0][index], decoder[1][index])
        results.append(jnp.where(is_first, enc, dec) + swapped(jnp.where(is_first, dec, enc)))
    own_sums, other_sums = ordered(enc_sums, dec_sums)
    sums = own_sums + swapped(other_sums)
    bias_rows = own[2].shape[1] // width
    results = results + [sums[vector_count : vector_count + bias_rows].reshape(-1), sums[:vector_count]]
    weight_grads = tuple(
        lax.psum_scatter(part, "dp", scatter_dimension=axis, tiled=True)
        for part, axis in zip(results, (0, 0, 0, 0, 0, 1))
    )

    def both_micro(enc_rows, dec_rows):
        own_rows, other_rows = ordered(enc_rows, dec_rows)
        return jnp.concatenate(ordered(own_rows, swapped(other_rows)), axis=0)

    return weight_grads, both_micro(*shown), both_micro(grad, code_grad)


def body(
    patches,
    cotangent,
    codes,
    lengths,
    codebook,
    qkv_weight,
    out_weight,
    up_weight,
    down_weight,
    up_bias,
    vectors,
):
    section_index = lax.axis_index("section")
    is_first = section_index == 0
    devices = lax.axis_size("dp")
    tok_rows, model_width = patches.shape
    row_count = tok_rows // lengths.shape[0]
    code_count = codebook.shape[0] * devices

    def swapped(array):
        return lax.ppermute(array, "section", [(0, 1), (1, 0)])

    def ordered(own, other):
        return jnp.where(is_first, own, other), jnp.where(is_first, other, own)

    own = (qkv_weight[0], out_weight[0], up_weight[0], down_weight[0])
    if devices == 16:
        other, tables, all_codes, chosen, encoded = opening(
            lengths, codes, vectors, up_bias, patches, codebook, own, devices, row_count
        )
        decoded, other_down = forward_swap(lengths, chosen, tables, own, other)
        other = (*other, other_down)
    else:
        other, tables, all_codes, chosen, encoded = plain_opening(
            lengths, codes, table_of(vectors[0], up_bias[0]), patches, codebook, own, swapped, ordered, row_count
        )
        decoded = block_forward(1, lengths, chosen, tables, own, other)
        shown = (encoded[8], decoded[8])
        enc_grads_in = (encoded[0], chosen)
        encoded, decoded = ((*made[1:8], made[9]) for made in (encoded, decoded))

    def saved(rows, made):
        hidden, _, projected, mixed, _, slope, _, stats = made
        return rows, hidden, projected, mixed, slope, stats

    if devices == 16:
        *weight_grads, vector_sums, bias_sums, counts, code_stats, outputs, input_grad = closing(
            lengths, tables, all_codes, code_count, cotangent, (chosen,), saved(chosen, decoded),
            saved(patches, encoded), own, other, (decoded[1], decoded[4], decoded[6]),
            (encoded[1], encoded[4], encoded[6]), devices,
        )
        histogram, code_stats = counts.reshape(-1)[:code_count], code_stats[0]
        *weight_grads, outputs, input_grad, bias_grad, vector_grad = finish(
            (*weight_grads, outputs, input_grad), vector_sums, bias_sums, devices
        )
        weight_grads = (*weight_grads, bias_grad[0], vector_grad)
    else:
        histogram = count_codes(all_codes, code_count)
        code_stats = code_statistics(histogram, tok_rows * devices)
        weight_grads, outputs, input_grad = plain_closing(
            is_first, lengths, tables, cotangent, enc_grads_in, saved(chosen, decoded), saved(patches, encoded), own,
            other, encoded, decoded, shown, swapped, ordered, vectors.shape[1], model_width,
        )
    return (outputs[None], input_grad[None], *(part[None] for part in weight_grads), histogram, code_stats)


def solution(mesh):
    placed = (
        P("dp", None),
        P("dp", None),
        P("dp"),
        P("dp", None),
        P("dp", None),
        P("section", None, None),
        P("section", None, None),
        P("section", None, None),
        P("section", None, None),
        P("section", None),
        P("section", None, None),
    )
    return jax.shard_map(
        body,
        mesh=mesh,
        in_specs=placed,
        out_specs=(
            P("section", "dp", None),
            P("section", "dp", None),
            P("section", "dp", None),
            P("section", "dp", None),
            P("section", "dp", None),
            P("section", "dp", None),
            P("section", "dp"),
            P("section", None, "dp"),
            P(),
            P(),
        ),
        check_vma=False,
    )
```

```python
import functools
import math

import jax
import jax.numpy as jnp
from jax import lax
from jax.experimental import pallas as pl
from jax.experimental.pallas import tpu as pltpu
from jax.sharding import PartitionSpec as P

HEADS = 12
LANES = 128
TILE = 256
MESH = pl.DeviceIdType.MESH
MASKED = -1e30
GELU_SCALE = math.sqrt(2.0 / math.pi)
GELU_CUBIC = 0.044715


def times_transposed(first_term, second_term):
    return lax.dot_general(
        first_term, second_term, (((1,), (1,)), ((), ())), preferred_element_type=jnp.float32
    )


def transposed_times(first_term, second_term):
    return lax.dot_general(
        first_term, second_term, (((0,), (0,)), ((), ())), preferred_element_type=jnp.float32
    )


def times(first_term, second_term):
    return jnp.dot(first_term, second_term, preferred_element_type=jnp.float32)


def in_vmem():
    return pl.BlockSpec(memory_space=pltpu.VMEM)


def in_smem():
    return pl.BlockSpec(memory_space=pltpu.SMEM)


def in_place():
    return pl.BlockSpec(memory_space=pl.ANY)


def normalized(rows):
    row_mean = jnp.mean(rows, axis=-1, keepdims=True)
    centered = rows - row_mean
    variance = jnp.mean(centered * centered, axis=-1, keepdims=True)
    scale = lax.rsqrt(variance + 1e-06)
    return centered * scale, scale


def norm_backward(grad, hat, scale, gain_row):
    grad_hat = grad * gain_row
    first = jnp.mean(grad_hat, axis=-1, keepdims=True)
    second = jnp.mean(grad_hat * hat, axis=-1, keepdims=True)
    return scale * (grad_hat - first - hat * second)


def column_sum(rows):
    return jnp.sum(rows.astype(jnp.float32), axis=0, keepdims=True)


def fill_marks(lengths_ref, head_size, query_marks, key_marks):
    heads, rows, _ = query_marks.shape
    images = lengths_ref.shape[1]
    for head in range(heads):
        lane = lax.broadcasted_iota(jnp.int32, (1, LANES), 1) - (1 - head) * head_size
        inside = jnp.logical_and(lane >= 0, lane < images)
        for start in range(0, rows, LANES):
            positions = lax.broadcasted_iota(jnp.int32, (LANES, 1), 0) + start
            end, label = 0, jnp.zeros_like(positions)
            for image in range(images - 1):
                end = end + lengths_ref[lax.axis_index("section"), image]
                label = label + (positions >= end).astype(jnp.int32)
            same = label == lane
            other = jnp.logical_and(inside, jnp.logical_not(same))
            same = jnp.logical_and(inside, same)
            part = pl.ds(start, LANES)
            query_marks[head, part, :] = jnp.where(other, MASKED, 0.0).astype(jnp.bfloat16)
            key_marks[head, part, :] = jnp.where(same, 1.0, 0.0).astype(jnp.bfloat16)


def head_lanes(head, head_size, factor):
    lane = lax.broadcasted_iota(jnp.int32, (1, LANES), 1)
    inside = jnp.logical_and(lane >= head * head_size, lane < (head + 1) * head_size)
    return jnp.where(inside, factor, 0.0).astype(jnp.bfloat16)


def lane_block(index):
    return pl.ds(pl.multiple_of(index * LANES, LANES), LANES)


class Weights:
    def __init__(self, own_flag, own, other, held, sems):
        self.own_flag, self.own, self.other, self.held, self.sems = own_flag, own, other, held, sems

    def place(self, index):
        return self.held[index], self.sems.at[index]

    def start(self, index):
        @pl.when(self.own_flag == 1)
        def _():
            pltpu.make_async_copy(self.own[index], *self.place(index)).start()

        @pl.when(self.own_flag != 1)
        def _():
            pltpu.make_async_copy(self.other[index], *self.place(index)).start()

    def wait(self, index):
        pltpu.make_async_copy(self.own[index], *self.place(index)).wait()
        return self.place(index)[0]


def table_of(vectors, up_bias):
    width = vectors.shape[1]
    rows = jnp.concatenate([vectors, up_bias.reshape(-1, width)], axis=0).astype(jnp.float32)
    return jnp.pad(rows, ((0, -rows.shape[0] % 8), (0, 0)))


def up_bias_tile(table, first_row, j, width):
    per_row = width // TILE
    column = pl.multiple_of(j % per_row * TILE, TILE)
    return table[pl.ds(first_row + j // per_row, 1), pl.ds(column, TILE)]


VECTORS = 8
GROUP = 1 << 14
UNROLL = 4
PIECES = 3
SAVED = ("out", "hidden", "normed", "qkv", "mixed", "second", "slope", "act", "shown")


def saved_shapes(row_count, width, hidden_units):
    bfloat16, float32 = jnp.bfloat16, jnp.float32
    return [
        ((row_count, width), float32),
        ((row_count, width), float32),
        ((row_count, width), bfloat16),
        ((row_count, 3 * width), bfloat16),
        ((row_count, width), bfloat16),
        ((row_count, width), bfloat16),
        ((row_count, hidden_units), bfloat16),
        ((row_count, hidden_units), bfloat16),
        ((row_count, width), bfloat16),
    ]


def turned_sources(buffers, work):
    out, hidden, _, qkv, mixed, _, *rest = buffers
    return (out, hidden, work[4], qkv, mixed, work[5], *rest)


def turned_shapes(kept):
    return [((shape[1], shape[0]), kind) if index in (2, 5) else (shape, kind) for index, (shape, kind) in enumerate(kept)]


def forward_steps(table, lengths_ref, rows_ref, stat_ref, buffers, work, weight, save, during):
    _, hidden_ref, normed_ref, qkv_ref, mixed_ref, second_ref = buffers[:6]
    query_marks, key_marks, max_columns, sum_columns, normed_turned, second_turned = work
    rows, width = rows_ref.shape
    head_size = width // HEADS
    per_block = LANES // head_size
    half = rows // 2
    per_part = width // TILE

    fill_marks(lengths_ref, head_size, query_marks, key_marks)
    for start in range(0, rows, LANES):
        part = pl.ds(start, LANES)
        hat, _ = normalized(rows_ref[part, :].astype(jnp.float32))
        normed_ref[part, :] = (hat * (1.0 + table[0:1, :]) + table[1:2, :]).astype(jnp.bfloat16)
    normed_turned[...] = jnp.transpose(normed_ref[...])
    save("normed")
    during("normed", 0)

    qkv_held = weight(0)
    for j in range(3 * per_part):
        columns = pl.ds(j * TILE, TILE)
        projected = times(normed_ref[...], qkv_held[:, columns])
        if j // per_part != 1:
            row = 2 + j // (2 * per_part)
            projected = projected + table[row : row + 1, pl.ds(j % per_part * TILE, TILE)]
        qkv_ref[:, columns] = projected.astype(jnp.bfloat16)

    save("qkv")
    during("qkv", 0)
    max_columns[...] = jnp.zeros_like(max_columns)
    sum_columns[...] = jnp.ones_like(sum_columns)

    @pl.loop(0, width // LANES)
    def _(i):
        keys = qkv_ref[:, lane_block(width // LANES + i)]
        values = qkv_ref[:, lane_block(2 * width // LANES + i)]
        lane = lax.broadcasted_iota(jnp.int32, (1, LANES), 1)
        keys_of = [keys * head_lanes(h, head_size, 1.0) + key_marks[h] for h in range(per_block)]
        values_of = [
            values * head_lanes(h, head_size, 1.0) + head_lanes(1 - h, head_size, 1.0) for h in range(per_block)
        ]
        units = [(start, h) for start in range(0, rows, half) for h in range(per_block)]

        def scores_of(unit):
            start, h = unit
            part = pl.ds(start, half)
            query = qkv_ref[part, lane_block(i)] * head_lanes(h, head_size, head_size**-0.5) + query_marks[h, part, :]
            return times_transposed(query, keys_of[h])

        ahead = scores_of(units[0])
        mixed = None
        for number, (start, h) in enumerate(units):
            part = pl.ds(start, half)
            scores = ahead
            if number + 1 < len(units):
                ahead = scores_of(units[number + 1])
            row_max = jnp.max(scores, axis=-1, keepdims=True)
            exponent = jnp.exp(scores - row_max).astype(jnp.bfloat16)
            sums = times(exponent, values_of[h])
            inside = jnp.logical_and(lane >= h * head_size, lane < (h + 1) * head_size)
            row_total = jnp.where(inside, pltpu.roll(sums, head_size, 1), sums)
            term = sums / row_total
            mixed = term if h == 0 else jnp.where(inside, term, mixed)
            here = lane == per_block * i + h
            max_columns[part, :] = jnp.where(here, row_max, max_columns[part, :])
            sum_columns[part, :] = jnp.where(here, row_total, sum_columns[part, :])
            if h == per_block - 1:
                mixed_ref[part, lane_block(i)] = mixed.astype(jnp.bfloat16)
        during("heads", i)

    save("mixed")
    stats = max_columns[...] + jnp.log(sum_columns[...])
    stat_ref[...] = jnp.transpose(stats)[: stat_ref.shape[0], :]

    out_held = weight(1)
    for start in range(0, width, TILE):
        columns = pl.ds(start, TILE)
        hidden_ref[:, columns] = (
            rows_ref[:, columns].astype(jnp.float32)
            + times(mixed_ref[...], out_held[:, columns])
            + table[4:5, columns]
        )
    save("hidden")
    for start in range(0, rows, LANES):
        part = pl.ds(start, LANES)
        hat, _ = normalized(hidden_ref[part, :])
        second_ref[part, :] = (hat * (1.0 + table[5:6, :]) + table[6:7, :]).astype(jnp.bfloat16)
    second_turned[...] = jnp.transpose(second_ref[...])
    save("second")
    during("second", 0)


def up_product(table, second_ref, up_held, slope_ref, act_ref):
    tiles, width = up_held.shape[1] // TILE, second_ref.shape[1]

    @pl.loop(0, tiles // UNROLL)
    def _(group):
        def columns_of(j):
            return pl.ds(pl.multiple_of((group * UNROLL + j) * TILE, TILE), TILE)

        def pre_of(j):
            return times(second_ref[...], up_held[:, columns_of(j)])

        ahead = pre_of(0)
        for j in range(UNROLL):
            pre = ahead + up_bias_tile(table, VECTORS, group * UNROLL + j, width)
            if j + 1 < UNROLL:
                ahead = pre_of(j + 1)
            square = pre * pre
            bent = jnp.tanh(pre * (GELU_SCALE + (GELU_SCALE * GELU_CUBIC) * square))
            share = 0.5 + 0.5 * bent
            act_ref[:, columns_of(j)] = (pre * share).astype(jnp.bfloat16)
            steep = (0.5 - 0.5 * (bent * bent)) * (GELU_SCALE + (3.0 * GELU_SCALE * GELU_CUBIC) * square)
            slope_ref[:, columns_of(j)] = (share + pre * steep).astype(jnp.bfloat16)


def last_product(table, hidden_ref, act_ref, down_held, out_ref, shown_ref):
    for start in range(0, hidden_ref.shape[1], TILE):
        columns = pl.ds(start, TILE)
        result = hidden_ref[:, columns] + times(act_ref[...], down_held[:, columns]) + table[7:8, columns]
        if out_ref is not None:
            out_ref[:, columns] = result
        if shown_ref is not None:
            shown_ref[:, columns] = result.astype(jnp.bfloat16)


def forward_kernel(block, lengths_ref, rows_ref, tables_ref, *refs):
    own, other, made, (stat_ref,), held, buffers, work, (weight_sems, save_sems) = split_refs(
        refs, (4, 4, 9, 1, 4, 9, 6, 2)
    )
    weights = Weights((lax.axis_index("section") == block).astype(jnp.int32), own, other, held, weight_sems)
    for index in range(4):
        weights.start(index)
    saves = {
        name: pltpu.make_async_copy(source, target, save_sems.at[index])
        for index, (name, source, target) in enumerate(zip(SAVED, turned_sources(buffers, work), made))
    }
    table = tables_ref.at[block]
    forward_steps(
        table, lengths_ref, rows_ref, stat_ref, buffers, work, weights.wait,
        lambda name: saves[name].start(), lambda place, i: None,
    )
    up_product(table, buffers[5], weights.wait(2), buffers[6], buffers[7])
    last_product(table, buffers[1], buffers[7], weights.wait(3), buffers[0], buffers[8])
    for name in ("slope", "act", "out", "shown"):
        saves[name].start()
    for save in saves.values():
        save.wait()


def forward_work(row_count, width):
    return [
        pltpu.VMEM((2, row_count, LANES), jnp.bfloat16),
        pltpu.VMEM((2, row_count, LANES), jnp.bfloat16),
        pltpu.VMEM((row_count, LANES), jnp.float32),
        pltpu.VMEM((row_count, LANES), jnp.float32),
        pltpu.VMEM((width, row_count), jnp.bfloat16),
        pltpu.VMEM((width, row_count), jnp.bfloat16),
    ]


def forward_scratch(own, kept, row_count):
    return (
        [pltpu.VMEM(w.shape, w.dtype) for w in own]
        + [pltpu.VMEM(s, t) for s, t in kept]
        + forward_work(row_count, kept[0][0][1])
        + [pltpu.SemaphoreType.DMA((4,)), pltpu.SemaphoreType.DMA((9,))]
    )


def forward_swap_kernel(lengths_ref, rows_ref, tables_ref, *refs):
    (
        own, other, (own_down,), made, (stat_ref, other_down), held, buffers, work,
        (own_held, other_held, weight_sems, save_sems, down_sems),
    ) = split_refs(refs, (3, 3, 1, 7, 2, 3, 8, 6, 5))
    section = lax.axis_index("section")
    barrier = pltpu.get_barrier_semaphore()
    pl.semaphore_signal(barrier, inc=1, device_id={"section": 1 - section}, device_id_type=MESH)
    weights = Weights((section == 1).astype(jnp.int32), own, other, held, weight_sems)
    for index in range(3):
        weights.start(index)
    size = own_down.shape[0] // PIECES
    parts = [pl.ds(piece * size, size) for piece in range(PIECES)]
    loads = [
        pltpu.make_async_copy(own_down.at[part], own_held.at[part], down_sems.at[0, piece])
        for piece, part in enumerate(parts)
    ]
    start_copies(loads)
    pl.semaphore_wait(barrier, 1)
    swaps = [
        pltpu.make_async_remote_copy(
            src_ref=own_held.at[part], dst_ref=other_held.at[part], send_sem=down_sems.at[1, piece],
            recv_sem=down_sems.at[2, piece], device_id={"section": 1 - section}, device_id_type=MESH,
        )
        for piece, part in enumerate(parts)
    ]
    for load, swap in zip(loads, swaps):
        load.wait()
        swap.start()
    saves = {
        name: pltpu.make_async_copy(source, target, save_sems.at[index])
        for index, (name, source, target) in enumerate(zip(SAVED[1:8], turned_sources(buffers, work)[1:], made))
    }
    forward_steps(
        tables_ref.at[1], lengths_ref, rows_ref, stat_ref, buffers, work, weights.wait,
        lambda name: saves[name].start(), lambda place, i: None,
    )
    wait_copies(swaps)
    keep = pltpu.make_async_copy(other_held, other_down, down_sems.at[0, 0])
    keep.start()
    up_product(tables_ref.at[1], buffers[5], weights.wait(2), buffers[6], buffers[7])
    saves["slope"].start()
    saves["act"].start()
    for save in saves.values():
        save.wait()
    keep.wait()


def forward_swap(lengths, rows, tables, own, other):
    row_count, width = rows.shape
    kept = saved_shapes(row_count, width, own[2].shape[1])[:8]
    shapes = turned_shapes(kept)[1:] + [((16, row_count), jnp.float32), (own[3].shape, own[3].dtype)]
    results = pl.pallas_call(
        forward_swap_kernel,
        out_shape=tuple(jax.ShapeDtypeStruct(s, t) for s, t in shapes),
        in_specs=[in_smem()] + [in_vmem()] * 2 + [in_place()] * 7,
        out_specs=[in_place()] * 7 + [in_vmem(), in_place()],
        scratch_shapes=[pltpu.VMEM(w.shape, w.dtype) for w in own[:3]]
        + [pltpu.VMEM(s, t) for s, t in kept]
        + forward_work(row_count, width)
        + [
            pltpu.VMEM(own[3].shape, own[3].dtype),
            pltpu.VMEM(own[3].shape, own[3].dtype),
            pltpu.SemaphoreType.DMA((4,)),
            pltpu.SemaphoreType.DMA((9,)),
            pltpu.SemaphoreType.DMA((3, PIECES)),
        ],
        compiler_params=pltpu.CompilerParams(
            collective_id=2, has_side_effects=True, vmem_limit_bytes=56 * 1024 * 1024
        ),
        name="forward_swap",
    )(lengths, rows, tables, *own[:3], *other, own[3])
    return results[:8], results[8]


def block_forward(block, lengths, rows, tables, own, other):
    row_count, width = rows.shape
    kept = saved_shapes(row_count, width, own[2].shape[1])
    stat_shape = (16, row_count)
    return pl.pallas_call(
        functools.partial(forward_kernel, block),
        out_shape=tuple(jax.ShapeDtypeStruct(s, t) for s, t in turned_shapes(kept))
        + (jax.ShapeDtypeStruct(stat_shape, jnp.float32),),
        in_specs=[in_smem()] + [in_vmem()] * 2 + [in_place()] * 8,
        out_specs=[in_place()] * 9 + [in_vmem()],
        scratch_shapes=forward_scratch(own, kept, row_count),
        compiler_params=pltpu.CompilerParams(vmem_limit_bytes=56 * 1024 * 1024),
        cost_estimate=pl.CostEstimate(
            flops=2 * row_count * (12 * width * width + 2 * row_count * width),
            bytes_accessed=40 * 1024 * 1024,
            transcendentals=row_count * row_count * HEADS,
        ),
        name="block_forward",
    )(lengths, rows, tables, *own, *other)


def split_refs(refs, counts):
    groups, start = [], 0
    for count in counts:
        groups.append(refs[start : start + count])
        start = start + count
    return groups


def opening_kernel(real_shard, lengths_ref, code_tile_ref, vectors_ref, up_bias_ref, patches_ref, book_ref, book_end_ref, *refs):
    (
        own, other, (tables_ref, all_codes_ref, chosen_ref), made, (stat_ref,), held, buffers, work,
        (weight_sems, save_sems),
        (rows_ref, book, total, half_out, half_in, table_in, code_slots, table_out, codes_ref),
        (load_sems, weight_send, weight_got, zero_send, zero_got, middle_send, middle_got, last_send, last_got,
         code_send, code_got, side_send, side_got, keep_sems),
    ) = split_refs(refs, (3, 3, 3, 7, 1, 3, 8, 6, 2, 9, 14))
    section, place = lax.axis_index("section"), lax.axis_index("dp")
    depth = book.shape[2]
    shard_rows, half_width = book.shape[3:]
    rows = rows_ref.shape[0]
    my_x, my_y, my_z = place % 2, place // 2 % 2, place // 4
    my_middle = my_y * (1 - section) + my_x * section
    my_last = my_x * (1 - section) + my_y * section
    middle_device = place + (1 - 2 * my_middle) * (2 - section)
    last_device = place + (1 - 2 * my_last) * (1 + section)

    barrier = pltpu.get_barrier_semaphore()
    pl.semaphore_signal(barrier, inc=1, device_id={"section": 1 - section}, device_id_type=MESH)
    for device in (middle_device, last_device):
        pl.semaphore_signal(barrier, inc=1, device_id={"dp": device}, device_id_type=MESH)
    for hop in range(1, depth):
        device = (my_z + hop) % depth * 4 + my_y * 2 + my_x
        pl.semaphore_signal(barrier, inc=1, device_id={"dp": device}, device_id_type=MESH)

    own_book = book.at[my_middle, my_last, my_z]
    columns = pl.ds(pl.multiple_of(section * half_width, LANES), half_width)
    whole = shard_rows - book_end_ref.shape[0]
    load_book = pltpu.make_async_copy(
        book_ref.at[pl.ds(0, whole), columns], own_book.at[pl.ds(0, whole)], load_sems.at[0]
    )
    load_end = pltpu.make_async_copy(
        book_end_ref.at[:, columns], own_book.at[pl.ds(whole, shard_rows - whole)], load_sems.at[2]
    )
    load_end.start()
    load_book.start()
    load_rows = pltpu.make_async_copy(
        patches_ref.at[pl.ds(pl.multiple_of(section * rows, rows), rows)], rows_ref, load_sems.at[1]
    )
    load_rows.start()
    own_codes = code_slots.at[my_z, my_middle, my_last]
    own_codes[...] = code_tile_ref[...]
    width = vectors_ref.shape[2]
    table_out[...] = jnp.zeros_like(table_out)
    table_out[:VECTORS, :] = vectors_ref[0].astype(jnp.float32)
    for j in range(up_bias_ref.shape[1] // width):
        table_out[VECTORS + j : VECTORS + j + 1, :] = up_bias_ref[:, j * width : (j + 1) * width].astype(jnp.float32)
    tables_ref[section] = table_out[...]
    codes = code_tile_ref[...]

    def shards_below(size):
        found = jnp.zeros_like(codes)
        for limit in range(size * real_shard, 4 * depth * real_shard, size * real_shard):
            found = found + (codes >= limit).astype(jnp.int32)
        return found

    holder, holder_z, holder_pair = shards_below(1), shards_below(4), shards_below(2)
    holder_y, holder_x = holder_pair - 2 * holder_z, holder - 2 * holder_pair
    holder_middle = holder_y * (1 - section) + holder_x * section
    holder_last = holder_x * (1 - section) + holder_y * section
    spot = (2 * holder_middle + holder_last) * GROUP + holder_z * shard_rows + codes - holder * real_shard
    turned = jnp.transpose(spot.astype(jnp.float32))
    for j in range(code_tile_ref.shape[0]):
        codes_ref[j * LANES : (j + 1) * LANES, :] = turned[:, j : j + 1].astype(jnp.int32)
    total[...] = jnp.zeros_like(total)

    def remote(source, land, send, got, **device):
        return pltpu.make_async_remote_copy(
            src_ref=source, dst_ref=land, send_sem=send, recv_sem=got, device_id=device, device_id_type=MESH
        )

    near = [sorted(range(depth), key=lambda z, here=here: (abs(z - here), z)) for here in range(depth)]

    def source_z(rank):
        found = my_z
        for here in range(depth):
            for other_rank in range(1, depth):
                here_now = jnp.logical_and(my_z == here, rank == other_rank)
                found = jnp.where(here_now, near[here][other_rank], found)
        return found

    def zero(source, target):
        part = book.at[my_middle, my_last, source]
        device = target * 4 + my_y * 2 + my_x
        return remote(part, part, zero_send.at[source, target], zero_got.at[source], dp=device)

    def zero_next(source):
        following = jnp.where(source < my_z, my_z + 1, my_z - 1)
        there = jnp.logical_and(following >= 0, following < depth)
        return jnp.clip(following, 0, depth - 1), there

    def zero_own(act):
        for step in (-1, 1):
            target = my_z + step
            there = jnp.logical_and(target >= 0, target < depth)

            @pl.when(there)
            def _():
                act(zero(my_z, jnp.clip(target, 0, depth - 1)))

    def middle(rank):
        source = source_z(rank)
        part = book.at[my_middle, my_last, source]
        return remote(part, part, middle_send.at[source], middle_got.at[source], dp=middle_device)

    def last(side, rank):
        source = source_z(rank)
        which = my_middle if side == 0 else 1 - my_middle
        part = book.at[which, my_last, source]
        return remote(part, part, last_send.at[side, source], last_got.at[side, source], dp=last_device)

    def codes_zero(hop):
        target = (my_z + hop) % depth * 4 + my_y * 2 + my_x
        return remote(own_codes, own_codes, code_send.at[hop - 1], code_got.at[hop - 1], dp=target)

    def codes_middle():
        part = code_slots.at[:, my_middle, my_last]
        return remote(part, part, code_send.at[depth], code_got.at[depth], dp=middle_device)

    def codes_last():
        part = code_slots.at[:, :, my_last]
        return remote(part, part, code_send.at[depth + 1], code_got.at[depth + 1], dp=last_device)

    def own_matrix(index):
        return pltpu.make_async_copy(own[index], held[index].at[section], weight_sems.at[index])

    def weight_across(index):
        copies, size = [], held[index].shape[1] // PIECES
        for piece in range(PIECES):
            part = held[index].at[section, pl.ds(piece * size, size)]
            send, got = weight_send.at[index, piece], weight_got.at[index, piece]
            copies.append(remote(part, part, send, got, section=1 - section))
        return copies

    def weight_arrived(index):
        for copy in weight_across(index):
            copy.wait_recv()

    def keep(index):
        return pltpu.make_async_copy(held[index].at[1 - section], other[index], keep_sems.at[index])

    def send_matrix(index):
        own_matrix(index).wait()
        start_copies(weight_across(index))

    table_across = remote(table_out, table_in, side_send.at[0], side_got.at[0], section=1 - section)
    half_across = remote(half_out, half_in, side_send.at[1], side_got.at[1], section=1 - section)

    def pick_rows(which_middle, which_last, block):
        group = 2 * which_middle + which_last
        part = pl.ds(pl.multiple_of(block * rows, rows), rows)
        inside = codes_ref[part, :] - group * GROUP
        lanes = lax.broadcasted_iota(jnp.int32, (1, depth * shard_rows), 1)
        hot = jnp.where(inside == lanes, 1.0, 0.0).astype(jnp.bfloat16)
        shards = book[which_middle, which_last].reshape(depth * shard_rows, half_width)
        total[part, :] = total[part, :] + times(hot, shards)

    def pick(which_middle, which_last):
        @pl.loop(0, total.shape[0] // rows)
        def _(block):
            pick_rows(which_middle, which_last, block)

    for index in range(3):
        own_matrix(index).start()
    pl.semaphore_wait(barrier, 3 + depth - 1)
    table_across.start()
    load_book.wait()
    load_end.wait()
    zero_own(lambda copy: copy.start())
    middle(0).start()
    last(0, 0).start()
    send_matrix(0)
    for hop in range(1, depth):
        codes_zero(hop).start()

    load_rows.wait()
    table_across.wait_recv()
    tables_ref[1 - section] = table_in[...]

    def weight(index):
        @pl.when(section == 1)
        def _():
            weight_arrived(index)
            keep(index).start()

        return held[index].at[0]

    def keep_late(index):
        @pl.when(section == 0)
        def _():
            weight_arrived(index)
            keep(index).start()

    saves = {
        name: pltpu.make_async_copy(source, target, save_sems.at[index])
        for index, (name, source, target) in enumerate(zip(SAVED[1:8], turned_sources(buffers, work)[1:], made))
    }

    def from_zero(rank):
        source = source_z(rank)
        following, there = zero_next(source)
        zero(source, following).wait_recv()

        @pl.when(there)
        def _():
            zero(source, following).start()

        middle(rank).start()
        last(0, rank).start()

    def from_middle(rank):
        middle(rank).wait_recv()
        last(1, rank).start()

    def arrived_last(side):
        for rank in range(depth):
            last(side, rank).wait_recv()

    def during(where, i):
        if where == "normed":
            from_zero(1)
            send_matrix(1)
            send_matrix(2)
        elif where == "qkv":
            from_middle(0)
            from_zero(2)
        elif where == "heads":

            @pl.when(i == 0)
            def _():
                from_middle(1)

            @pl.when(i == 1)
            def _():
                from_zero(3)

            @pl.when(i == 2)
            def _():
                from_middle(2)

            @pl.when(i == 3)
            def _():
                from_middle(3)

            @pl.when(i == 4)
            def _():
                pick(my_middle, my_last)

        elif where == "second":
            for hop in range(1, depth):
                codes_zero(hop).wait_recv()
            codes_middle().start()
            pick(1 - my_middle, my_last)

    forward_steps(
        tables_ref.at[0], lengths_ref, rows_ref, stat_ref, buffers, work, weight,
        lambda name: saves[name].start(), during,
    )
    table = tables_ref.at[0]
    keep_late(0)
    up_product(table, buffers[5], weight(2), buffers[6], buffers[7])
    saves["slope"].start()
    saves["act"].start()
    arrived_last(0)
    pick(my_middle, 1 - my_last)
    codes_middle().wait_recv()
    codes_last().start()
    keep_late(1)
    keep_late(2)
    arrived_last(1)
    own_rows = pl.ds(pl.multiple_of(section * rows, rows), rows)
    other_rows = pl.ds(pl.multiple_of((1 - section) * rows, rows), rows)
    pick_rows(1 - my_middle, 1 - my_last, 1 - section)
    half_out[...] = total[other_rows, :].astype(half_out.dtype)
    half_across.start()
    pick_rows(1 - my_middle, 1 - my_last, section)
    chosen_ref[:, pl.ds(pl.multiple_of(section * half_width, LANES), half_width)] = total[own_rows, :].astype(
        chosen_ref.dtype
    )
    half_across.wait_recv()
    chosen_ref[:, pl.ds(pl.multiple_of((1 - section) * half_width, LANES), half_width)] = half_in[...]
    codes_last().wait_recv()
    all_codes_ref[...] = code_slots[...]
    for index in range(3):
        for copy in weight_across(index):
            copy.wait_send()
        keep(index).wait()
    table_across.wait_send()
    half_across.wait_send()
    zero_own(lambda copy: copy.wait_send())
    for hop in range(1, depth):
        source = source_z(hop)
        following, there = zero_next(source)

        @pl.when(there)
        def _():
            zero(source, following).wait_send()

        codes_zero(hop).wait_send()
    for hop in range(depth):
        middle(hop).wait_send()
        for side in range(2):
            last(side, hop).wait_send()
    codes_middle().wait_send()
    codes_last().wait_send()
    for save in saves.values():
        save.wait()


def opening(lengths, codes, vectors, up_bias, patches, codebook, own, devices, row_count):
    tokens, width = patches.shape
    half_width = width // 2
    depth, shard_rows = devices // 4, codebook.shape[0]
    whole = (shard_rows - 1) // 16 * 16
    book_end = jnp.pad(codebook[whole:], ((0, -shard_rows % 16), (0, 0)))
    padded_rows = whole + book_end.shape[0]
    table_shape = (16, width)
    code_tile = codes.reshape(-1, LANES)
    kept = saved_shapes(row_count, width, own[2].shape[1])[:8]
    bfloat16, float32 = jnp.bfloat16, jnp.float32
    shapes = (
        [(w.shape, w.dtype) for w in own[:3]]
        + [
            ((2, *table_shape), float32),
            ((depth, 2, 2, *code_tile.shape), codes.dtype),
            ((row_count, width), bfloat16),
        ]
        + turned_shapes(kept)[1:]
        + [((16, row_count), float32)]
    )
    dma = pltpu.SemaphoreType.DMA
    results = pl.pallas_call(
        functools.partial(opening_kernel, shard_rows),
        out_shape=tuple(jax.ShapeDtypeStruct(s, t) for s, t in shapes),
        in_specs=[in_smem()] + [in_vmem()] * 3 + [in_place()] * 6,
        out_specs=[in_place()] * 3 + [in_vmem()] * 3 + [in_place()] * 7 + [in_vmem()],
        scratch_shapes=[pltpu.VMEM((2, *w.shape), w.dtype) for w in own[:3]] + forward_scratch((), kept, row_count)
        + [
            pltpu.VMEM((row_count, width), bfloat16),
            pltpu.VMEM((2, 2, depth, padded_rows, half_width), bfloat16),
            pltpu.VMEM((tokens, half_width), float32),
            pltpu.VMEM((row_count, half_width), bfloat16),
            pltpu.VMEM((row_count, half_width), bfloat16),
            pltpu.VMEM(table_shape, float32),
            pltpu.VMEM((depth, 2, 2, *code_tile.shape), codes.dtype),
            pltpu.VMEM(table_shape, float32),
            pltpu.VMEM((tokens, 1), jnp.int32),
            dma((3,)),
            dma((3, PIECES)),
            dma((3, PIECES)),
            dma((depth, depth)),
            dma((depth,)),
            dma((depth,)),
            dma((depth,)),
            dma((2, depth)),
            dma((2, depth)),
            dma((depth + 2,)),
            dma((depth + 2,)),
            dma((2,)),
            dma((2,)),
            dma((4,)),
        ],
        compiler_params=pltpu.CompilerParams(
            collective_id=1, has_side_effects=True, vmem_limit_bytes=60 * 1024 * 1024
        ),
        name="opening",
    )(lengths, code_tile, vectors, up_bias, patches, codebook, book_end, *own[:3])
    return results[:3], results[3], results[4].reshape(devices, -1, LANES), results[5], results[6:]


def plain_opening(lengths, codes, table, patches, codebook, own, swapped, ordered, row_count):
    section = lax.axis_index("section")
    other = tuple(swapped(weight) for weight in own)
    tables = jnp.stack(ordered(table, swapped(table)))
    all_codes = lax.all_gather(codes, "dp", axis=0, tiled=True)
    half_width = patches.shape[1] // 2
    half_book = lax.dynamic_slice_in_dim(codebook, section * half_width, half_width, 1)
    half_book = lax.all_gather(half_book, "dp", axis=0, tiled=True)
    half_rows = jnp.take(half_book, codes, axis=0)

    def micro_rows(array, index):
        return lax.dynamic_slice_in_dim(array, index * row_count, row_count, 0)

    half_own = micro_rows(half_rows, section)
    half_other = swapped(micro_rows(half_rows, 1 - section))
    chosen = jnp.concatenate(ordered(half_own, half_other), axis=1)
    encoded = block_forward(0, lengths, micro_rows(patches, section), tables, own, other)
    return other, tables, all_codes, chosen, encoded


def backward_steps(from_code, lengths_ref, table, buffers, sums_ref, weight, arrived, save, during):
    (
        rows_ref, hidden_ref, qkv_ref, mixed_ref, slope_ref, stat_ref, branch_ref, attn_ref, projected_ref,
        grad_ref, second_ref, moved_ref, query_marks, key_marks,
    ) = buffers
    rows, width = rows_ref.shape
    hidden_units = slope_ref.shape[1]
    head_size = width // HEADS
    per_block = LANES // head_size
    half = rows // 2
    per_row = width // TILE
    sums_ref[...] = jnp.zeros_like(sums_ref)

    fill_marks(lengths_ref, head_size, query_marks, key_marks)
    arrived(("grads",))
    total = jnp.zeros((1, width), jnp.float32)
    for start in range(0, rows, LANES):
        part = pl.ds(start, LANES)
        grad = moved_ref[part, :].astype(jnp.float32)
        if from_code:
            grad = grad_ref[part, :] + 0.5 * (second_ref[part, :] - grad)
        grad_ref[part, :] = grad
        branch = grad.astype(jnp.bfloat16)
        branch_ref[part, :] = branch
        total = total + column_sum(branch)
    sums_ref[7:8, :] = total
    save("branch")
    during("branch")

    down_held = weight(3)
    arrived(("slope", "hidden"))

    def through_gelu(first, count):
        at_once = 3 if count % 3 == 0 else 1

        @pl.loop(0, count // at_once)
        def _(group):
            def tile_of(j):
                return first + group * at_once + j

            def block_of(j):
                return pl.ds(pl.multiple_of(tile_of(j) * TILE, TILE), TILE)

            def act_of(j):
                return times_transposed(branch_ref[...], down_held[block_of(j), :])

            ahead = act_of(0)
            for j in range(at_once):
                grad_act, block = ahead, block_of(j)
                if j + 1 < at_once:
                    ahead = act_of(j + 1)
                grad_pre = (grad_act * slope_ref[:, block].astype(jnp.float32)).astype(jnp.bfloat16)
                slope_ref[:, block] = grad_pre
                column = pl.multiple_of(tile_of(j) % per_row * TILE, TILE)
                sums_ref[pl.ds(VECTORS + tile_of(j) // per_row, 1), pl.ds(column, TILE)] = column_sum(grad_pre)

    tiles = hidden_units // TILE
    through_gelu(0, tiles // 4)
    during("gelu")
    through_gelu(tiles // 4, tiles - tiles // 4)
    save("pre")
    during("pre")
    up_held = weight(2)
    for start in range(0, width, TILE):
        block = pl.ds(start, TILE)
        second_ref[:, block] = times_transposed(slope_ref[...], up_held[block, :])
    during("second")

    gain_total, shift_total, attn_total = (jnp.zeros((1, width), jnp.float32) for _ in range(3))
    for start in range(0, rows, LANES):
        part = pl.ds(start, LANES)
        hat, scale = normalized(hidden_ref[part, :])
        grad = second_ref[part, :]
        gain_total = gain_total + column_sum(grad * hat)
        shift_total = shift_total + column_sum(grad)
        grad_hidden = grad_ref[part, :] + norm_backward(grad, hat, scale, 1.0 + table[5:6, :])
        grad_ref[part, :] = grad_hidden
        attn = grad_hidden.astype(jnp.bfloat16)
        attn_ref[part, :] = attn
        attn_total = attn_total + column_sum(attn)
    sums_ref[5:6, :] = gain_total
    sums_ref[6:7, :] = shift_total
    sums_ref[4:5, :] = attn_total
    save("attn")

    out_held = weight(1)
    for start in range(0, width, TILE):
        block = pl.ds(start, TILE)
        moved_ref[:, block] = times_transposed(attn_ref[...], out_held[block, :]).astype(jnp.bfloat16)
    during("attn")
    arrived(("mixed", "qkv", "stat"))

    def through_heads(first, count):
        @pl.loop(first, first + count)
        def _(i):
            query = qkv_ref[:, lane_block(i)]
            grad_mixed = moved_ref[:, lane_block(i)]
            products = jnp.transpose(
                grad_mixed.astype(jnp.float32) * mixed_ref[:, lane_block(i)].astype(jnp.float32)
            )
            mine = [head_lanes(h, head_size, 1.0) for h in range(per_block)]
            scaled = [head_lanes(h, head_size, head_size**-0.5) for h in range(per_block)]
            query_of = [query * scaled[h] for h in range(per_block)]
            marked_of = [query_of[h] + query_marks[h] for h in range(per_block)]
            grad_of = [grad_mixed * mine[h] for h in range(per_block)]
            row_dot = [
                jnp.sum(products[h * head_size : (h + 1) * head_size, :], axis=0, keepdims=True)
                for h in range(per_block)
            ]
            units = [(start, h) for start in range(0, rows, half) for h in range(per_block)]

            def products_of(unit):
                start, h = unit
                part = pl.ds(start, half)
                keys = qkv_ref[part, lane_block(width // LANES + i)]
                values = qkv_ref[part, lane_block(2 * width // LANES + i)]
                return (
                    times_transposed(keys * mine[h] + key_marks[h, part, :], marked_of[h]),
                    times_transposed(values, grad_of[h]),
                )

            ahead = products_of(units[0])
            grad_query = jnp.zeros((rows, LANES), jnp.float32)
            value_total = jnp.zeros((1, LANES), jnp.float32)
            for number, (start, h) in enumerate(units):
                part = pl.ds(start, half)
                scores, grad_probs = ahead
                if number + 1 < len(units):
                    ahead = products_of(units[number + 1])
                keys = qkv_ref[part, lane_block(width // LANES + i)]
                exact = jnp.exp(scores - stat_ref[pl.ds(per_block * i + h, 1), :])
                grad_scores = (exact * (grad_probs - row_dot[h])).astype(jnp.bfloat16)
                value_term = times(exact.astype(jnp.bfloat16), grad_of[h])
                key_term = times(grad_scores, query_of[h])
                grad_query = grad_query + transposed_times(grad_scores, keys * scaled[h])
                grad_value = value_term if h == 0 else grad_value + value_term
                grad_key = key_term if h == 0 else grad_key + key_term
                if h == per_block - 1:
                    grad_value = grad_value.astype(jnp.bfloat16)
                    projected_ref[part, lane_block(2 * width // LANES + i)] = grad_value
                    projected_ref[part, lane_block(width // LANES + i)] = grad_key.astype(jnp.bfloat16)
                    value_total = value_total + column_sum(grad_value)
            grad_query = grad_query.astype(jnp.bfloat16)
            projected_ref[:, lane_block(i)] = grad_query
            sums_ref[2:3, lane_block(i)] = column_sum(grad_query)
            sums_ref[3:4, lane_block(i)] = value_total

    groups = width // LANES
    for part in range(3):
        first, end = groups * part // 3, groups * (part + 1) // 3
        if end > first:
            through_heads(first, end - first)
        during(("heads", part))

    save("projected")
    qkv_held = weight(0)
    for start in range(0, width, TILE):
        grad_rows = None
        for j in range(3):
            term = times_transposed(
                projected_ref[:, j * width : (j + 1) * width], qkv_held[pl.ds(j * width + start, TILE), :]
            )
            grad_rows = term if grad_rows is None else grad_rows + term
        second_ref[:, pl.ds(start, TILE)] = grad_rows
    during("rows")

    arrived(("rows",))
    gain_total, shift_total = (jnp.zeros((1, width), jnp.float32) for _ in range(2))
    for start in range(0, rows, LANES):
        part = pl.ds(start, LANES)
        hat, scale = normalized(rows_ref[part, :].astype(jnp.float32))
        grad = second_ref[part, :]
        gain_total = gain_total + column_sum(grad * hat)
        shift_total = shift_total + column_sum(grad)
        grad_rows = grad_ref[part, :] + norm_backward(grad, hat, scale, 1.0 + table[0:1, :])
        grad_ref[part, :] = grad_rows if from_code else grad_rows.astype(jnp.bfloat16).astype(jnp.float32)
    sums_ref[0:1, :] = gain_total
    sums_ref[1:2, :] = shift_total
    save("grad")


class BackwardWeights(Weights):
    def place(self, index):
        return self.held[index - 1], self.sems.at[index - 1]

    def start(self, index):
        if index != 0:
            super().start(index)
            return
        width = self.own[0].shape[0]

        def begin(matrix):
            for j in range(3):
                block = pl.ds(j * width, width)
                pltpu.make_async_copy(
                    matrix[0].at[:, block], self.held[2].at[block, :], self.sems.at[3 + j]
                ).start()

        @pl.when(self.own_flag == 1)
        def _():
            begin(self.own)

        @pl.when(self.own_flag != 1)
        def _():
            begin(self.other)

    def wait(self, index):
        if index == 0:
            width = self.own[0].shape[0]
            for j in range(3):
                block = pl.ds(j * width, width)
                pltpu.make_async_copy(
                    self.own[0].at[:, block], self.held[2].at[block, :], self.sems.at[3 + j]
                ).wait()
            return self.held[2]
        return super().wait(index)


def backward_scratch(own, row_count):
    width, hidden_units = own[2].shape
    bfloat16, float32 = jnp.bfloat16, jnp.float32
    return [pltpu.VMEM(w.shape, w.dtype) for w in own[1:]] + [
        pltpu.VMEM((row_count, width), bfloat16),
        pltpu.VMEM((row_count, width), float32),
        pltpu.VMEM((row_count, 3 * width), bfloat16),
        pltpu.VMEM((row_count, width), bfloat16),
        pltpu.VMEM((row_count, hidden_units), bfloat16),
        pltpu.VMEM((16, row_count), float32),
        pltpu.VMEM((row_count, width), bfloat16),
        pltpu.VMEM((row_count, width), bfloat16),
        pltpu.VMEM((row_count, 3 * width), bfloat16),
        pltpu.VMEM((row_count, width), float32),
        pltpu.VMEM((row_count, width), float32),
        pltpu.VMEM((row_count, width), bfloat16),
        pltpu.VMEM((2, row_count, LANES), bfloat16),
        pltpu.VMEM((2, row_count, LANES), bfloat16),
        pltpu.SemaphoreType.DMA((6,)),
        pltpu.SemaphoreType.DMA((9,)),
    ]


def backward_loads(kept, grads_in, buffers, sems, whole_rows, whole_grad):
    rows_hbm, hidden_hbm, qkv_hbm, mixed_hbm, slope_hbm, stat_hbm = kept
    rows_ref, hidden_ref, qkv_ref, mixed_ref, slope_ref, stat_ref = buffers[:6]
    row_count = rows_ref.shape[0]
    mine = pl.ds(pl.multiple_of(lax.axis_index("section") * row_count, row_count), row_count)
    if whole_rows:
        rows_hbm = rows_hbm.at[mine, :]
    if len(grads_in) == 1 and not whole_grad:
        grad_pairs = [(grads_in[0], buffers[11])]
    elif whole_grad:
        grad_pairs = [(grads_in[0].at[mine, :], buffers[11])]
    else:
        grad_pairs = list(zip(grads_in, buffers[9:12]))
    pairs = {
        "slope": [(slope_hbm, slope_ref)], "hidden": [(hidden_hbm, hidden_ref)], "mixed": [(mixed_hbm, mixed_ref)],
        "qkv": [(qkv_hbm, qkv_ref)], "stat": [(stat_hbm, stat_ref)], "rows": [(rows_hbm, rows_ref)],
    }
    copies, index = {}, 0
    for name, entries in [("grads", grad_pairs), *pairs.items()]:
        copies[name] = []
        for source, target in entries:
            copies[name].append(pltpu.make_async_copy(source, target, sems.at[index]))
            index = index + 1
    return copies


def start_copies(copies):
    for copy in copies:
        copy.start()


def wait_copies(copies):
    for copy in copies:
        copy.wait()


def backward_kernel(block, lengths_ref, tables_ref, *refs):
    from_code = block == 0
    grads_in, kept, own, other, made, (sums_ref,), held, buffers, (weight_sems, load_sems, save_sems) = split_refs(
        refs, (3 if from_code else 1, 6, 4, 4, 5, 1, 3, 14, 3)
    )
    weights = BackwardWeights(
        (lax.axis_index("section") == block).astype(jnp.int32), own, other,
        held, weight_sems,
    )
    loads = backward_loads(kept, grads_in, buffers, load_sems, from_code, not from_code)
    saves = {
        name: pltpu.make_async_copy(source, target, save_sems.at[index])
        for index, (name, source, target) in enumerate(zip(
            ("grad", "branch", "pre", "attn", "projected"),
            (buffers[9], buffers[6], buffers[4], buffers[7], buffers[8]),
            made,
        ))
    }
    start_copies(loads["grads"])
    weights.start(3)
    start_copies(loads["slope"])
    weights.start(2)
    start_copies(loads["hidden"])
    weights.start(1)
    for name in ("mixed", "qkv", "stat", "rows"):
        start_copies(loads[name])

    def arrived(names):
        for name in names:
            wait_copies(loads[name])

    def during(where):
        if where == "pre":
            weights.start(0)

    backward_steps(
        from_code, lengths_ref, tables_ref.at[block], buffers, sums_ref, weights.wait, arrived,
        lambda name: saves[name].start(), during,
    )
    for save in saves.values():
        save.wait()


def block_backward(block, lengths, tables, grads_in, kept, own, other):
    row_count, width = kept[1].shape
    hidden_units = own[2].shape[1]
    bfloat16, float32 = jnp.bfloat16, jnp.float32
    made = [
        ((row_count, width), float32),
        ((row_count, width), bfloat16),
        ((row_count, hidden_units), bfloat16),
        ((row_count, width), bfloat16),
        ((row_count, 3 * width), bfloat16),
        (tables.shape[1:], float32),
    ]
    return pl.pallas_call(
        functools.partial(backward_kernel, block),
        out_shape=tuple(jax.ShapeDtypeStruct(s, t) for s, t in made),
        in_specs=[in_smem(), in_vmem()] + [in_place()] * (14 + len(grads_in)),
        out_specs=[in_place()] * 5 + [in_vmem()],
        scratch_shapes=backward_scratch(own, row_count) + [pltpu.SemaphoreType.DMA((5,))],
        compiler_params=pltpu.CompilerParams(vmem_limit_bytes=56 * 1024 * 1024),
        cost_estimate=pl.CostEstimate(
            flops=2 * row_count * (12 * width * width + 5 * row_count * width),
            bytes_accessed=40 * 1024 * 1024,
            transcendentals=row_count * row_count * HEADS,
        ),
        name="block_backward",
    )(lengths, tables, *grads_in, *kept, *own, *other)


SLOTS, HELD, RING = 4, 6, 16


def chunk_list(width, hidden_units):
    ups = hidden_units // width

    def of(block, operand, count):
        return [(block, operand, j) for j in range(count)]

    return (
        of(1, 3, ups) + of(1, 2, ups) + of(1, 1, 1) + of(1, 0, 3)
        + of(0, 3, ups) + of(0, 2, ups) + of(0, 1, 1) + of(0, 0, 3)
    )


def count_codes_in(codes_ref, code_count, counts_ref, stats_ref):
    high_count = counts_ref.shape[0]
    high_rows = -(-high_count // 16) * 16

    @pl.loop(0, codes_ref.shape[0], init_carry=jnp.zeros((high_rows, LANES), jnp.float32))
    def counts(block, total):
        codes = codes_ref[block]

        def hot(values, size):
            rows = lax.broadcasted_iota(jnp.int32, (size, 1), 0)
            pieces = [jnp.where(values[j : j + 1, :] == rows, 1.0, 0.0) for j in range(codes.shape[0])]
            return jnp.concatenate(pieces, axis=1).astype(jnp.bfloat16)

        return total + times_transposed(hot(codes >> 7, high_rows), hot(codes & (LANES - 1), LANES))

    counts = counts[:high_count, :]
    counts_ref[...] = counts.astype(jnp.int32)
    share = counts / float(codes_ref.shape[0] * codes_ref.shape[1] * LANES)
    used = counts > 0.0
    terms = jnp.where(used, share * jnp.log(jnp.where(used, share, 1.0)), 0.0)
    usage = jnp.sum(jnp.where(used, 1.0, 0.0), axis=(0, 1), keepdims=True) / code_count
    perplexity = jnp.exp(-jnp.sum(terms, axis=(0, 1), keepdims=True)) / code_count
    stats_ref[...] = jnp.concatenate([usage, perplexity], axis=1)


def closing_kernel(chunks, code_count, lengths_ref, tables_ref, codes_ref, *refs):
    (
        dec_grads_in, enc_grads_in, dec_kept, enc_kept, own, other, dec_left, enc_left,
        results, (vector_sums_ref, bias_sums_ref, counts_ref, stats_ref, shown_out, grads_out), held_weights, buffers,
        (weight_sems, load_sems, enc_weight_sems, enc_load_sems),
        (stage, zero, held, one, two, three, finals, fourth), (narrow, wide), (dec_grad_ref, dec_sums, enc_sums),
        (sums_send, sums_zero, sums_held, sums_first, sums_second, sums_third),
        (operand_sems, zero_send, zero_got, first_send, first_got, second_send, second_got, third_send, third_got,
         fourth_send, fourth_got, swap_sems, credit),
    ) = split_refs(refs, (1, 1, 6, 6, 4, 4, 3, 3, 4, 6, 3, 14, 4, 8, 2, 3, 6, 13))
    count = len(chunks)
    depth, share, width = stage.shape[1], stage.shape[4], stage.shape[5]
    half = width // 2
    rows = buffers[0].shape[0]
    ups = sum(1 for block, operand, _ in chunks if block == 0 and operand == 3)
    section, place = lax.axis_index("section"), lax.axis_index("dp")
    my_x, my_y, my_z = place % 2, place // 2 % 2, place // 4
    beside_x, beside_y = place + 1 - 2 * my_x, place + 2 - 4 * my_y
    first_device = beside_x * (1 - section) + beside_y * section
    second_device = beside_y * (1 - section) + beside_x * section
    own_half = pl.ds(pl.multiple_of(section * half, LANES), half)
    other_half = pl.ds(pl.multiple_of((1 - section) * half, LANES), half)

    barrier = pltpu.get_barrier_semaphore()
    pl.semaphore_signal(barrier, inc=1, device_id={"section": 1 - section}, device_id_type=MESH)
    for device in (beside_x, beside_y):
        pl.semaphore_signal(barrier, inc=1, device_id={"dp": device}, device_id_type=MESH)
    for hop in range(1, depth):
        device = (my_z + hop) % depth * 4 + my_y * 2 + my_x
        pl.semaphore_signal(barrier, inc=1, device_id={"dp": device}, device_id_type=MESH)

    operands = {
        0: (narrow.at[1], buffers[8]), 1: (buffers[3], buffers[7]), 2: (narrow.at[0], buffers[4]), 3: (wide, buffers[6]),
    }
    moves = {}
    for block, left in ((0, enc_left), (1, dec_left)):
        for operand, source in ((0, left[0]), (2, left[1]), (3, left[2])):
            moves[block, operand] = pltpu.make_async_copy(
                source, operands[operand][0], operand_sems.at[block, operand]
            )

    def matrices(block, sems):
        return BackwardWeights((section == block).astype(jnp.int32), own, other, held_weights, sems)

    dec_weights, enc_weights = matrices(1, weight_sems), matrices(0, enc_weight_sems)
    dec_loads = backward_loads(dec_kept, dec_grads_in, buffers, load_sems, False, True)
    enc_loads = backward_loads(enc_kept, enc_grads_in, buffers, enc_load_sems, True, False)
    start_copies(dec_loads["grads"])
    moves[1, 3].start()
    dec_weights.start(3)
    start_copies(dec_loads["slope"])
    dec_weights.start(2)
    moves[1, 2].start()
    start_copies(dec_loads["hidden"])
    dec_weights.start(1)
    for name in ("mixed", "qkv", "stat", "rows"):
        start_copies(dec_loads[name])
    moves[1, 0].start()
    pl.semaphore_wait(barrier, 3 + depth - 1)

    def remote(source, land, send, got, **device):
        return pltpu.make_async_remote_copy(
            src_ref=source, dst_ref=land, send_sem=send, recv_sem=got, device_id=device, device_id_type=MESH
        )

    def across(k):
        if k == count:
            return remote(sums_send, sums_zero, zero_send.at[k], zero_got.at[k], section=1 - section)
        return remote(
            stage.at[k % SLOTS, :, :, :, :, other_half], zero.at[k % SLOTS], zero_send.at[k], zero_got.at[k],
            section=1 - section,
        )

    def first(k):
        if k == count:
            return remote(sums_held, sums_first, first_send.at[k], first_got.at[k], dp=first_device)
        return remote(
            held.at[k % HELD, 1], one.at[k % RING], first_send.at[k], first_got.at[k], dp=first_device
        )

    def second(k):
        if k == count:
            return remote(sums_first, sums_second, second_send.at[k], second_got.at[k], dp=second_device)
        return remote(
            one.at[k % RING, 1], two.at[k % RING], second_send.at[k], second_got.at[k], dp=second_device
        )

    def third(k, hop):
        target = (my_z + hop) % depth
        device = target * 4 + my_y * 2 + my_x
        send, got = third_send.at[k, hop - 1], third_got.at[k, hop - 1]
        if k == count:
            return remote(sums_second, sums_third.at[hop - 1], send, got, dp=device)
        return remote(two.at[k % RING, target], three.at[k % RING, hop - 1], send, got, dp=device)

    def last(k):
        index = k % (count // 2)
        return remote(finals.at[index], fourth.at[index], fourth_send.at[k], fourth_got.at[k], section=1 - section)

    def send_across(k):
        if k >= SLOTS:
            pl.semaphore_wait(credit, 1)
        across(k).start()

    def give(k):
        if k == count:
            dec, enc = dec_sums[...], enc_sums[...]
            sums_held[...] = jnp.where(section == 0, enc, dec)
            sums_send[...] = jnp.where(section == 0, dec, enc)
            across(k).start()
            return
        block, operand, j = chunks[k]
        key = (block, operand)
        if operand == 3 and j != 0:
            send_across(k)
            return
        if j == 0 and key in moves and key != (0, 3):
            moves[key].wait()
        made = range(k, k + ups) if operand == 3 else range(k, k + 1)
        for each in made:
            if each >= SLOTS:
                across(each - SLOTS).wait_send()
        left, right = operands[operand]
        if operand == 3:

            @pl.loop(0, depth)
            def _(tile):
                columns = pl.ds(pl.multiple_of(tile * 4 * ups * share, LANES), 4 * ups * share)
                product = transposed_times(left[:, columns], right[...]).astype(stage.dtype)
                product = product.reshape(2, 2, ups, share, width)
                for j in range(ups):
                    stage[(k + j) % SLOTS, tile] = product[:, :, j]

        else:
            columns = right[:, j * width : (j + 1) * width]
            product = transposed_times(left[...], columns) if operand == 1 else times(left[...], columns)
            product = product.astype(stage.dtype)
            stage[k % SLOTS] = product.reshape(depth, 2, 2, share, width)
        send_across(k)
        last_of_key = operand == 3 or k + 1 == count or chunks[k + 1][:2] != key
        if last_of_key and block == 1 and operand in (0, 2):
            moves[0, operand].start()

    def begin(k):
        across(k).wait_recv()
        if k == count:
            sums_held[...] = sums_held[...] + sums_zero[...]
            first(k).start()
            return
        if k >= HELD:
            first(k - HELD).wait_send()
        slot = k % SLOTS
        for a in range(2):
            for b in range(2):
                chip_x = (my_x + (a * (1 - section) + b * section)) % 2
                chip_y = (my_y + (b * (1 - section) + a * section)) % 2
                held[k % HELD, a, b] = stage[slot, :, chip_y, chip_x, :, own_half] + zero[slot, :, chip_y, chip_x]
        first(k).start()
        if k + SLOTS < count:
            pl.semaphore_signal(credit, inc=1, device_id={"section": 1 - section}, device_id_type=MESH)

    def after_first(k):
        first(k).wait_recv()
        if k == count:
            first(k).wait_send()
            sums_first[...] = sums_first[...] + sums_held[...]
        else:
            slot = k % RING
            one[slot] = one[slot] + held[k % HELD, 0]
        second(k).start()

    def after_second(k):
        second(k).wait()
        if k == count:
            sums_second[...] = sums_second[...] + sums_first[...]
        else:
            slot = k % RING
            two[slot] = two[slot] + one[slot, 0]
        for hop in range(1, depth):
            third(k, hop).start()

    def after_third(k):
        if k == count:
            total = sums_second[...]
            for hop in range(1, depth):
                third(k, hop).wait()
                total = total + sums_third[hop - 1]
            vector_sums_ref[...] = total[:VECTORS, :]
            bias_sums_ref[...] = jnp.zeros_like(bias_sums_ref)
            for j in range(ups):
                bias_sums_ref[0:1, j * width : (j + 1) * width] = total[VECTORS + j : VECTORS + j + 1, :]
            return
        block = chunks[k][0]
        slot = k % RING
        total = two[slot, my_z].astype(jnp.float32)
        for hop in range(1, depth):
            third(k, hop).wait()
            total = total + three[k % RING, hop - 1].astype(jnp.float32)

        @pl.when(section == block)
        def _():
            put(k, total, own_half, section * half)

        @pl.when(section != block)
        def _():
            finals[k % (count // 2)] = total
            last(k).start()

    def put(k, total, lanes, offset):
        _, operand, j = chunks[k]
        if operand == 3:
            results[3][j * share : (j + 1) * share, lanes] = total
        else:
            start = pl.multiple_of(j * width + offset, LANES)
            results[operand][:, pl.ds(start, half)] = total

    def after_fourth(k):
        if k == count:
            return
        block = chunks[k][0]

        @pl.when(section == block)
        def _():
            last(k).wait_recv()
            put(k, fourth[k % (count // 2)], other_half, (1 - section) * half)

        @pl.when(section != block)
        def _():
            last(k).wait_send()

    close = 11

    def times_of(k):
        start = min(k, count - 1) // 2
        return tuple(start + stage_number for stage_number in range(6))

    phases = ((1, begin), (0, give), (2, after_first), (3, after_second), (4, after_third), (5, after_fourth))

    def step(number):
        for phase, action in phases:
            for k in range(count + 1):
                if times_of(k)[phase] == number:
                    action(k)

    mine = pl.ds(pl.multiple_of(section * rows, rows), rows)

    def deliver(block, source, target, sem, start):
        stay = pltpu.make_async_copy(source, target.at[mine, :], swap_sems.at[sem, 0])
        go = remote(source, target.at[mine, :], swap_sems.at[sem, 1], swap_sems.at[sem, 2], section=1 - section)

        @pl.when(section == block)
        def _():
            if start:
                stay.start()
            else:
                stay.wait()
                go.wait_recv()

        @pl.when(section != block)
        def _():
            if start:
                go.start()
            else:
                go.wait_send()

    branch_buffer, grad_buffer, second_buffer = buffers[6], buffers[9], buffers[10]
    shown_dec = (1, branch_buffer, shown_out, 0)
    grads_dec = (1, dec_grad_ref, grads_out, 1)
    shown_enc = (0, branch_buffer, shown_out, 2)
    grads_enc = (0, grad_buffer, grads_out, 3)

    def once(act):
        seen = set()

        def acted(name):
            if name not in seen:
                seen.add(name)
                act(name)

        return acted

    dec_arrive = once(lambda name: wait_copies(dec_loads[name]))
    enc_arrive = once(lambda name: wait_copies(enc_loads[name]))
    enc_matrix = once(lambda index: enc_weights.wait(index))

    def enc_weight(index):
        enc_matrix(index)
        return held_weights[2] if index == 0 else enc_weights.place(index)[0]

    def dec_arrived(names):
        for name in names:
            dec_arrive(name)

    def enc_arrived(names):
        for name in names:
            enc_arrive(name)
        if "grads" in names:
            enc_arrive("hidden")
            moves[0, 3].wait()
            last_product(tables_ref.at[0], buffers[1], wide, enc_weight(3), second_buffer, None)

    dec_steps = {"branch": 0, "gelu": 1, "pre": 2, "attn": 3, ("heads", 2): 4, "rows": 5}
    enc_steps = {"branch": 6, "gelu": 7, "pre": 8, ("heads", 0): 9, ("heads", 2): 10}

    def during_decoder(where):
        if where == "pre":
            last_product(tables_ref.at[1], buffers[1], wide, held_weights[2], None, branch_buffer)
            deliver(*shown_dec, True)
            dec_weights.start(0)
            moves[0, 3].start()
        if where in dec_steps:
            step(dec_steps[where])
        if where == "second":
            enc_weights.start(2)
        elif where == "attn":
            start_copies(enc_loads["slope"])
            start_copies(enc_loads["hidden"])
            enc_weights.start(1)
        elif where == ("heads", 2):
            for name in ("mixed", "qkv", "stat"):
                start_copies(enc_loads[name])
        elif where == "rows":
            enc_weights.start(3)

    def during_encoder(where):
        if where == "pre":
            branch_buffer[...] = second_buffer[...].astype(branch_buffer.dtype)
            deliver(*shown_enc, True)
            enc_weights.start(0)
        if where in enc_steps:
            step(enc_steps[where])

    def nothing(name):
        return None

    backward_steps(
        False, lengths_ref, tables_ref.at[1], buffers, dec_sums, dec_weights.wait, dec_arrived, nothing,
        during_decoder,
    )
    start_copies(enc_loads["grads"])
    start_copies(enc_loads["rows"])
    dec_grad_ref[...] = grad_buffer[...]
    deliver(*grads_dec, True)
    deliver(*shown_dec, False)
    backward_steps(
        True, lengths_ref, tables_ref.at[0], buffers, enc_sums, enc_weight, enc_arrived, nothing, during_encoder,
    )
    deliver(*grads_enc, True)
    for number in range(close, times_of(count)[5] + 1):
        step(number)
        if number == 13:
            count_codes_in(codes_ref, code_count, counts_ref, stats_ref)
    for parts in (grads_dec, shown_enc, grads_enc):
        deliver(*parts, False)
    for k in range(count + 1):
        if k + SLOTS >= count:
            across(k).wait_send()
        if k != count and k + HELD >= count:
            first(k).wait_send()


def closing(lengths, tables, codes, code_count, cotangent, enc_grads_in, dec_kept, enc_kept, own, other, dec_left, enc_left, devices):
    row_count, width = dec_kept[0].shape
    hidden_units = own[2].shape[1]
    chunks = chunk_list(width, hidden_units)
    count, depth, share, half = len(chunks), devices // 4, width // devices, width // 2
    bfloat16, float32 = jnp.bfloat16, jnp.float32
    tokens = cotangent.shape[0]
    table = pltpu.VMEM(tables.shape[1:], float32)
    dma = pltpu.SemaphoreType.DMA
    shapes = [
        ((share, 3 * width), float32),
        ((share, width), float32),
        ((share, hidden_units), float32),
        ((hidden_units // devices, width), float32),
        ((VECTORS, width), float32),
        ((8, hidden_units), float32),
        ((-(-code_count // LANES), LANES), jnp.int32),
        ((1, 2), float32),
        ((tokens, width), bfloat16),
        ((tokens, width), float32),
    ]
    return pl.pallas_call(
        functools.partial(closing_kernel, chunks, code_count),
        out_shape=tuple(jax.ShapeDtypeStruct(s, t) for s, t in shapes),
        in_specs=[in_smem()] + [in_vmem()] * 2 + [in_place()] * 28,
        out_specs=[in_vmem()] * 8 + [in_place()] * 2,
        scratch_shapes=backward_scratch(own, row_count)
        + [
            dma((6,)),
            dma((9,)),
            pltpu.VMEM((SLOTS, depth, 2, 2, share, width), bfloat16),
            pltpu.VMEM((SLOTS, depth, 2, 2, share, half), bfloat16),
            pltpu.VMEM((HELD, 2, 2, depth, share, half), bfloat16),
            pltpu.VMEM((RING, 2, depth, share, half), bfloat16),
            pltpu.VMEM((RING, depth, share, half), bfloat16),
            pltpu.VMEM((RING, depth - 1, share, half), bfloat16),
            pltpu.VMEM((count // 2, share, half), float32),
            pltpu.VMEM((count // 2, share, half), float32),
            pltpu.VMEM((2, width, row_count), bfloat16),
            pltpu.VMEM((row_count, hidden_units), bfloat16),
            pltpu.VMEM((row_count, width), float32),
            table,
            table,
            table,
            table,
            table,
            table,
            table,
            pltpu.VMEM((depth - 1, *tables.shape[1:]), float32),
            dma((2, 4)),
        ]
        + [dma((count + 1,))] * 6
        + [dma((count + 1, depth - 1))] * 2
        + [dma((count,))] * 2
        + [dma((4, 3)), pltpu.SemaphoreType.REGULAR],
        compiler_params=pltpu.CompilerParams(
            collective_id=0, has_side_effects=True, vmem_limit_bytes=62 * 1024 * 1024
        ),
        name="closing",
    )(lengths, tables, codes, cotangent, *enc_grads_in, *dec_kept, *enc_kept, *own, *other, *dec_left, *enc_left)


def finish_kernel(vectors_ref, bias_ref, *refs):
    sources, targets, (bias_out, vectors_out), held, (in_sems, out_sems) = split_refs(refs, (6, 6, 2, 6, 2))
    pieces = []
    for source, target, room in zip(sources, targets, held):
        rows = source.shape[0]
        step = rows // 4 if rows >= 512 else rows
        pieces = pieces + [
            tuple(ref.at[pl.ds(start, step)] for ref in (source, room, target)) for start in range(0, rows, step)
        ]
    loads = [pltpu.make_async_copy(s, h, in_sems.at[i]) for i, (s, h, _) in enumerate(pieces)]
    saves = [pltpu.make_async_copy(h, t, out_sems.at[i]) for i, (_, h, t) in enumerate(pieces)]
    start_copies(loads)
    place = lax.axis_index("dp")

    def from_place(ref, out):
        whole, part = ref.shape[1], out.shape[1]
        turned = pltpu.roll(ref[...], (whole - place * part) % whole, 1)
        out[...] = turned[: out.shape[0], :part]

    for load, save in zip(loads, saves):
        load.wait()
        save.start()
    from_place(vectors_ref, vectors_out)
    from_place(bias_ref, bias_out)
    wait_copies(saves)


def finish(results, vector_sums, bias_sums, devices):
    small = [
        jax.ShapeDtypeStruct((1, bias_sums.shape[1] // devices), jnp.float32),
        jax.ShapeDtypeStruct((VECTORS, vector_sums.shape[1] // devices), jnp.float32),
    ]
    return pl.pallas_call(
        finish_kernel,
        out_shape=tuple(jax.ShapeDtypeStruct(a.shape, a.dtype) for a in results) + tuple(small),
        in_specs=[in_vmem()] * 2 + [in_place()] * 6,
        out_specs=[in_place()] * 6 + [in_vmem()] * 2,
        scratch_shapes=[pltpu.VMEM(a.shape, a.dtype) for a in results]
        + [pltpu.SemaphoreType.DMA((12,)), pltpu.SemaphoreType.DMA((12,))],
        compiler_params=pltpu.CompilerParams(vmem_limit_bytes=60 * 1024 * 1024),
        name="finish",
    )(vector_sums, bias_sums, *results)


def count_codes(all_codes, code_count):
    high = -(-code_count // LANES)
    high_hot = (all_codes[:, None] // LANES == jnp.arange(high, dtype=jnp.int32)).astype(jnp.bfloat16)
    low_hot = (all_codes[:, None] % LANES == jnp.arange(LANES, dtype=jnp.int32)).astype(jnp.bfloat16)
    counts = transposed_times(high_hot, low_hot)
    return counts.reshape(-1)[:code_count].astype(jnp.int32)


def code_statistics(histogram, rows):
    code_share = histogram.astype(jnp.float32) / rows
    is_used = histogram > 0
    usage_share = jnp.mean(is_used.astype(jnp.float32))
    entropy = -jnp.sum(
        jnp.where(is_used, code_share * jnp.log(jnp.where(is_used, code_share, 1.0)), 0.0)
    )
    return jnp.stack([usage_share, jnp.exp(entropy) / histogram.shape[0]])


def plain_closing(
    is_first, lengths, tables, cotangent, enc_grads_in, dec_kept, enc_kept, own, other, encoded, decoded, shown,
    swapped, ordered, vector_count, width,
):
    code_grad, dec_branch, dec_pre, dec_attn, dec_projected, dec_sums = block_backward(
        1, lengths, tables, (cotangent,), dec_kept, own, other
    )
    grad, branch, pre, attn, projected, enc_sums = block_backward(
        0, lengths, tables, (code_grad, *enc_grads_in), enc_kept, own, other
    )
    encoder = ((encoded[1], encoded[3], encoded[4], encoded[6]), (projected, attn, pre, branch))
    decoder = ((decoded[1], decoded[3], decoded[4], decoded[6]), (dec_projected, dec_attn, dec_pre, dec_branch))
    results = []
    for index in range(4):
        product = times if index in (0, 2) else transposed_times
        enc = product(encoder[0][index], encoder[1][index])
        dec = product(decoder[0][index], decoder[1][index])
        results.append(jnp.where(is_first, enc, dec) + swapped(jnp.where(is_first, dec, enc)))
    own_sums, other_sums = ordered(enc_sums, dec_sums)
    sums = own_sums + swapped(other_sums)
    bias_rows = own[2].shape[1] // width
    results = results + [sums[vector_count : vector_count + bias_rows].reshape(-1), sums[:vector_count]]
    weight_grads = tuple(
        lax.psum_scatter(part, "dp", scatter_dimension=axis, tiled=True)
        for part, axis in zip(results, (0, 0, 0, 0, 0, 1))
    )

    def both_micro(enc_rows, dec_rows):
        own_rows, other_rows = ordered(enc_rows, dec_rows)
        return jnp.concatenate(ordered(own_rows, swapped(other_rows)), axis=0)

    return weight_grads, both_micro(*shown), both_micro(grad, code_grad)


def body(
    patches,
    cotangent,
    codes,
    lengths,
    codebook,
    qkv_weight,
    out_weight,
    up_weight,
    down_weight,
    up_bias,
    vectors,
):
    section_index = lax.axis_index("section")
    is_first = section_index == 0
    devices = lax.axis_size("dp")
    tok_rows, model_width = patches.shape
    row_count = tok_rows // lengths.shape[0]
    code_count = codebook.shape[0] * devices

    def swapped(array):
        return lax.ppermute(array, "section", [(0, 1), (1, 0)])

    def ordered(own, other):
        return jnp.where(is_first, own, other), jnp.where(is_first, other, own)

    own = (qkv_weight[0], out_weight[0], up_weight[0], down_weight[0])
    if devices == 16:
        other, tables, all_codes, chosen, encoded = opening(
            lengths, codes, vectors, up_bias, patches, codebook, own, devices, row_count
        )
        decoded, other_down = forward_swap(lengths, chosen, tables, own, other)
        other = (*other, other_down)
    else:
        other, tables, all_codes, chosen, encoded = plain_opening(
            lengths, codes, table_of(vectors[0], up_bias[0]), patches, codebook, own, swapped, ordered, row_count
        )
        decoded = block_forward(1, lengths, chosen, tables, own, other)
        shown = (encoded[8], decoded[8])
        enc_grads_in = (encoded[0], chosen)
        encoded, decoded = ((*made[1:8], made[9]) for made in (encoded, decoded))

    def saved(rows, made):
        hidden, _, projected, mixed, _, slope, _, stats = made
        return rows, hidden, projected, mixed, slope, stats

    if devices == 16:
        *weight_grads, vector_sums, bias_sums, counts, code_stats, outputs, input_grad = closing(
            lengths, tables, all_codes, code_count, cotangent, (chosen,), saved(chosen, decoded),
            saved(patches, encoded), own, other, (decoded[1], decoded[4], decoded[6]),
            (encoded[1], encoded[4], encoded[6]), devices,
        )
        histogram, code_stats = counts.reshape(-1)[:code_count], code_stats[0]
        *weight_grads, outputs, input_grad, bias_grad, vector_grad = finish(
            (*weight_grads, outputs, input_grad), vector_sums, bias_sums, devices
        )
        weight_grads = (*weight_grads, bias_grad[0], vector_grad)
    else:
        histogram = count_codes(all_codes, code_count)
        code_stats = code_statistics(histogram, tok_rows * devices)
        weight_grads, outputs, input_grad = plain_closing(
            is_first, lengths, tables, cotangent, enc_grads_in, saved(chosen, decoded), saved(patches, encoded), own,
            other, encoded, decoded, shown, swapped, ordered, vectors.shape[1], model_width,
        )
    return (outputs[None], input_grad[None], *(part[None] for part in weight_grads), histogram, code_stats)


def solution(mesh):
    placed = (
        P("dp", None),
        P("dp", None),
        P("dp"),
        P("dp", None),
        P("dp", None),
        P("section", None, None),
        P("section", None, None),
        P("section", None, None),
        P("section", None, None),
        P("section", None),
        P("section", None, None),
    )
    return jax.shard_map(
        body,
        mesh=mesh,
        in_specs=placed,
        out_specs=(
            P("section", "dp", None),
            P("section", "dp", None),
            P("section", "dp", None),
            P("section", "dp", None),
            P("section", "dp", None),
            P("section", "dp", None),
            P("section", "dp"),
            P("section", None, "dp"),
            P(),
            P(),
        ),
        check_vma=False,
    )
```
